32 devices in a mesh: tm: 2 (over x), row: 4 (over y, core), col: 4 (over z).
Axes of the slice: x: 2, y: 2, z: 4, core: 2. Of those that a mesh axis runs over, the one named last changes fastest.
Arguments:
- resid: bfloat16 [2, 48, 160, 1152], P('tm', 'row', 'col'), may hold values from -8 to 8
- spatial_qkv: bfloat16 [3, 2, 48, 160, 1152], P(None, 'tm', 'row', 'col'), may hold values from -12 to 12
- key_keep: int32 [2, 48, 160], P('tm', 'row', 'col'), may hold values 0 or 1
- w_spatial_out: bfloat16 [1152, 1152], replicated, may hold values from -0.1875 to 0.1875
- modulation: float32 [2, 1152], replicated, may hold values from -3 to 3
- w_temporal_qkv: bfloat16 [1152, 3456], replicated, may hold values from -4 to 4
Outputs:
- temporal_heads: bfloat16 [2, 48, 160, 1152], P('tm', 'row', 'col')
The draws below stay inside these ranges and needn't reach their ends.
All inputs are finite; a program needn't handle non-finite values. No bound on the sum of `key_keep` on one device may be relied on, other than what follows from the above.
Results may differ from the reference program's by a relative error of at most 0.0084.
Values may be sent and summed in bfloat16 or wider, within the bound.
No kernel may reach another device: no remote copies, remote signals or barrier semaphores. Data moves between devices by JAX's collectives and lax.ppermute only.
A program may use at most 128 MiB of HBM per device.

```python
import jax
import jax.numpy as jnp
from jax import lax

D = 1152
HEADS = 16
HEAD_DIM = 72
RADIUS = 3
FRAMES = 2
H = 48
W = 160


def draw_resid(key, part):
    values = jax.random.normal(key, (FRAMES, H, W, D), jnp.float32)
    return jnp.clip(values, -8.0, 8.0).astype(jnp.bfloat16)


def draw_spatial_qkv(key, part):
    first_key, second_key, third_key = jax.random.split(key, 3)
    shape_one = (FRAMES, H, W, D)
    queries_part = jnp.clip(jax.random.normal(first_key, shape_one, jnp.float32), -6.0, 6.0)
    keys_part = jnp.clip(jax.random.normal(second_key, shape_one, jnp.float32), -6.0, 6.0)
    values_part = jnp.clip(jax.random.normal(third_key, shape_one, jnp.float32), -6.0, 6.0)
    return jnp.stack([queries_part, keys_part, values_part], 0).astype(jnp.bfloat16)


def draw_w_temporal_qkv(key, part):
    first_key = jax.random.fold_in(key, 0)
    base = jax.random.normal(first_key, (D, 3 * D), jnp.float32) * D ** (-0.5)
    return jnp.clip(base, -4.0, 4.0).astype(jnp.bfloat16)


def touch_ends(values, stream_key, smallest, top_value):
    dims = values.shape
    index_at = [jax.random.randint(jax.random.fold_in(stream_key, axis), (), 0, dims[axis]) for axis in range(len(dims))]
    values = values.at[tuple(index_at)].set(smallest)
    longest = dims.index(max(dims))
    index_at[longest] = (index_at[longest] + 1) % dims[longest]
    return values.at[tuple(index_at)].set(top_value)


def gaussian(own_key, extent, deviation, reach, kind=jnp.bfloat16):
    return jnp.clip(deviation * jax.random.normal(own_key, extent, jnp.float32), -reach, reach).astype(kind)


def setup_inputs(seed: int = 0) -> dict:
    key_list = jax.random.split(jax.random.key(seed), 7)
    return {
        "resid": draw_resid(jax.random.fold_in(key_list[6], 71), 0),
        "spatial_qkv": draw_spatial_qkv(jax.random.fold_in(key_list[6], 71), 0),
        "key_keep": touch_ends((jax.random.randint(key_list[2], (FRAMES, H, W), 0, 16) < 13).astype(jnp.int32), jax.random.fold_in(key_list[2], 1), 0, 1),
        "w_spatial_out": gaussian(key_list[3], (D, D), D ** -0.5, 0.1875),
        "modulation": gaussian(key_list[4], (2, D), 0.5, 3.0, jnp.float32),
        "w_temporal_qkv": draw_w_temporal_qkv(jax.random.fold_in(key_list[6], 71), 0),
    }


NEG_FILL = -1e+30
EPSILON = 1e-06

def reference(resid, spatial_qkv, key_keep, w_spatial_out, modulation, w_temporal_qkv):
    score_scale = HEAD_DIM ** (-0.5)
    span = 2 * RADIUS + 1
    shape_heads = (H, W, HEADS, HEAD_DIM)
    padding = ((RADIUS, RADIUS), (RADIUS, RADIUS), (0, 0), (0, 0))

    def spatial_frame(frame):
        queries = spatial_qkv[0, frame].astype(jnp.float32).reshape(shape_heads)
        keys_pad = jnp.pad(spatial_qkv[1, frame].astype(jnp.float32).reshape(shape_heads), padding)
        values_pad = jnp.pad(spatial_qkv[2, frame].astype(jnp.float32).reshape(shape_heads), padding)
        keep_pad = jnp.pad(key_keep[frame], ((RADIUS, RADIUS), (RADIUS, RADIUS)))
        score_list = []
        allow_list = []
        for row_step in range(span):
            for col_step in range(span):
                key_slice = keys_pad[row_step:row_step + H, col_step:col_step + W]
                score_list.append(jnp.einsum('yxhd,yxhd->yxh', queries, key_slice) * score_scale)
                keep_slice = keep_pad[row_step:row_step + H, col_step:col_step + W] == 1
                if row_step == RADIUS and col_step == RADIUS:
                    keep_slice = jnp.ones_like(keep_slice)
                allow_list.append(keep_slice)
        scores = jnp.stack(score_list, -1)
        allowed = jnp.stack(allow_list, -1)[:, :, None, :]
        masked = jnp.where(allowed, scores, NEG_FILL)
        top_score = lax.optimization_barrier(jnp.max(masked, -1, keepdims=True))
        weights_f = jnp.where(allowed, jnp.exp(masked - top_score), 0.0)
        totals = lax.optimization_barrier(jnp.sum(weights_f, -1))
        weights_b = lax.optimization_barrier(weights_f.astype(jnp.bfloat16)).astype(jnp.float32)
        weighted = jnp.zeros(shape_heads, jnp.float32)
        for row_step in range(span):
            for col_step in range(span):
                position = row_step * span + col_step
                value_slice = values_pad[row_step:row_step + H, col_step:col_step + W]
                weighted = weighted + weights_b[..., position, None] * value_slice
        spatial_heads = (weighted / totals[..., None]).astype(jnp.bfloat16).reshape(H * W, D)
        stream = resid[frame].reshape(H * W, D).astype(jnp.float32) + jnp.dot(spatial_heads, w_spatial_out, preferred_element_type=jnp.float32)
        average = lax.optimization_barrier(jnp.mean(stream, -1, keepdims=True))
        centered = stream - average
        variance = lax.optimization_barrier(jnp.mean(centered * centered, -1, keepdims=True))
        normed = (centered * lax.rsqrt(variance + EPSILON) * (1.0 + modulation[1]) + modulation[0]).astype(jnp.bfloat16)
        return normed.reshape(H, W, D)
    normed_all = lax.map(spatial_frame, jnp.arange(FRAMES, dtype=jnp.int32))

    def temporal_row(row_index):
        block = lax.dynamic_index_in_dim(normed_all, row_index, 1, keepdims=False)
        projected = jnp.dot(block.reshape(FRAMES * W, D), w_temporal_qkv, preferred_element_type=jnp.float32).astype(jnp.bfloat16)
        projected = projected.reshape(FRAMES, W, 3, HEADS, HEAD_DIM).astype(jnp.float32)
        tscores = jnp.einsum('fphd,gphd->phfg', projected[:, :, 0], projected[:, :, 1]) * score_scale
        ttop = lax.optimization_barrier(jnp.max(tscores, -1, keepdims=True))
        tweights = jnp.exp(tscores - ttop)
        ttotals = lax.optimization_barrier(jnp.sum(tweights, -1))
        tweights_b = lax.optimization_barrier(tweights.astype(jnp.bfloat16)).astype(jnp.float32)
        tweighted = jnp.einsum('phfg,gphd->fphd', tweights_b, projected[:, :, 2])
        result = tweighted / jnp.transpose(ttotals, (2, 0, 1))[..., None]
        return result.astype(jnp.bfloat16).reshape(FRAMES, W, D)
    rows_out = lax.map(temporal_row, jnp.arange(H, dtype=jnp.int32))
    return jnp.transpose(rows_out, (1, 0, 2, 3))
```

```python
import functools
import math

import jax
import jax.numpy as jnp
from jax import lax
from jax.experimental import pallas as pl
from jax.experimental.pallas import tpu as pltpu
from jax.sharding import PartitionSpec as P

HEADS = 16
RADIUS = 3


NEG_FILL = -1e30
EPSILON = 1e-06

LANES = 128
STRIP = 8
EDGE = STRIP // 2
MIB = 1024 * 1024
VMEM = pl.BlockSpec(memory_space=pltpu.VMEM)


def extended(array, sides, width):
    for axis, dim in sides:
        count, length = (lax.axis_size(axis), array.shape[dim])
        up = [(i, (i + 1) % count) for i in range(count - 1)]
        down = [(j, i) for i, j in up]
        last = lax.slice_in_dim(array, length - width, length, axis=dim)
        leading = lax.slice_in_dim(array, 0, width, axis=dim)
        before = lax.ppermute(last, axis, up)
        after = lax.ppermute(leading, axis, down)
        array = jnp.concatenate([before, array, after], axis=dim)
    return array


def softmax_parts(scores, allowed):
    masked = jnp.where(allowed, scores, NEG_FILL)
    top_score = jnp.max(masked, -1, keepdims=True)
    weights_f = jnp.where(allowed, jnp.exp(masked - top_score), 0.0)
    return (weights_f.astype(jnp.bfloat16), jnp.sum(weights_f, -1))


def frame_attend(gathered, head_count):
    frames_all, single, items, width_three = gathered.shape
    width = width_three // 3
    head_size = width // head_count
    split_qkv = gathered.reshape(frames_all, items, 3, head_count, head_size)
    scores = jnp.einsum(
        "fphd,gphd->phfg",
        split_qkv[:, :, 0],
        split_qkv[:, :, 1],
        preferred_element_type=jnp.float32,
    ) * head_size ** (-0.5)
    weights_b, totals = softmax_parts(scores, True)
    weighted = jnp.einsum(
        "phfg,gphd->fphd", weights_b, split_qkv[:, :, 2], preferred_element_type=jnp.float32
    )
    result = weighted / jnp.transpose(totals, (2, 0, 1))[..., None]
    return result.astype(jnp.bfloat16).reshape(frames_all, single, items, width)


def general_device(resid, spatial_qkv, key_keep, w_spatial_out, modulation, w_temporal_qkv):
    frame_count, tile_rows, tile_cols, width = resid.shape
    head_size = width // HEADS
    score_scale = head_size ** (-0.5)
    tile_tokens = tile_rows * tile_cols
    pair = spatial_qkv[1:3]
    keep_flags = key_keep.astype(jnp.bfloat16)[None, :, :, :, None]
    padded_pair, padded_keep = (
        extended(pair, (("row", 2), ("col", 3)), RADIUS),
        extended(keep_flags, (("row", 2), ("col", 3)), RADIUS),
    )
    pad_rows = tile_rows + 2 * RADIUS
    pad_cols = tile_cols + 2 * RADIUS
    key_count = pad_rows * pad_cols
    queries = spatial_qkv[0].reshape(frame_count, tile_tokens, HEADS, head_size)
    keys_pad = padded_pair[0].reshape(frame_count, key_count, HEADS, head_size)
    values_pad = padded_pair[1].reshape(frame_count, key_count, HEADS, head_size)
    query_index = jnp.arange(tile_tokens)
    query_row = query_index // tile_cols
    query_col = query_index % tile_cols
    key_index = jnp.arange(key_count)
    key_row = key_index // pad_cols
    key_col = key_index % pad_cols
    row_gap = key_row[None, :] - query_row[:, None] - RADIUS
    col_gap = key_col[None, :] - query_col[:, None] - RADIUS
    in_window = (jnp.abs(row_gap) <= RADIUS) & (jnp.abs(col_gap) <= RADIUS)
    itself = (row_gap == 0) & (col_gap == 0)
    key_live = padded_keep.reshape(frame_count, key_count) > 0.5
    allowed = (in_window[None] & (key_live[:, None, :] | itself[None]))[:, None]
    scores = (
        jnp.einsum("fqhd,fkhd->fhqk", queries, keys_pad, preferred_element_type=jnp.float32)
        * score_scale
    )
    weights_b, totals = softmax_parts(scores, allowed)
    weighted = jnp.einsum(
        "fhqk,fkhd->fqhd", weights_b, values_pad, preferred_element_type=jnp.float32
    )
    spatial_heads = (weighted / jnp.transpose(totals, (0, 2, 1))[..., None]).astype(jnp.bfloat16)
    spatial_heads = spatial_heads.reshape(frame_count * tile_tokens, width)
    stream = resid.reshape(frame_count * tile_tokens, width).astype(jnp.float32) + jnp.dot(
        spatial_heads, w_spatial_out, preferred_element_type=jnp.float32
    )
    average = jnp.mean(stream, -1, keepdims=True)
    centered = stream - average
    variance = jnp.mean(centered * centered, -1, keepdims=True)
    normed = (
        centered * lax.rsqrt(variance + EPSILON) * (1.0 + modulation[1]) + modulation[0]
    ).astype(jnp.bfloat16)
    tm_count = lax.axis_size("tm")
    part_tokens = tile_tokens // tm_count
    normed_parts = normed.reshape(frame_count, tm_count, part_tokens, width)
    gathered = lax.all_to_all(normed_parts, "tm", split_axis=1, concat_axis=0, tiled=True)
    frames_all, single, items, unused = gathered.shape
    projected = jnp.dot(
        gathered.reshape(frames_all * single * items, width),
        w_temporal_qkv,
        preferred_element_type=jnp.float32,
    ).astype(jnp.bfloat16)
    projected = projected.reshape(frames_all, single, items, 3 * width)
    result = lax.all_to_all(
        frame_attend(projected, HEADS), "tm", split_axis=0, concat_axis=1, tiled=True
    )
    return result.reshape(frame_count, tile_rows, tile_cols, width)


def iota(shape, dim):
    return lax.broadcasted_iota(jnp.int32, shape, dim)


def tile_attend(queries, keys, values, bias):
    count, width = queries.shape
    head = width // HEADS
    factor = head ** (-0.5) * math.log2(math.e)
    lane = iota((1, 2 * LANES), 1)
    bias_two = jnp.concatenate([bias, bias], axis=0)
    pairs = []
    for pair in range(HEADS // 2):
        start = LANES * pair
        low = 2 * head * pair - start
        mid, high = low + head, low + 2 * head
        window = queries[:, start : start + 2 * LANES]
        first = jnp.where((lane >= low) & (lane < mid), window, 0.0)
        second = jnp.where((lane >= mid) & (lane < high), window, 0.0)
        both = jnp.concatenate([first, second], axis=0).astype(jnp.bfloat16)
        scores = lax.dot_general(
            both,
            keys[:, start : start + 2 * LANES],
            (((1,), (1,)), ((), ())),
            preferred_element_type=jnp.float32,
        )
        scores = scores + bias_two
        top = jnp.max(scores, -1, keepdims=True)
        weights = jnp.exp2((scores - top) * factor)
        total = jnp.sum(weights, -1, keepdims=True)
        mixed = jnp.dot(
            weights.astype(jnp.bfloat16),
            values[:, start : start + 2 * LANES],
            preferred_element_type=jnp.float32,
        )
        mixed = mixed / total
        pairs.append(jnp.where(lane < mid, mixed[:count], mixed[count:]))
    lane = iota((1, LANES), 1)
    blocks = [pairs[0][:, :LANES]]
    for pair in range(1, HEADS // 2):
        cut = 2 * head * pair - LANES * pair
        blocks.append(jnp.where(lane < cut, pairs[pair - 1][:, LANES:], pairs[pair][:, :LANES]))
    blocks.append(pairs[-1][:, LANES:])
    return jnp.concatenate(blocks, axis=1)


def keep_row(count, keep):
    picker = jnp.where(iota((count, LANES), 1) == 0, 1.0, 0.0).astype(jnp.bfloat16)
    return lax.dot_general(
        picker, keep, (((1,), (1,)), ((), ())), preferred_element_type=jnp.float32
    )


def make_bias(q_row, q_col, k_row, k_col, keep):
    row_gap, col_gap = k_row - q_row, k_col - q_col
    near = (jnp.abs(row_gap) <= RADIUS) & (jnp.abs(col_gap) <= RADIUS)
    itself = (row_gap == 0) & (col_gap == 0)
    return jnp.where(near & ((keep > 0.5) | itself), 0.0, NEG_FILL)


def strip_bias(rows, keep):
    count, keys = rows * STRIP, (rows + 2 * RADIUS) * 2 * STRIP
    q, k = iota((count, keys), 0), iota((count, keys), 1)
    return make_bias(
        q // STRIP + RADIUS, q % STRIP + EDGE, k // (2 * STRIP), k % (2 * STRIP), keep_row(count, keep)
    )


def finish(heads, resid, w_out, modulation):
    stream = resid + jnp.dot(heads, w_out, preferred_element_type=jnp.float32)
    average = jnp.mean(stream, -1, keepdims=True)
    centered = stream - average
    variance = jnp.mean(centered * centered, -1, keepdims=True)
    scaled = centered * lax.rsqrt(variance + EPSILON)
    return (scaled * (1.0 + modulation[1:2]) + modulation[0:1]).astype(jnp.bfloat16)


def window(ref, plane, rows, strip):
    found = ref[plane, rows, pl.ds(STRIP * strip, 2 * STRIP), :].astype(jnp.float32)
    return found.reshape(found.shape[0] * found.shape[1], found.shape[2]).astype(jnp.bfloat16)


def middle(ref, plane, rows, strip):
    found = ref[plane, rows, pl.ds(STRIP * strip, 2 * STRIP), :].astype(jnp.float32)
    found = found[:, EDGE : EDGE + STRIP]
    return found.reshape(found.shape[0] * STRIP, found.shape[2])


def inner_kernel(qkv, keep, resid, w_out, modulation, out, heads):
    tile_rows, tile_cols, width = resid.shape[1:]
    rows = tile_rows - 2 * RADIUS
    strips = tile_cols // STRIP - 1
    every = pl.ds(0, tile_rows)
    mine = pl.ds(RADIUS, rows)
    for strip in range(strips):
        bias = strip_bias(rows, window(keep, 0, every, strip))
        mixed = tile_attend(
            middle(qkv, 0, mine, strip), window(qkv, 1, every, strip), window(qkv, 2, every, strip), bias
        )
        heads[strip] = mixed.astype(jnp.bfloat16)
        stream = finish(heads[strip], middle(resid, 0, mine, strip), w_out[...], modulation[...])
        out[strip] = stream


def rim_kernel(qkv, keep, above, below, resid, w_out, modulation, out, heads):
    tile_rows, tile_cols, width = resid.shape[1:]
    strips = tile_cols // STRIP - 1
    near = 2 * RADIUS
    for strip in range(strips):
        halves = []
        sources = []
        for side in range(2):
            inner = pl.ds(0 if side == 0 else tile_rows - near, near)
            mine = pl.ds(0 if side == 0 else tile_rows - RADIUS, RADIUS)
            halo_ref = above if side == 0 else below
            halo = window(halo_ref, 0, pl.ds(0, RADIUS), strip)
            parts = []
            for at, local in (
                (0, window(qkv, 1, inner, strip)),
                (width, window(qkv, 2, inner, strip)),
                (2 * width, window(keep, 0, inner, strip)),
            ):
                far = halo[:, at : at + local.shape[1]]
                parts.append(jnp.concatenate([far, local] if side == 0 else [local, far], axis=0))
            bias = strip_bias(RADIUS, parts[2])
            halves.append(tile_attend(middle(qkv, 0, mine, strip), parts[0], parts[1], bias))
            sources.append(middle(resid, 0, mine, strip))
        heads[strip] = jnp.concatenate(halves, axis=0).astype(jnp.bfloat16)
        out[strip] = finish(heads[strip], jnp.concatenate(sources, axis=0), w_out[...], modulation[...])


def edge_columns(ref, plane, row):
    found = ref[plane, row].astype(jnp.float32)
    return found[:STRIP], found[found.shape[0] - STRIP :]


def edge_kernel(qkv, keep, above, below, left, right, resid, w_out, modulation, out, far, ends, mine):
    tile_rows, tile_cols, width = resid.shape[1:]
    pad_rows = tile_rows + 2 * RADIUS
    far[...] = jnp.zeros_like(far)
    for row in range(pad_rows):
        local = row - RADIUS
        if 0 <= local < tile_rows:
            sources = ((qkv, 1, local, 0, width), (qkv, 2, local, width, width), (keep, 0, local, 2 * width, LANES))
        elif local < 0:
            sources = ((above, 0, row, 0, 2 * width + LANES),)
        else:
            sources = ((below, 0, local - tile_rows, 0, 2 * width + LANES),)
        for ref, plane, at, lane, lanes in sources:
            head, tail = edge_columns(ref, plane, at)
            far[row, 0:STRIP, lane : lane + lanes] = head
            far[row, STRIP : 2 * STRIP, lane : lane + lanes] = tail
        far[row, 2 * STRIP : 2 * STRIP + RADIUS, :] = left[0, row].astype(jnp.float32)
        far[row, 2 * STRIP + RADIUS : 2 * STRIP + 2 * RADIUS, :] = right[0, row].astype(jnp.float32)
    for row in range(tile_rows):
        for ref, plane, target in ((qkv, 0, ends), (resid, 0, mine)):
            head, tail = edge_columns(ref, plane, row)
            target[row, 0:EDGE] = head[:EDGE]
            target[row, EDGE:STRIP] = tail[EDGE:]
    rows = 4
    span = 3 * STRIP
    for start in range(0, tile_rows, rows):
        count, keys = rows * STRIP, (rows + 2 * RADIUS) * span
        found = far[start : start + rows + 2 * RADIUS].reshape(keys, 2 * width + LANES).astype(jnp.bfloat16)
        q, k = iota((count, keys), 0), iota((count, keys), 1)
        q_col = q % STRIP
        q_col = jnp.where(q_col < EDGE, q_col, q_col + tile_cols - STRIP)
        k_col = k % span
        k_col = jnp.where(
            k_col < STRIP,
            k_col,
            jnp.where(
                k_col < 2 * STRIP,
                k_col + tile_cols - 2 * STRIP,
                jnp.where(
                    k_col < 2 * STRIP + RADIUS,
                    k_col - 2 * STRIP - RADIUS,
                    jnp.where(
                        k_col < 2 * STRIP + 2 * RADIUS,
                        k_col - 2 * STRIP - RADIUS + tile_cols,
                        -100 * tile_cols,
                    ),
                ),
            ),
        )
        bias = make_bias(
            q // STRIP + RADIUS, q_col, k // span, k_col, keep_row(count, found[:, 2 * width :])
        )
        mixed = tile_attend(
            ends[start : start + rows].reshape(count, width), found[:, :width], found[:, width : 2 * width], bias
        )
        out[start * STRIP : (start + rows) * STRIP] = finish(
            mixed.astype(jnp.bfloat16), mine[start : start + rows].reshape(count, width), w_out[...], modulation[...]
        )


def own_kernel(normed, w_qkv, out):
    out[...] = jnp.dot(normed[...], w_qkv[...], preferred_element_type=jnp.float32).astype(jnp.bfloat16)


def head_marks(width):
    feature, lane = iota((width, LANES), 0), iota((width, LANES), 1)
    head = width // HEADS
    return jnp.where((feature >= lane * head) & (feature < lane * head + head), 1.0, 0.0).astype(jnp.bfloat16)


def mark_heads(width):
    row, feature = iota((2 * LANES, width), 0) % LANES, iota((2 * LANES, width), 1)
    head = width // HEADS
    return jnp.where((feature >= row * head) & (feature < row * head + head), 1.0, 0.0).astype(jnp.bfloat16)


def halves_of(values):
    high = values.astype(jnp.bfloat16)
    low = (values - high.astype(jnp.float32)).astype(jnp.bfloat16)
    return high, low


def temporal(own, other_kv):
    width = own.shape[1] // 3
    scale = (width // HEADS) ** (-0.5)
    query = own[:, :width].astype(jnp.float32)
    key_gap = other_kv[:, :width].astype(jnp.float32) - own[:, width : 2 * width].astype(jnp.float32)
    high, low = halves_of(query * key_gap)
    marks = head_marks(width)
    gap = (
        jnp.dot(high, marks, preferred_element_type=jnp.float32)
        + jnp.dot(low, marks, preferred_element_type=jnp.float32)
    ) * scale
    own_weight = jnp.exp(jnp.minimum(-gap, 0.0))
    other_weight = jnp.exp(jnp.minimum(gap, 0.0))
    inverse = 1.0 / (own_weight + other_weight)
    spread = mark_heads(width)

    def share(weight):
        part = weight.astype(jnp.bfloat16).astype(jnp.float32) * inverse
        return jnp.dot(jnp.concatenate(halves_of(part), axis=1), spread, preferred_element_type=jnp.float32)

    mixed = share(own_weight) * own[:, 2 * width :].astype(jnp.float32) + share(other_weight) * other_kv[
        :, width:
    ].astype(jnp.float32)
    return mixed


def temporal_kernel(own, other, w_qkv, out):
    width = other.shape[1]
    other_kv = jnp.dot(other[...], w_qkv[:, width:], preferred_element_type=jnp.float32).astype(jnp.bfloat16)
    out[...] = temporal(own[...], other_kv).astype(jnp.bfloat16)


def last_kernel(own, other, w_qkv, inner, rim, out, mixed_ref):
    tile_rows, tile_cols, width = out.shape[1:]
    other_kv = jnp.dot(other[...], w_qkv[:, width:], preferred_element_type=jnp.float32).astype(jnp.bfloat16)
    edge = temporal(own[...], other_kv)
    strips = tile_cols // STRIP - 1
    for row in range(tile_rows):
        if row < RADIUS:
            source, at = rim, row
        elif row < tile_rows - RADIUS:
            source, at = inner, row - RADIUS
        else:
            source, at = rim, row - tile_rows + 2 * RADIUS
        mixed_ref[row, 0:EDGE] = edge[STRIP * row : STRIP * row + EDGE]
        mixed_ref[row, tile_cols - EDGE :] = edge[STRIP * row + EDGE : STRIP * row + STRIP]
        for strip in range(strips):
            piece = source[strip, STRIP * at : STRIP * at + STRIP, :].astype(jnp.float32)
            mixed_ref[row, EDGE + STRIP * strip : EDGE + STRIP * strip + STRIP] = piece
    out[0] = mixed_ref[...].astype(jnp.bfloat16)


def call(body, out_shape, operands, scratch=(), flops=0, limit=32):
    size = sum(x.size * x.dtype.itemsize for x in operands)
    return pl.pallas_call(
        body,
        out_shape=out_shape,
        in_specs=[VMEM] * len(operands),
        out_specs=VMEM,
        scratch_shapes=list(scratch),
        cost_estimate=pl.CostEstimate(flops=flops, bytes_accessed=size, transcendentals=0),
        compiler_params=pltpu.CompilerParams(vmem_limit_bytes=limit * MIB),
        name=body.__name__,
    )(*operands)


def fast_device(resid, spatial_qkv, key_keep, w_spatial_out, modulation, w_temporal_qkv):
    frame_count, tile_rows, tile_cols, width = resid.shape
    qkv = spatial_qkv[:, 0]
    keep = jnp.broadcast_to(key_keep.astype(jnp.bfloat16)[..., None], key_keep.shape + (LANES,))
    strips = tile_cols // STRIP - 1
    row_count, col_count = lax.axis_size("row"), lax.axis_size("col")
    rising = lambda count: [(i, i + 1) for i in range(count - 1)]
    falling = lambda count: [(i + 1, i) for i in range(count - 1)]
    swap = [(0, 1), (1, 0)]
    bf16 = jnp.bfloat16

    def border(rows):
        return jnp.concatenate([qkv[1, rows], qkv[2, rows], keep[0, rows]], axis=-1)[None]

    above = lax.ppermute(border(slice(tile_rows - RADIUS, None)), "row", rising(row_count))
    below = lax.ppermute(border(slice(0, RADIUS)), "row", falling(row_count))

    half = (tile_rows - 2 * RADIUS) * STRIP
    inner = call(
        inner_kernel,
        jax.ShapeDtypeStruct((strips, half, width), bf16),
        (qkv, keep, resid, w_spatial_out, modulation),
        [pltpu.VMEM((strips, half, width), bf16)],
        flops=10**9,
    )
    inner_other = lax.ppermute(inner, "tm", swap)

    def side(cols):
        local = jnp.concatenate([qkv[1, :, cols], qkv[2, :, cols], keep[0, :, cols]], axis=-1)
        return jnp.concatenate([above[0, :, cols], local, below[0, :, cols]], axis=0)[None]

    left = lax.ppermute(side(slice(tile_cols - RADIUS, None)), "col", rising(col_count))
    right = lax.ppermute(side(slice(0, RADIUS)), "col", falling(col_count))

    rim_half = 2 * RADIUS * STRIP
    rim = call(
        rim_kernel,
        jax.ShapeDtypeStruct((strips, rim_half, width), bf16),
        (qkv, keep, above, below, resid, w_spatial_out, modulation),
        [pltpu.VMEM((strips, rim_half, width), bf16)],
        flops=10**9,
    )
    rim_other = lax.ppermute(rim, "tm", swap)

    edge_count = tile_rows * STRIP
    edge = call(
        edge_kernel,
        jax.ShapeDtypeStruct((edge_count, width), bf16),
        (qkv, keep, above, below, left, right, resid, w_spatial_out, modulation),
        [
            pltpu.VMEM((tile_rows + 2 * RADIUS, 3 * STRIP, 2 * width + LANES), jnp.float32),
            pltpu.VMEM((tile_rows, STRIP, width), jnp.float32),
            pltpu.VMEM((tile_rows, STRIP, width), jnp.float32),
        ],
        flops=10**9,
    )
    edge_other = lax.ppermute(edge, "tm", swap)

    def own(normed):
        count = normed.shape[0]
        return call(
            own_kernel,
            jax.ShapeDtypeStruct((count, 3 * width), bf16),
            (normed, w_temporal_qkv),
            flops=count * width * width * 6,
        )

    def attend(own_qkv, other):
        count = other.shape[0]
        return call(
            temporal_kernel,
            jax.ShapeDtypeStruct((count, width), bf16),
            (own_qkv, other, w_temporal_qkv),
            flops=count * width * width * 4,
        )

    flat = lambda x: x.reshape(-1, width)
    inner_own, rim_own, edge_own = own(flat(inner)), own(flat(rim)), own(edge)
    inner_done = attend(inner_own, flat(inner_other)).reshape(inner.shape)
    rim_done = attend(rim_own, flat(rim_other)).reshape(rim.shape)
    return call(
        last_kernel,
        jax.ShapeDtypeStruct(resid.shape, bf16),
        (edge_own, edge_other, w_temporal_qkv, inner_done, rim_done),
        [pltpu.VMEM((tile_rows, tile_cols, width), jnp.float32)],
        flops=edge_count * width * width * 4,
    )


def per_device(resid, *rest):
    frame_count, tile_rows, tile_cols, width = resid.shape
    fits = (
        frame_count == 1
        and lax.axis_size("tm") == 2
        and width == 9 * LANES
        and tile_cols % STRIP == 0
        and tile_cols >= 2 * STRIP
        and tile_rows % 4 == 0
        and tile_rows > 2 * RADIUS
    )
    return (fast_device if fits else general_device)(resid, *rest)


def solution(mesh):
    return jax.shard_map(
        per_device,
        mesh=mesh,
        in_specs=(
            P("tm", "row", "col", None),
            P(None, "tm", "row", "col", None),
            P("tm", "row", "col"),
            P(),
            P(),
            P(),
        ),
        out_specs=P("tm", "row", "col", None),
        check_vma=False,
    )
```

```python
import functools
import math

import jax
import jax.numpy as jnp
from jax import lax
from jax.experimental import pallas as pl
from jax.experimental.pallas import tpu as pltpu
from jax.sharding import PartitionSpec as P

HEADS = 16
RADIUS = 3


NEG_FILL = -1e30
EPSILON = 1e-06

LANES = 128
STRIP = 8
EDGE = STRIP // 2
MIB = 1024 * 1024
VMEM = pl.BlockSpec(memory_space=pltpu.VMEM)


def extended(array, sides, width):
    for axis, dim in sides:
        count, length = (lax.axis_size(axis), array.shape[dim])
        up = [(i, (i + 1) % count) for i in range(count - 1)]
        down = [(j, i) for i, j in up]
        last = lax.slice_in_dim(array, length - width, length, axis=dim)
        leading = lax.slice_in_dim(array, 0, width, axis=dim)
        before = lax.ppermute(last, axis, up)
        after = lax.ppermute(leading, axis, down)
        array = jnp.concatenate([before, array, after], axis=dim)
    return array


def softmax_parts(scores, allowed):
    masked = jnp.where(allowed, scores, NEG_FILL)
    top_score = jnp.max(masked, -1, keepdims=True)
    weights_f = jnp.where(allowed, jnp.exp(masked - top_score), 0.0)
    return (weights_f.astype(jnp.bfloat16), jnp.sum(weights_f, -1))


def frame_attend(gathered, head_count):
    frames_all, single, items, width_three = gathered.shape
    width = width_three // 3
    head_size = width // head_count
    split_qkv = gathered.reshape(frames_all, items, 3, head_count, head_size)
    scores = jnp.einsum(
        "fphd,gphd->phfg",
        split_qkv[:, :, 0],
        split_qkv[:, :, 1],
        preferred_element_type=jnp.float32,
    ) * head_size ** (-0.5)
    weights_b, totals = softmax_parts(scores, True)
    weighted = jnp.einsum(
        "phfg,gphd->fphd", weights_b, split_qkv[:, :, 2], preferred_element_type=jnp.float32
    )
    result = weighted / jnp.transpose(totals, (2, 0, 1))[..., None]
    return result.astype(jnp.bfloat16).reshape(frames_all, single, items, width)


def general_device(resid, spatial_qkv, key_keep, w_spatial_out, modulation, w_temporal_qkv):
    frame_count, tile_rows, tile_cols, width = resid.shape
    head_size = width // HEADS
    score_scale = head_size ** (-0.5)
    tile_tokens = tile_rows * tile_cols
    pair = spatial_qkv[1:3]
    keep_flags = key_keep.astype(jnp.bfloat16)[None, :, :, :, None]
    padded_pair, padded_keep = (
        extended(pair, (("row", 2), ("col", 3)), RADIUS),
        extended(keep_flags, (("row", 2), ("col", 3)), RADIUS),
    )
    pad_rows = tile_rows + 2 * RADIUS
    pad_cols = tile_cols + 2 * RADIUS
    key_count = pad_rows * pad_cols
    queries = spatial_qkv[0].reshape(frame_count, tile_tokens, HEADS, head_size)
    keys_pad = padded_pair[0].reshape(frame_count, key_count, HEADS, head_size)
    values_pad = padded_pair[1].reshape(frame_count, key_count, HEADS, head_size)
    query_index = jnp.arange(tile_tokens)
    query_row = query_index // tile_cols
    query_col = query_index % tile_cols
    key_index = jnp.arange(key_count)
    key_row = key_index // pad_cols
    key_col = key_index % pad_cols
    row_gap = key_row[None, :] - query_row[:, None] - RADIUS
    col_gap = key_col[None, :] - query_col[:, None] - RADIUS
    in_window = (jnp.abs(row_gap) <= RADIUS) & (jnp.abs(col_gap) <= RADIUS)
    itself = (row_gap == 0) & (col_gap == 0)
    key_live = padded_keep.reshape(frame_count, key_count) > 0.5
    allowed = (in_window[None] & (key_live[:, None, :] | itself[None]))[:, None]
    scores = (
        jnp.einsum("fqhd,fkhd->fhqk", queries, keys_pad, preferred_element_type=jnp.float32)
        * score_scale
    )
    weights_b, totals = softmax_parts(scores, allowed)
    weighted = jnp.einsum(
        "fhqk,fkhd->fqhd", weights_b, values_pad, preferred_element_type=jnp.float32
    )
    spatial_heads = (weighted / jnp.transpose(totals, (0, 2, 1))[..., None]).astype(jnp.bfloat16)
    spatial_heads = spatial_heads.reshape(frame_count * tile_tokens, width)
    stream = resid.reshape(frame_count * tile_tokens, width).astype(jnp.float32) + jnp.dot(
        spatial_heads, w_spatial_out, preferred_element_type=jnp.float32
    )
    average = jnp.mean(stream, -1, keepdims=True)
    centered = stream - average
    variance = jnp.mean(centered * centered, -1, keepdims=True)
    normed = (
        centered * lax.rsqrt(variance + EPSILON) * (1.0 + modulation[1]) + modulation[0]
    ).astype(jnp.bfloat16)
    tm_count = lax.axis_size("tm")
    part_tokens = tile_tokens // tm_count
    normed_parts = normed.reshape(frame_count, tm_count, part_tokens, width)
    gathered = lax.all_to_all(normed_parts, "tm", split_axis=1, concat_axis=0, tiled=True)
    frames_all, single, items, unused = gathered.shape
    projected = jnp.dot(
        gathered.reshape(frames_all * single * items, width),
        w_temporal_qkv,
        preferred_element_type=jnp.float32,
    ).astype(jnp.bfloat16)
    projected = projected.reshape(frames_all, single, items, 3 * width)
    result = lax.all_to_all(
        frame_attend(projected, HEADS), "tm", split_axis=0, concat_axis=1, tiled=True
    )
    return result.reshape(frame_count, tile_rows, tile_cols, width)


def iota(shape, dim):
    return lax.broadcasted_iota(jnp.int32, shape, dim)


def attend(tiles):
    width = tiles[0][0].shape[1]
    head = width // HEADS
    factor = head ** (-0.5) * math.log2(math.e)
    lane = iota((1, 2 * LANES), 1)
    spans = []
    for pair in range(HEADS // 2):
        start = LANES * pair
        low = 2 * head * pair - start
        spans.append((slice(start, start + 2 * LANES), low, low + head, low + 2 * head))
    scores = []
    for queries, keys, values, bias in tiles:
        for span, low, mid, high in spans:
            first = jnp.where((lane >= low) & (lane < mid), queries[:, span], 0.0)
            second = jnp.where((lane >= mid) & (lane < high), queries[:, span], 0.0)
            both = jnp.concatenate([first, second], axis=0).astype(jnp.bfloat16)
            scores.append(
                lax.dot_general(
                    both, keys[:, span], (((1,), (1,)), ((), ())), preferred_element_type=jnp.float32
                )
            )
    weights = []
    for index, (queries, keys, values, bias) in enumerate(tiles):
        bias_two = jnp.concatenate([bias, bias], axis=0)
        for pair in range(len(spans)):
            score = scores[index * len(spans) + pair] + bias_two
            top = jnp.max(score, -1, keepdims=True)
            weight = jnp.exp2((score - top) * factor)
            weights.append((weight.astype(jnp.bfloat16), 1.0 / jnp.sum(weight, -1, keepdims=True)))
    results = []
    edge_lane = iota((1, LANES), 1)
    for index, (queries, keys, values, bias) in enumerate(tiles):
        count = queries.shape[0]
        pairs = []
        for pair, (span, low, mid, high) in enumerate(spans):
            weight, inverse = weights[index * len(spans) + pair]
            mixed = jnp.dot(weight, values[:, span], preferred_element_type=jnp.float32) * inverse
            pairs.append(jnp.where(lane < mid, mixed[:count], mixed[count:]))
        blocks = [pairs[0][:, :LANES]]
        for pair in range(1, len(spans)):
            cut = spans[pair][1]
            blocks.append(jnp.where(edge_lane < cut, pairs[pair - 1][:, LANES:], pairs[pair][:, :LANES]))
        blocks.append(pairs[-1][:, LANES:])
        results.append(jnp.concatenate(blocks, axis=1))
    return results


def keep_row(count, keep):
    picker = jnp.where(iota((count, LANES), 1) == 0, 1.0, 0.0).astype(jnp.bfloat16)
    return lax.dot_general(
        picker, keep, (((1,), (1,)), ((), ())), preferred_element_type=jnp.float32
    )


def make_bias(q_row, q_col, k_row, k_col, keep):
    row_gap, col_gap = k_row - q_row, k_col - q_col
    near = (jnp.abs(row_gap) <= RADIUS) & (jnp.abs(col_gap) <= RADIUS)
    itself = (row_gap == 0) & (col_gap == 0)
    return jnp.where(near & ((keep > 0.5) | itself), 0.0, NEG_FILL)


def strip_bias(rows, keep):
    count, keys = rows * STRIP, (rows + 2 * RADIUS) * 2 * STRIP
    q, k = iota((count, keys), 0), iota((count, keys), 1)
    return make_bias(
        q // STRIP + RADIUS, q % STRIP + EDGE, k // (2 * STRIP), k % (2 * STRIP), keep_row(count, keep)
    )


def finish(heads, resid, w_out, modulation):
    stream = resid + jnp.dot(heads, w_out, preferred_element_type=jnp.float32)
    average = jnp.mean(stream, -1, keepdims=True)
    centered = stream - average
    variance = jnp.mean(centered * centered, -1, keepdims=True)
    scaled = centered * lax.rsqrt(variance + EPSILON)
    return (scaled * (1.0 + modulation[1:2]) + modulation[0:1]).astype(jnp.bfloat16)


def window(ref, plane, rows, strip):
    found = ref[plane, rows, pl.ds(STRIP * strip, 2 * STRIP), :].astype(jnp.float32)
    return found.reshape(found.shape[0] * found.shape[1], found.shape[2]).astype(jnp.bfloat16)


def middle(ref, plane, rows, strip):
    found = ref[plane, rows, pl.ds(STRIP * strip, 2 * STRIP), :].astype(jnp.float32)
    found = found[:, EDGE : EDGE + STRIP]
    return found.reshape(found.shape[0] * STRIP, found.shape[2])


INNER_ROWS = 6
INNER_BATCH = 4
RIM_BATCH = 4
EDGE_BATCH = 3


def batched(tiles, size):
    found = []
    for start in range(0, len(tiles), size):
        found += attend(tiles[start : start + size])
    return found


def inner_kernel(qkv, keep, resid, w_out, modulation, out, heads):
    tile_rows, tile_cols, width = resid.shape[1:]
    rows = tile_rows - 2 * RADIUS
    strips = tile_cols // STRIP - 1
    every = pl.ds(0, tile_rows)
    mine = pl.ds(RADIUS, rows)
    step = INNER_ROWS
    tiles = []
    for strip in range(strips):
        queries = middle(qkv, 0, mine, strip)
        keys, values, flags = (window(ref, plane, every, strip) for ref, plane in ((qkv, 1), (qkv, 2), (keep, 0)))
        for start in range(0, rows, step):
            span = slice(start * 2 * STRIP, (start + step + 2 * RADIUS) * 2 * STRIP)
            tiles.append(
                (
                    queries[start * STRIP : (start + step) * STRIP],
                    keys[span],
                    values[span],
                    strip_bias(step, flags[span]),
                )
            )
    mixed = batched(tiles, INNER_BATCH * rows // step)
    heads[...] = jnp.concatenate(mixed, axis=0).astype(jnp.bfloat16)
    source = jnp.concatenate([middle(resid, 0, mine, strip) for strip in range(strips)], axis=0)
    out[...] = finish(heads[...], source, w_out[...], modulation[...]).reshape(out.shape)


def rim_kernel(qkv, keep, above, below, resid, w_out, modulation, out, heads):
    tile_rows, tile_cols, width = resid.shape[1:]
    strips = tile_cols // STRIP - 1
    near = 2 * RADIUS
    tiles = []
    sources = []
    for strip in range(strips):
        for side in range(2):
            inner = pl.ds(0 if side == 0 else tile_rows - near, near)
            mine = pl.ds(0 if side == 0 else tile_rows - RADIUS, RADIUS)
            halo_ref = above if side == 0 else below
            halo = window(halo_ref, 0, pl.ds(0, RADIUS), strip)
            parts = []
            for at, local in (
                (0, window(qkv, 1, inner, strip)),
                (width, window(qkv, 2, inner, strip)),
                (2 * width, window(keep, 0, inner, strip)),
            ):
                far = halo[:, at : at + local.shape[1]]
                parts.append(jnp.concatenate([far, local] if side == 0 else [local, far], axis=0))
            bias = strip_bias(RADIUS, parts[2])
            tiles.append((middle(qkv, 0, mine, strip), parts[0], parts[1], bias))
            sources.append(middle(resid, 0, mine, strip))
    heads[...] = jnp.concatenate(batched(tiles, RIM_BATCH), axis=0).astype(jnp.bfloat16)
    out[...] = finish(heads[...], jnp.concatenate(sources, axis=0), w_out[...], modulation[...]).reshape(out.shape)


def edge_columns(ref, plane, row):
    found = ref[plane, row].astype(jnp.float32)
    return found[:STRIP], found[found.shape[0] - STRIP :]


def edge_kernel(qkv, keep, above, below, left, right, resid, w_out, modulation, out, heads, far, ends, mine):
    tile_rows, tile_cols, width = resid.shape[1:]
    pad_rows = tile_rows + 2 * RADIUS
    far[...] = jnp.zeros_like(far)
    for row in range(pad_rows):
        local = row - RADIUS
        if 0 <= local < tile_rows:
            sources = ((qkv, 1, local, 0, width), (qkv, 2, local, width, width), (keep, 0, local, 2 * width, LANES))
        elif local < 0:
            sources = ((above, 0, row, 0, 2 * width + LANES),)
        else:
            sources = ((below, 0, local - tile_rows, 0, 2 * width + LANES),)
        for ref, plane, at, lane, lanes in sources:
            head, tail = edge_columns(ref, plane, at)
            far[row, 0:STRIP, lane : lane + lanes] = head
            far[row, STRIP : 2 * STRIP, lane : lane + lanes] = tail
        far[row, 2 * STRIP : 2 * STRIP + RADIUS, :] = left[0, row].astype(jnp.float32)
        far[row, 2 * STRIP + RADIUS : 2 * STRIP + 2 * RADIUS, :] = right[0, row].astype(jnp.float32)
    for row in range(tile_rows):
        for ref, plane, target in ((qkv, 0, ends), (resid, 0, mine)):
            head, tail = edge_columns(ref, plane, row)
            target[row, 0:EDGE] = head[:EDGE]
            target[row, EDGE:STRIP] = tail[EDGE:]
    rows = 4
    span = 3 * STRIP
    tiles = []
    for start in range(0, tile_rows, rows):
        count, keys = rows * STRIP, (rows + 2 * RADIUS) * span
        found = far[start : start + rows + 2 * RADIUS].reshape(keys, 2 * width + LANES).astype(jnp.bfloat16)
        q, k = iota((count, keys), 0), iota((count, keys), 1)
        q_col = q % STRIP
        q_col = jnp.where(q_col < EDGE, q_col, q_col + tile_cols - STRIP)
        k_col = k % span
        k_col = jnp.where(
            k_col < STRIP,
            k_col,
            jnp.where(
                k_col < 2 * STRIP,
                k_col + tile_cols - 2 * STRIP,
                jnp.where(
                    k_col < 2 * STRIP + RADIUS,
                    k_col - 2 * STRIP - RADIUS,
                    jnp.where(
                        k_col < 2 * STRIP + 2 * RADIUS,
                        k_col - 2 * STRIP - RADIUS + tile_cols,
                        -100 * tile_cols,
                    ),
                ),
            ),
        )
        bias = make_bias(
            q // STRIP + RADIUS, q_col, k // span, k_col, keep_row(count, found[:, 2 * width :])
        )
        tiles.append(
            (ends[start : start + rows].reshape(count, width), found[:, :width], found[:, width : 2 * width], bias)
        )
    mixed = batched(tiles, EDGE_BATCH)
    source = mine[...].reshape(tile_rows * STRIP, width)
    heads[...] = jnp.concatenate(mixed, axis=0).astype(jnp.bfloat16)
    out[...] = finish(heads[...], source, w_out[...], modulation[...])


def own_kernel(normed, w_qkv, out):
    out[...] = jnp.dot(normed[...], w_qkv[...], preferred_element_type=jnp.float32).astype(jnp.bfloat16)


def head_marks(width):
    feature, lane = iota((width, LANES), 0), iota((width, LANES), 1)
    head = width // HEADS
    return jnp.where((feature >= lane * head) & (feature < lane * head + head), 1.0, 0.0).astype(jnp.bfloat16)


def mark_heads(width):
    row, feature = iota((2 * LANES, width), 0) % LANES, iota((2 * LANES, width), 1)
    head = width // HEADS
    return jnp.where((feature >= row * head) & (feature < row * head + head), 1.0, 0.0).astype(jnp.bfloat16)


def halves_of(values):
    high = values.astype(jnp.bfloat16)
    low = (values - high.astype(jnp.float32)).astype(jnp.bfloat16)
    return high, low


def temporal(own, other_kv):
    width = own.shape[1] // 3
    scale = (width // HEADS) ** (-0.5)
    query = own[:, :width].astype(jnp.float32)
    key_gap = other_kv[:, :width].astype(jnp.float32) - own[:, width : 2 * width].astype(jnp.float32)
    high, low = halves_of(query * key_gap)
    marks = head_marks(width)
    gap = (
        jnp.dot(high, marks, preferred_element_type=jnp.float32)
        + jnp.dot(low, marks, preferred_element_type=jnp.float32)
    ) * scale
    own_weight = jnp.exp(jnp.minimum(-gap, 0.0))
    other_weight = jnp.exp(jnp.minimum(gap, 0.0))
    inverse = 1.0 / (own_weight + other_weight)
    spread = mark_heads(width)

    def share(weight):
        part = weight.astype(jnp.bfloat16).astype(jnp.float32) * inverse
        return jnp.dot(jnp.concatenate(halves_of(part), axis=1), spread, preferred_element_type=jnp.float32)

    mixed = share(own_weight) * own[:, 2 * width :].astype(jnp.float32) + share(other_weight) * other_kv[
        :, width:
    ].astype(jnp.float32)
    return mixed


def temporal_kernel(own, other, w_qkv, out):
    width = other.shape[1]
    other_kv = jnp.dot(other[...], w_qkv[:, width:], preferred_element_type=jnp.float32).astype(jnp.bfloat16)
    out[...] = temporal(own[...], other_kv).astype(jnp.bfloat16)


def last_kernel(own, other, w_qkv, inner, rim, out, mixed_ref):
    tile_rows, tile_cols, width = out.shape[1:]
    other_kv = jnp.dot(other[...], w_qkv[:, width:], preferred_element_type=jnp.float32).astype(jnp.bfloat16)
    edge = temporal(own[...], other_kv)
    strips = tile_cols // STRIP - 1
    for row in range(tile_rows):
        if row < RADIUS:
            source, at = rim, row
        elif row < tile_rows - RADIUS:
            source, at = inner, row - RADIUS
        else:
            source, at = rim, row - tile_rows + 2 * RADIUS
        mixed_ref[row, 0:EDGE] = edge[STRIP * row : STRIP * row + EDGE]
        mixed_ref[row, tile_cols - EDGE :] = edge[STRIP * row + EDGE : STRIP * row + STRIP]
        for strip in range(strips):
            piece = source[strip, STRIP * at : STRIP * at + STRIP, :].astype(jnp.float32)
            mixed_ref[row, EDGE + STRIP * strip : EDGE + STRIP * strip + STRIP] = piece
    out[0] = mixed_ref[...].astype(jnp.bfloat16)


def call(body, out_shape, operands, scratch=(), flops=0, limit=32):
    size = sum(x.size * x.dtype.itemsize for x in operands)
    return pl.pallas_call(
        body,
        out_shape=out_shape,
        in_specs=[VMEM] * len(operands),
        out_specs=VMEM,
        scratch_shapes=list(scratch),
        cost_estimate=pl.CostEstimate(flops=flops, bytes_accessed=size, transcendentals=0),
        compiler_params=pltpu.CompilerParams(vmem_limit_bytes=limit * MIB),
        name=body.__name__,
    )(*operands)


def fast_device(resid, spatial_qkv, key_keep, w_spatial_out, modulation, w_temporal_qkv):
    frame_count, tile_rows, tile_cols, width = resid.shape
    qkv = spatial_qkv[:, 0]
    keep = jnp.broadcast_to(key_keep.astype(jnp.bfloat16)[..., None], key_keep.shape + (LANES,))
    strips = tile_cols // STRIP - 1
    row_count, col_count = lax.axis_size("row"), lax.axis_size("col")
    rising = lambda count: [(i, i + 1) for i in range(count - 1)]
    falling = lambda count: [(i + 1, i) for i in range(count - 1)]
    swap = [(0, 1), (1, 0)]
    bf16 = jnp.bfloat16

    def border(rows):
        return jnp.concatenate([qkv[1, rows], qkv[2, rows], keep[0, rows]], axis=-1)[None]

    above = lax.ppermute(border(slice(tile_rows - RADIUS, None)), "row", rising(row_count))
    below = lax.ppermute(border(slice(0, RADIUS)), "row", falling(row_count))

    half = (tile_rows - 2 * RADIUS) * STRIP
    inner = call(
        inner_kernel,
        jax.ShapeDtypeStruct((strips, half, width), bf16),
        (qkv, keep, resid, w_spatial_out, modulation),
        [pltpu.VMEM((strips * half, width), bf16)],
        flops=10**9,
    )
    inner_other = lax.ppermute(inner, "tm", swap)

    def side(cols):
        local = jnp.concatenate([qkv[1, :, cols], qkv[2, :, cols], keep[0, :, cols]], axis=-1)
        return jnp.concatenate([above[0, :, cols], local, below[0, :, cols]], axis=0)[None]

    left = lax.ppermute(side(slice(tile_cols - RADIUS, None)), "col", rising(col_count))
    right = lax.ppermute(side(slice(0, RADIUS)), "col", falling(col_count))

    rim_half = 2 * RADIUS * STRIP
    rim = call(
        rim_kernel,
        jax.ShapeDtypeStruct((strips, rim_half, width), bf16),
        (qkv, keep, above, below, resid, w_spatial_out, modulation),
        [pltpu.VMEM((strips * rim_half, width), bf16)],
        flops=10**9,
    )
    rim_other = lax.ppermute(rim, "tm", swap)

    edge_count = tile_rows * STRIP
    edge = call(
        edge_kernel,
        jax.ShapeDtypeStruct((edge_count, width), bf16),
        (qkv, keep, above, below, left, right, resid, w_spatial_out, modulation),
        [
            pltpu.VMEM((edge_count, width), bf16),
            pltpu.VMEM((tile_rows + 2 * RADIUS, 3 * STRIP, 2 * width + LANES), jnp.float32),
            pltpu.VMEM((tile_rows, STRIP, width), jnp.float32),
            pltpu.VMEM((tile_rows, STRIP, width), jnp.float32),
        ],
        flops=10**9,
    )
    edge_other = lax.ppermute(edge, "tm", swap)

    def own(normed):
        count = normed.shape[0]
        return call(
            own_kernel,
            jax.ShapeDtypeStruct((count, 3 * width), bf16),
            (normed, w_temporal_qkv),
            flops=count * width * width * 6,
        )

    def attend(own_qkv, other):
        count = other.shape[0]
        return call(
            temporal_kernel,
            jax.ShapeDtypeStruct((count, width), bf16),
            (own_qkv, other, w_temporal_qkv),
            flops=count * width * width * 4,
        )

    flat = lambda x: x.reshape(-1, width)
    inner_own, rim_own, edge_own = own(flat(inner)), own(flat(rim)), own(edge)
    inner_done = attend(inner_own, flat(inner_other)).reshape(inner.shape)
    rim_done = attend(rim_own, flat(rim_other)).reshape(rim.shape)
    return call(
        last_kernel,
        jax.ShapeDtypeStruct(resid.shape, bf16),
        (edge_own, edge_other, w_temporal_qkv, inner_done, rim_done),
        [pltpu.VMEM((tile_rows, tile_cols, width), jnp.float32)],
        flops=edge_count * width * width * 4,
    )


def per_device(resid, *rest):
    frame_count, tile_rows, tile_cols, width = resid.shape
    fits = (
        frame_count == 1
        and lax.axis_size("tm") == 2
        and width == 9 * LANES
        and tile_cols % STRIP == 0
        and tile_cols >= 2 * STRIP
        and tile_rows % 4 == 0
        and tile_rows > 2 * RADIUS
    )
    return (fast_device if fits else general_device)(resid, *rest)


def solution(mesh):
    return jax.shard_map(
        per_device,
        mesh=mesh,
        in_specs=(
            P("tm", "row", "col", None),
            P(None, "tm", "row", "col", None),
            P("tm", "row", "col"),
            P(),
            P(),
            P(),
        ),
        out_specs=P("tm", "row", "col", None),
        check_vma=False,
    )
```

```python
import functools
import math

import jax
import jax.numpy as jnp
import numpy as np
from jax import lax
from jax.experimental import pallas as pl
from jax.experimental.pallas import tpu as pltpu
from jax.sharding import PartitionSpec as P

HEADS = 16
RADIUS = 3


NEG_FILL = -1e30
EPSILON = 1e-06

LANES = 128
STRIP = 8
EDGE = STRIP // 2
MIB = 1024 * 1024
VMEM = pl.BlockSpec(memory_space=pltpu.VMEM)


def extended(array, sides, width):
    for axis, dim in sides:
        count, length = (lax.axis_size(axis), array.shape[dim])
        up = [(i, (i + 1) % count) for i in range(count - 1)]
        down = [(j, i) for i, j in up]
        last = lax.slice_in_dim(array, length - width, length, axis=dim)
        leading = lax.slice_in_dim(array, 0, width, axis=dim)
        before = lax.ppermute(last, axis, up)
        after = lax.ppermute(leading, axis, down)
        array = jnp.concatenate([before, array, after], axis=dim)
    return array


def softmax_parts(scores, allowed):
    masked = jnp.where(allowed, scores, NEG_FILL)
    top_score = jnp.max(masked, -1, keepdims=True)
    weights_f = jnp.where(allowed, jnp.exp(masked - top_score), 0.0)
    return (weights_f.astype(jnp.bfloat16), jnp.sum(weights_f, -1))


def frame_attend(gathered, head_count):
    frames_all, single, items, width_three = gathered.shape
    width = width_three // 3
    head_size = width // head_count
    split_qkv = gathered.reshape(frames_all, items, 3, head_count, head_size)
    scores = jnp.einsum(
        "fphd,gphd->phfg",
        split_qkv[:, :, 0],
        split_qkv[:, :, 1],
        preferred_element_type=jnp.float32,
    ) * head_size ** (-0.5)
    weights_b, totals = softmax_parts(scores, True)
    weighted = jnp.einsum(
        "phfg,gphd->fphd", weights_b, split_qkv[:, :, 2], preferred_element_type=jnp.float32
    )
    result = weighted / jnp.transpose(totals, (2, 0, 1))[..., None]
    return result.astype(jnp.bfloat16).reshape(frames_all, single, items, width)


def general_device(resid, spatial_qkv, key_keep, w_spatial_out, modulation, w_temporal_qkv):
    frame_count, tile_rows, tile_cols, width = resid.shape
    head_size = width // HEADS
    score_scale = head_size ** (-0.5)
    tile_tokens = tile_rows * tile_cols
    pair = spatial_qkv[1:3]
    keep_flags = key_keep.astype(jnp.bfloat16)[None, :, :, :, None]
    padded_pair, padded_keep = (
        extended(pair, (("row", 2), ("col", 3)), RADIUS),
        extended(keep_flags, (("row", 2), ("col", 3)), RADIUS),
    )
    pad_rows = tile_rows + 2 * RADIUS
    pad_cols = tile_cols + 2 * RADIUS
    key_count = pad_rows * pad_cols
    queries = spatial_qkv[0].reshape(frame_count, tile_tokens, HEADS, head_size)
    keys_pad = padded_pair[0].reshape(frame_count, key_count, HEADS, head_size)
    values_pad = padded_pair[1].reshape(frame_count, key_count, HEADS, head_size)
    query_index = jnp.arange(tile_tokens)
    query_row = query_index // tile_cols
    query_col = query_index % tile_cols
    key_index = jnp.arange(key_count)
    key_row = key_index // pad_cols
    key_col = key_index % pad_cols
    row_gap = key_row[None, :] - query_row[:, None] - RADIUS
    col_gap = key_col[None, :] - query_col[:, None] - RADIUS
    in_window = (jnp.abs(row_gap) <= RADIUS) & (jnp.abs(col_gap) <= RADIUS)
    itself = (row_gap == 0) & (col_gap == 0)
    key_live = padded_keep.reshape(frame_count, key_count) > 0.5
    allowed = (in_window[None] & (key_live[:, None, :] | itself[None]))[:, None]
    scores = (
        jnp.einsum("fqhd,fkhd->fhqk", queries, keys_pad, preferred_element_type=jnp.float32)
        * score_scale
    )
    weights_b, totals = softmax_parts(scores, allowed)
    weighted = jnp.einsum(
        "fhqk,fkhd->fqhd", weights_b, values_pad, preferred_element_type=jnp.float32
    )
    spatial_heads = (weighted / jnp.transpose(totals, (0, 2, 1))[..., None]).astype(jnp.bfloat16)
    spatial_heads = spatial_heads.reshape(frame_count * tile_tokens, width)
    stream = resid.reshape(frame_count * tile_tokens, width).astype(jnp.float32) + jnp.dot(
        spatial_heads, w_spatial_out, preferred_element_type=jnp.float32
    )
    average = jnp.mean(stream, -1, keepdims=True)
    centered = stream - average
    variance = jnp.mean(centered * centered, -1, keepdims=True)
    normed = (
        centered * lax.rsqrt(variance + EPSILON) * (1.0 + modulation[1]) + modulation[0]
    ).astype(jnp.bfloat16)
    tm_count = lax.axis_size("tm")
    part_tokens = tile_tokens // tm_count
    normed_parts = normed.reshape(frame_count, tm_count, part_tokens, width)
    gathered = lax.all_to_all(normed_parts, "tm", split_axis=1, concat_axis=0, tiled=True)
    frames_all, single, items, unused = gathered.shape
    projected = jnp.dot(
        gathered.reshape(frames_all * single * items, width),
        w_temporal_qkv,
        preferred_element_type=jnp.float32,
    ).astype(jnp.bfloat16)
    projected = projected.reshape(frames_all, single, items, 3 * width)
    result = lax.all_to_all(
        frame_attend(projected, HEADS), "tm", split_axis=0, concat_axis=1, tiled=True
    )
    return result.reshape(frame_count, tile_rows, tile_cols, width)


def iota(shape, dim):
    return lax.broadcasted_iota(jnp.int32, shape, dim)


def attend(tiles):
    width = tiles[0][0].shape[1]
    head = width // HEADS
    factor = head ** (-0.5) * math.log2(math.e)
    lane = iota((1, 2 * LANES), 1)
    spans = []
    for pair in range(HEADS // 2):
        start = LANES * pair
        low = 2 * head * pair - start
        spans.append((slice(start, start + 2 * LANES), low, low + head, low + 2 * head))
    scores = []
    for queries, keys, values, bias in tiles:
        for span, low, mid, high in spans:
            first = jnp.where((lane >= low) & (lane < mid), queries[:, span], 0.0)
            second = jnp.where((lane >= mid) & (lane < high), queries[:, span], 0.0)
            both = jnp.concatenate([first, second], axis=0).astype(jnp.bfloat16)
            scores.append(
                lax.dot_general(
                    both, keys[:, span], (((1,), (1,)), ((), ())), preferred_element_type=jnp.float32
                )
            )
    weights = []
    for index, (queries, keys, values, bias) in enumerate(tiles):
        bias_two = jnp.concatenate([bias, bias], axis=0)
        for pair in range(len(spans)):
            score = scores[index * len(spans) + pair] + bias_two
            top = jnp.max(score, -1, keepdims=True)
            weight = jnp.exp2((score - top) * factor)
            weights.append((weight.astype(jnp.bfloat16), 1.0 / jnp.sum(weight, -1, keepdims=True)))
    results = []
    edge_lane = iota((1, LANES), 1)
    for index, (queries, keys, values, bias) in enumerate(tiles):
        count = queries.shape[0]
        pairs = []
        for pair, (span, low, mid, high) in enumerate(spans):
            weight, inverse = weights[index * len(spans) + pair]
            mixed = jnp.dot(weight, values[:, span], preferred_element_type=jnp.float32) * inverse
            pairs.append(jnp.where(lane < mid, mixed[:count], mixed[count:]))
        blocks = [pairs[0][:, :LANES]]
        for pair in range(1, len(spans)):
            cut = spans[pair][1]
            blocks.append(jnp.where(edge_lane < cut, pairs[pair - 1][:, LANES:], pairs[pair][:, :LANES]))
        blocks.append(pairs[-1][:, LANES:])
        results.append(jnp.concatenate(blocks, axis=1))
    return results


def keep_row(count, keep):
    picker = jnp.where(iota((count, LANES), 1) == 0, 1.0, 0.0).astype(jnp.bfloat16)
    return lax.dot_general(
        picker, keep, (((1,), (1,)), ((), ())), preferred_element_type=jnp.float32
    )


def make_bias(q_row, q_col, k_row, k_col, keep):
    row_gap, col_gap = k_row - q_row, k_col - q_col
    near = (jnp.abs(row_gap) <= RADIUS) & (jnp.abs(col_gap) <= RADIUS)
    itself = (row_gap == 0) & (col_gap == 0)
    return jnp.where(near & ((keep > 0.5) | itself), 0.0, NEG_FILL)


def strip_bias(rows, keep):
    count, keys = rows * STRIP, (rows + 2 * RADIUS) * 2 * STRIP
    q, k = iota((count, keys), 0), iota((count, keys), 1)
    return make_bias(
        q // STRIP + RADIUS, q % STRIP + EDGE, k // (2 * STRIP), k % (2 * STRIP), keep_row(count, keep)
    )


def finish(heads, resid, w_out, modulation):
    stream = resid + jnp.dot(heads, w_out, preferred_element_type=jnp.float32)
    average = jnp.mean(stream, -1, keepdims=True)
    centered = stream - average
    variance = jnp.mean(centered * centered, -1, keepdims=True)
    scaled = centered * lax.rsqrt(variance + EPSILON)
    return (scaled * (1.0 + modulation[1:2]) + modulation[0:1]).astype(jnp.bfloat16)


def window(ref, plane, rows, strip):
    found = ref[plane, rows, pl.ds(STRIP * strip, 2 * STRIP), :].astype(jnp.float32)
    return found.reshape(found.shape[0] * found.shape[1], found.shape[2]).astype(jnp.bfloat16)


def middle(ref, plane, rows, strip):
    found = ref[plane, rows, pl.ds(STRIP * strip, 2 * STRIP), :].astype(jnp.float32)
    found = found[:, EDGE : EDGE + STRIP]
    return found.reshape(found.shape[0] * STRIP, found.shape[2])


INNER_ROWS = 6
INNER_BATCH = 4
RIM_BATCH = 4
EDGE_BATCH = 3


def batched(tiles, size):
    found = []
    for start in range(0, len(tiles), size):
        found += attend(tiles[start : start + size])
    return found


def inner_kernel(qkv, keep, resid_hbm, w_hbm, modulation, out, resid, w_out, heads, arrived):
    copies = [
        pltpu.make_async_copy(resid_hbm, resid, arrived.at[0]),
        pltpu.make_async_copy(w_hbm, w_out, arrived.at[1]),
    ]
    for copy in copies:
        copy.start()
    tile_rows, tile_cols, width = resid.shape[1:]
    rows = tile_rows - 2 * RADIUS
    strips = tile_cols // STRIP - 1
    every = pl.ds(0, tile_rows)
    mine = pl.ds(RADIUS, rows)
    step = INNER_ROWS
    tiles = []
    for strip in range(strips):
        queries = middle(qkv, 0, mine, strip)
        keys, values, flags = (window(ref, plane, every, strip) for ref, plane in ((qkv, 1), (qkv, 2), (keep, 0)))
        for start in range(0, rows, step):
            span = slice(start * 2 * STRIP, (start + step + 2 * RADIUS) * 2 * STRIP)
            tiles.append(
                (
                    queries[start * STRIP : (start + step) * STRIP],
                    keys[span],
                    values[span],
                    strip_bias(step, flags[span]),
                )
            )
    mixed = batched(tiles, INNER_BATCH * rows // step)
    heads[...] = jnp.concatenate(mixed, axis=0).astype(jnp.bfloat16)
    for copy in copies:
        copy.wait()
    source = jnp.concatenate([middle(resid, 0, mine, strip) for strip in range(strips)], axis=0)
    out[...] = finish(heads[...], source, w_out[...], modulation[...]).reshape(out.shape)


def rim_kernel(odd, qkv, keep, first, second, resid, w_out, modulation, out, halo, heads, arrived):
    tile_rows, tile_cols, width = resid.shape[1:]
    strips = tile_cols // STRIP - 1
    near = 2 * RADIUS
    above = jnp.where(odd[0] == 1, 0, 1)
    copies = [
        pltpu.make_async_copy(first, halo.at[pl.ds(above, 1)], arrived.at[0]),
        pltpu.make_async_copy(second, halo.at[pl.ds(1 - above, 1)], arrived.at[1]),
    ]
    for copy in copies:
        copy.start()
    cases = [(strip, side) for strip in range(strips) for side in range(2)]
    locals_ = []
    for strip, side in cases:
        inner = pl.ds(0 if side == 0 else tile_rows - near, near)
        locals_.append([window(ref, plane, inner, strip) for ref, plane in ((qkv, 1), (qkv, 2), (keep, 0))])
    for copy in copies:
        copy.wait()
    tiles = []
    sources = []
    for (strip, side), parts in zip(cases, locals_):
        mine = pl.ds(0 if side == 0 else tile_rows - RADIUS, RADIUS)
        far = window(halo, side, pl.ds(0, RADIUS), strip)
        joined = []
        for at, local in zip((0, width, 2 * width), parts):
            piece = far[:, at : at + local.shape[1]]
            joined.append(jnp.concatenate([piece, local] if side == 0 else [local, piece], axis=0))
        bias = strip_bias(RADIUS, joined[2])
        tiles.append((middle(qkv, 0, mine, strip), joined[0], joined[1], bias))
        sources.append(middle(resid, 0, mine, strip))
    heads[...] = jnp.concatenate(batched(tiles, RIM_BATCH), axis=0).astype(jnp.bfloat16)
    out[...] = finish(heads[...], jnp.concatenate(sources, axis=0), w_out[...], modulation[...]).reshape(out.shape)


def load_kernel(odd, qkv_hbm, keep_hbm, one, two, qkv, keep, flags, arrived):
    tile_rows, tile_cols, width = qkv.shape[1:]
    last = tile_rows - RADIUS
    starts = (jnp.where(odd[0] == 1, 0, last), jnp.where(odd[0] == 1, last, 0))
    copies = [pltpu.make_async_copy(keep_hbm, flags, arrived.at[0])]
    for out, start in zip((one, two), starts):
        for plane in (1, 2):
            copies.append(
                pltpu.make_async_copy(
                    qkv_hbm.at[plane, pl.ds(start, RADIUS)],
                    out.at[0, :, :, pl.ds((plane - 1) * width, width)],
                    arrived.at[len(copies)],
                )
            )
    copies.append(pltpu.make_async_copy(qkv_hbm, qkv, arrived.at[len(copies)]))
    for copy in copies:
        copy.start()
    copies[0].wait()
    for row in range(tile_rows):
        spread = jnp.broadcast_to(flags[row].astype(jnp.float32), (LANES, tile_cols))
        keep[0, row] = spread.T.astype(jnp.bfloat16)
    for out, start in zip((one, two), starts):
        out[0, :, :, 2 * width :] = keep[0, pl.ds(start, RADIUS)]
    for copy in copies[1:]:
        copy.wait()


def columns_kernel(odd, qkv, keep, halo, one, two):
    tile_rows, tile_cols, width = qkv.shape[1:]
    even = odd[1] == 0
    body = slice(RADIUS, RADIUS + tile_rows)
    for ref, plane, rows, lane, lanes in (
        (qkv, 1, body, 0, width),
        (qkv, 2, body, width, width),
        (keep, 0, body, 2 * width, LANES),
        (halo, 0, slice(0, RADIUS), 0, 2 * width + LANES),
        (halo, 1, slice(RADIUS + tile_rows, 2 * RADIUS + tile_rows), 0, 2 * width + LANES),
    ):
        head = ref[plane, :, 0:STRIP, :].astype(jnp.float32)[:, :RADIUS]
        tail = ref[plane, :, tile_cols - STRIP : tile_cols, :].astype(jnp.float32)[:, STRIP - RADIUS :]
        one[0, rows, :, lane : lane + lanes] = jnp.where(even, tail, head).astype(jnp.bfloat16)
        two[0, rows, :, lane : lane + lanes] = jnp.where(even, head, tail).astype(jnp.bfloat16)


def edge_columns(ref, plane, row):
    found = ref[plane, row].astype(jnp.float32)
    return found[:STRIP], found[found.shape[0] - STRIP :]


def edge_kernel(odd, qkv, keep, halo, side_one, side_two, resid, w_out, modulation, out, heads, far, ends, mine):
    tile_rows, tile_cols, width = resid.shape[1:]
    pad_rows = tile_rows + 2 * RADIUS
    far[...] = jnp.zeros_like(far)
    for row in range(pad_rows):
        local = row - RADIUS
        if 0 <= local < tile_rows:
            sources = ((qkv, 1, local, 0, width), (qkv, 2, local, width, width), (keep, 0, local, 2 * width, LANES))
        elif local < 0:
            sources = ((halo, 0, row, 0, 2 * width + LANES),)
        else:
            sources = ((halo, 1, local - tile_rows, 0, 2 * width + LANES),)
        for ref, plane, at, lane, lanes in sources:
            head, tail = edge_columns(ref, plane, at)
            far[row, 0:STRIP, lane : lane + lanes] = head
            far[row, STRIP : 2 * STRIP, lane : lane + lanes] = tail
        far[row, 2 * STRIP : 2 * STRIP + RADIUS, :] = side_one[0, row].astype(jnp.float32)
        far[row, 2 * STRIP + RADIUS : 2 * STRIP + 2 * RADIUS, :] = side_two[0, row].astype(jnp.float32)
    one_left = odd[1] == 1
    one_col = jnp.where(one_left, -RADIUS, tile_cols)
    two_col = jnp.where(one_left, tile_cols, -RADIUS)
    for row in range(tile_rows):
        for ref, plane, target in ((qkv, 0, ends), (resid, 0, mine)):
            head, tail = edge_columns(ref, plane, row)
            target[row, 0:EDGE] = head[:EDGE]
            target[row, EDGE:STRIP] = tail[EDGE:]
    rows = 4
    span = 3 * STRIP
    tiles = []
    for start in range(0, tile_rows, rows):
        count, keys = rows * STRIP, (rows + 2 * RADIUS) * span
        found = far[start : start + rows + 2 * RADIUS].reshape(keys, 2 * width + LANES).astype(jnp.bfloat16)
        q, k = iota((count, keys), 0), iota((count, keys), 1)
        q_col = q % STRIP
        q_col = jnp.where(q_col < EDGE, q_col, q_col + tile_cols - STRIP)
        k_col = k % span
        k_col = jnp.where(
            k_col < STRIP,
            k_col,
            jnp.where(
                k_col < 2 * STRIP,
                k_col + tile_cols - 2 * STRIP,
                jnp.where(
                    k_col < 2 * STRIP + RADIUS,
                    k_col - 2 * STRIP + one_col,
                    jnp.where(
                        k_col < 2 * STRIP + 2 * RADIUS,
                        k_col - 2 * STRIP - RADIUS + two_col,
                        -100 * tile_cols,
                    ),
                ),
            ),
        )
        bias = make_bias(
            q // STRIP + RADIUS, q_col, k // span, k_col, keep_row(count, found[:, 2 * width :])
        )
        tiles.append(
            (ends[start : start + rows].reshape(count, width), found[:, :width], found[:, width : 2 * width], bias)
        )
    mixed = batched(tiles, EDGE_BATCH)
    source = mine[...].reshape(tile_rows * STRIP, width)
    heads[...] = jnp.concatenate(mixed, axis=0).astype(jnp.bfloat16)
    out[...] = finish(heads[...], source, w_out[...], modulation[...])


def project(normed, w_qkv, plane):
    width = normed.shape[1]
    return jnp.dot(normed, w_qkv[:, plane * width : (plane + 1) * width], preferred_element_type=jnp.float32)


def own_kernel(*refs):
    half = (len(refs) - 1) // 2
    w_qkv = refs[half]
    width = w_qkv.shape[0]
    normed = jnp.concatenate([ref[...] for ref in refs[:half]], axis=0)
    for plane in range(3):
        found = project(normed, w_qkv, plane).astype(jnp.bfloat16)
        start = 0
        for ref in refs[half + 1 :]:
            count = ref.shape[0]
            ref[:, plane * width : (plane + 1) * width] = found[start : start + count]
            start += count


def head_marks(width):
    feature, lane = np.arange(width)[:, None], np.arange(LANES)[None, :]
    return jnp.asarray(feature // (width // HEADS) == lane % HEADS, jnp.bfloat16)


def mark_heads(width):
    row, feature = np.arange(LANES)[:, None], np.arange(width)[None, :]
    return jnp.asarray((feature // (width // HEADS) == row % HEADS) & (row < 2 * HEADS), jnp.bfloat16)


def halves_of(values):
    high = values.astype(jnp.bfloat16)
    low = (values - high.astype(jnp.float32)).astype(jnp.bfloat16)
    return high, low


def temporal(own, other_key, other_value, marks, spread):
    width = other_key.shape[1]
    scale = (width // HEADS) ** (-0.5)
    lane = iota((1, LANES), 1)
    key_gap = other_key.astype(jnp.float32) - own[:, width : 2 * width].astype(jnp.float32)
    high, low = halves_of(own[:, :width].astype(jnp.float32) * key_gap)
    gap = (
        jnp.dot(high, marks, preferred_element_type=jnp.float32)
        + jnp.dot(low, marks, preferred_element_type=jnp.float32)
    ) * scale
    own_weight = jnp.exp(jnp.minimum(-gap, 0.0))
    other_weight = jnp.exp(jnp.minimum(gap, 0.0))
    inverse = 1.0 / (own_weight + other_weight)

    def share(weight):
        part = weight.astype(jnp.bfloat16).astype(jnp.float32) * inverse
        high, low = halves_of(part)
        packed = jnp.where(lane < HEADS, high.astype(jnp.float32), low.astype(jnp.float32)).astype(jnp.bfloat16)
        return jnp.dot(packed, spread, preferred_element_type=jnp.float32)

    return share(own_weight) * own[:, 2 * width :].astype(jnp.float32) + share(other_weight) * other_value.astype(
        jnp.float32
    )


def middle_kernel(inner_own, rim_own, inner_other, rim_other, edge, w_qkv, marks, spread, inner, rim, edge_own):
    width = edge.shape[1]
    first, second = inner.shape[0], inner.shape[0] + rim.shape[0]
    stacked = jnp.concatenate([inner_other[...], rim_other[...], edge[...]], axis=0)
    edge_own[:, :width] = project(edge[...], w_qkv, 0).astype(jnp.bfloat16)
    keys = project(stacked, w_qkv, 1).astype(jnp.bfloat16)
    values = project(stacked, w_qkv, 2).astype(jnp.bfloat16)
    edge_own[:, width : 2 * width] = keys[second:]
    edge_own[:, 2 * width :] = values[second:]
    for own, out, rows in ((inner_own, inner, slice(0, first)), (rim_own, rim, slice(first, second))):
        out[...] = temporal(own[...], keys[rows], values[rows], marks[...], spread[...]).astype(jnp.bfloat16)


def last_kernel(own, other, w_qkv, marks, spread, inner, rim, out, mixed_ref):
    tile_rows, tile_cols, width = out.shape[1:]
    strips = tile_cols // STRIP - 1
    for row in range(tile_rows):
        if row < RADIUS:
            source, at = rim, row
        elif row < tile_rows - RADIUS:
            source, at = inner, row - RADIUS
        else:
            source, at = rim, row - tile_rows + 2 * RADIUS
        rows = tile_rows - 2 * RADIUS if source is inner else 2 * RADIUS
        for strip in range(strips):
            start = (strip * rows + at) * STRIP
            piece = source[start : start + STRIP, :].astype(jnp.float32)
            mixed_ref[row, EDGE + STRIP * strip : EDGE + STRIP * strip + STRIP] = piece
    keys = project(other[...], w_qkv, 1).astype(jnp.bfloat16)
    values = project(other[...], w_qkv, 2).astype(jnp.bfloat16)
    edge = temporal(own[...], keys, values, marks[...], spread[...])
    for row in range(tile_rows):
        mixed_ref[row, 0:EDGE] = edge[STRIP * row : STRIP * row + EDGE]
        mixed_ref[row, tile_cols - EDGE :] = edge[STRIP * row + EDGE : STRIP * row + STRIP]
    out[0] = mixed_ref[...].astype(jnp.bfloat16)


def call(body, out_shape, operands, scratch=(), flops=0, limit=24, specs=()):
    size = sum(math.prod(x.shape) * x.dtype.itemsize for x in operands)
    in_specs = [VMEM] * len(operands)
    for index, spec in specs:
        in_specs[index] = spec
    return pl.pallas_call(
        body,
        out_shape=out_shape,
        in_specs=in_specs,
        out_specs=[VMEM] * len(out_shape) if isinstance(out_shape, list) else VMEM,
        scratch_shapes=list(scratch),
        cost_estimate=pl.CostEstimate(flops=flops, bytes_accessed=size, transcendentals=0),
        compiler_params=pltpu.CompilerParams(vmem_limit_bytes=limit * MIB),
        name=body.__name__,
    )(*operands)


def exchanges(count):
    found = []
    for start in (0, 1):
        pairs = [(i, i + 1) for i in range(start, count - 1, 2)]
        found.append(pairs + [(j, i) for i, j in pairs])
    return found


def fast_device(resid, spatial_qkv, key_keep, w_spatial_out, modulation, w_temporal_qkv):
    frame_count, tile_rows, tile_cols, width = resid.shape
    strips = tile_cols // STRIP - 1
    odd = jnp.stack([lax.axis_index("row") % 2, lax.axis_index("col") % 2]).astype(jnp.int32)
    swap = [(0, 1), (1, 0)]
    bf16 = jnp.bfloat16
    struct = lambda *shape: jax.ShapeDtypeStruct(shape, bf16)
    held = lambda *shape: pltpu.VMEM(shape, bf16)
    stay = lambda x: pltpu.with_memory_space_constraint(x, pltpu.HBM)
    smem = pl.BlockSpec(memory_space=pltpu.SMEM)
    hbm = pl.BlockSpec(memory_space=pltpu.HBM)
    marks, spread = head_marks(width), mark_heads(width)
    lanes = 2 * width + LANES
    pad_rows = tile_rows + 2 * RADIUS
    edge_count = tile_rows * STRIP

    one, two, qkv, keep = call(
        load_kernel,
        [struct(1, RADIUS, tile_cols, lanes)] * 2
        + [held(3, tile_rows, tile_cols, width), held(1, tile_rows, tile_cols, LANES)],
        (odd, stay(spatial_qkv[:, 0]), stay(key_keep.reshape(tile_rows, 1, tile_cols))),
        [pltpu.VMEM((tile_rows, 1, tile_cols), jnp.int32), pltpu.SemaphoreType.DMA((6,))],
        specs=[(0, smem), (1, hbm), (2, hbm)],
    )
    pairs_one, pairs_two = exchanges(lax.axis_size("row"))
    first = lax.ppermute(one, "row", pairs_one)
    second = lax.ppermute(two, "row", pairs_two)

    inner_count = strips * (tile_rows - 2 * RADIUS) * STRIP
    inner, resid, w_spatial_out = call(
        inner_kernel,
        [struct(inner_count, width), held(*resid.shape), held(width, width)],
        (qkv, keep, stay(resid), stay(w_spatial_out), modulation),
        [held(inner_count, width), pltpu.SemaphoreType.DMA((2,))],
        flops=10**9,
        specs=[(2, hbm), (3, hbm)],
    )
    inner_other = lax.ppermute(inner, "tm", swap)

    rim_count = strips * 2 * RADIUS * STRIP
    rim, halo = call(
        rim_kernel,
        [struct(rim_count, width), held(2, RADIUS, tile_cols, lanes)],
        (odd, qkv, keep, first, second, resid, w_spatial_out, modulation),
        [held(rim_count, width), pltpu.SemaphoreType.DMA((2,))],
        flops=10**9,
        specs=[(0, smem)],
    )
    rim_other = lax.ppermute(rim, "tm", swap)

    one, two = call(
        columns_kernel, [struct(1, pad_rows, RADIUS, lanes)] * 2, (odd, qkv, keep, halo), specs=[(0, smem)]
    )
    pairs_one, pairs_two = exchanges(lax.axis_size("col"))
    side_one = lax.ppermute(one, "col", pairs_one)
    side_two = lax.ppermute(two, "col", pairs_two)

    inner_own, rim_own = call(
        own_kernel,
        [struct(inner_count, 3 * width), struct(rim_count, 3 * width)],
        (inner, rim, w_temporal_qkv),
        flops=(inner_count + rim_count) * width * width * 6,
    )

    edge = call(
        edge_kernel,
        struct(edge_count, width),
        (odd, qkv, keep, halo, side_one, side_two, resid, w_spatial_out, modulation),
        [
            held(edge_count, width),
            pltpu.VMEM((pad_rows, 3 * STRIP, lanes), jnp.float32),
            pltpu.VMEM((tile_rows, STRIP, width), jnp.float32),
            pltpu.VMEM((tile_rows, STRIP, width), jnp.float32),
        ],
        flops=10**9,
        specs=[(0, smem)],
    )
    edge_other = lax.ppermute(edge, "tm", swap)

    inner_done, rim_done, edge_own = call(
        middle_kernel,
        [struct(inner_count, width), struct(rim_count, width), struct(edge_count, 3 * width)],
        (inner_own, rim_own, inner_other, rim_other, edge, w_temporal_qkv, marks, spread),
        flops=(inner_count + rim_count + edge_count) * width * width * 4,
    )
    return call(
        last_kernel,
        jax.ShapeDtypeStruct((frame_count, tile_rows, tile_cols, width), bf16),
        (edge_own, edge_other, w_temporal_qkv, marks, spread, inner_done, rim_done),
        [pltpu.VMEM((tile_rows, tile_cols, width), jnp.float32)],
        flops=edge_count * width * width * 4,
    )


def per_device(resid, *rest):
    frame_count, tile_rows, tile_cols, width = resid.shape
    fits = (
        frame_count == 1
        and lax.axis_size("tm") == 2
        and width == 9 * LANES
        and tile_cols % STRIP == 0
        and tile_cols >= 2 * STRIP
        and tile_rows % 4 == 0
        and tile_rows > 2 * RADIUS
    )
    return (fast_device if fits else general_device)(resid, *rest)


def solution(mesh):
    return jax.shard_map(
        per_device,
        mesh=mesh,
        in_specs=(
            P("tm", "row", "col", None),
            P(None, "tm", "row", "col", None),
            P("tm", "row", "col"),
            P(),
            P(),
            P(),
        ),
        out_specs=P("tm", "row", "col", None),
        check_vma=False,
    )
```

```python
import functools
import math

import jax
import jax.numpy as jnp
import numpy as np
from jax import lax
from jax.experimental import pallas as pl
from jax.experimental.pallas import tpu as pltpu
from jax.sharding import PartitionSpec as P

HEADS = 16
RADIUS = 3


NEG_FILL = -1e30
EPSILON = 1e-06

LANES = 128
STRIP = 8
EDGE = STRIP // 2
MIB = 1024 * 1024
VMEM = pl.BlockSpec(memory_space=pltpu.VMEM)


def extended(array, sides, width):
    for axis, dim in sides:
        count, length = (lax.axis_size(axis), array.shape[dim])
        up = [(i, (i + 1) % count) for i in range(count - 1)]
        down = [(j, i) for i, j in up]
        last = lax.slice_in_dim(array, length - width, length, axis=dim)
        leading = lax.slice_in_dim(array, 0, width, axis=dim)
        before = lax.ppermute(last, axis, up)
        after = lax.ppermute(leading, axis, down)
        array = jnp.concatenate([before, array, after], axis=dim)
    return array


def softmax_parts(scores, allowed):
    masked = jnp.where(allowed, scores, NEG_FILL)
    top_score = jnp.max(masked, -1, keepdims=True)
    weights_f = jnp.where(allowed, jnp.exp(masked - top_score), 0.0)
    return (weights_f.astype(jnp.bfloat16), jnp.sum(weights_f, -1))


def frame_attend(gathered, head_count):
    frames_all, single, items, width_three = gathered.shape
    width = width_three // 3
    head_size = width // head_count
    split_qkv = gathered.reshape(frames_all, items, 3, head_count, head_size)
    scores = jnp.einsum(
        "fphd,gphd->phfg",
        split_qkv[:, :, 0],
        split_qkv[:, :, 1],
        preferred_element_type=jnp.float32,
    ) * head_size ** (-0.5)
    weights_b, totals = softmax_parts(scores, True)
    weighted = jnp.einsum(
        "phfg,gphd->fphd", weights_b, split_qkv[:, :, 2], preferred_element_type=jnp.float32
    )
    result = weighted / jnp.transpose(totals, (2, 0, 1))[..., None]
    return result.astype(jnp.bfloat16).reshape(frames_all, single, items, width)


def general_device(resid, spatial_qkv, key_keep, w_spatial_out, modulation, w_temporal_qkv):
    frame_count, tile_rows, tile_cols, width = resid.shape
    head_size = width // HEADS
    score_scale = head_size ** (-0.5)
    tile_tokens = tile_rows * tile_cols
    pair = spatial_qkv[1:3]
    keep_flags = key_keep.astype(jnp.bfloat16)[None, :, :, :, None]
    padded_pair, padded_keep = (
        extended(pair, (("row", 2), ("col", 3)), RADIUS),
        extended(keep_flags, (("row", 2), ("col", 3)), RADIUS),
    )
    pad_rows = tile_rows + 2 * RADIUS
    pad_cols = tile_cols + 2 * RADIUS
    key_count = pad_rows * pad_cols
    queries = spatial_qkv[0].reshape(frame_count, tile_tokens, HEADS, head_size)
    keys_pad = padded_pair[0].reshape(frame_count, key_count, HEADS, head_size)
    values_pad = padded_pair[1].reshape(frame_count, key_count, HEADS, head_size)
    query_index = jnp.arange(tile_tokens)
    query_row = query_index // tile_cols
    query_col = query_index % tile_cols
    key_index = jnp.arange(key_count)
    key_row = key_index // pad_cols
    key_col = key_index % pad_cols
    row_gap = key_row[None, :] - query_row[:, None] - RADIUS
    col_gap = key_col[None, :] - query_col[:, None] - RADIUS
    in_window = (jnp.abs(row_gap) <= RADIUS) & (jnp.abs(col_gap) <= RADIUS)
    itself = (row_gap == 0) & (col_gap == 0)
    key_live = padded_keep.reshape(frame_count, key_count) > 0.5
    allowed = (in_window[None] & (key_live[:, None, :] | itself[None]))[:, None]
    scores = (
        jnp.einsum("fqhd,fkhd->fhqk", queries, keys_pad, preferred_element_type=jnp.float32)
        * score_scale
    )
    weights_b, totals = softmax_parts(scores, allowed)
    weighted = jnp.einsum(
        "fhqk,fkhd->fqhd", weights_b, values_pad, preferred_element_type=jnp.float32
    )
    spatial_heads = (weighted / jnp.transpose(totals, (0, 2, 1))[..., None]).astype(jnp.bfloat16)
    spatial_heads = spatial_heads.reshape(frame_count * tile_tokens, width)
    stream = resid.reshape(frame_count * tile_tokens, width).astype(jnp.float32) + jnp.dot(
        spatial_heads, w_spatial_out, preferred_element_type=jnp.float32
    )
    average = jnp.mean(stream, -1, keepdims=True)
    centered = stream - average
    variance = jnp.mean(centered * centered, -1, keepdims=True)
    normed = (
        centered * lax.rsqrt(variance + EPSILON) * (1.0 + modulation[1]) + modulation[0]
    ).astype(jnp.bfloat16)
    tm_count = lax.axis_size("tm")
    part_tokens = tile_tokens // tm_count
    normed_parts = normed.reshape(frame_count, tm_count, part_tokens, width)
    gathered = lax.all_to_all(normed_parts, "tm", split_axis=1, concat_axis=0, tiled=True)
    frames_all, single, items, unused = gathered.shape
    projected = jnp.dot(
        gathered.reshape(frames_all * single * items, width),
        w_temporal_qkv,
        preferred_element_type=jnp.float32,
    ).astype(jnp.bfloat16)
    projected = projected.reshape(frames_all, single, items, 3 * width)
    result = lax.all_to_all(
        frame_attend(projected, HEADS), "tm", split_axis=0, concat_axis=1, tiled=True
    )
    return result.reshape(frame_count, tile_rows, tile_cols, width)


def iota(shape, dim):
    return lax.broadcasted_iota(jnp.int32, shape, dim)


def attend(tiles):
    width = tiles[0][0].shape[1]
    head = width // HEADS
    factor = head ** (-0.5) * math.log2(math.e)
    lane = iota((1, 2 * LANES), 1)
    spans = []
    for pair in range(HEADS // 2):
        start = LANES * pair
        low = 2 * head * pair - start
        spans.append((slice(start, start + 2 * LANES), low, low + head, low + 2 * head))
    scores = []
    for queries, keys, values, bias in tiles:
        for span, low, mid, high in spans:
            first = jnp.where((lane >= low) & (lane < mid), queries[:, span], 0.0)
            second = jnp.where((lane >= mid) & (lane < high), queries[:, span], 0.0)
            both = jnp.concatenate([first, second], axis=0).astype(jnp.bfloat16)
            scores.append(
                lax.dot_general(
                    both, keys[:, span], (((1,), (1,)), ((), ())), preferred_element_type=jnp.float32
                )
            )
    weights = []
    for index, (queries, keys, values, bias) in enumerate(tiles):
        bias_two = jnp.concatenate([bias, bias], axis=0)
        for pair in range(len(spans)):
            score = scores[index * len(spans) + pair] + bias_two
            top = jnp.max(score, -1, keepdims=True)
            weight = jnp.exp2((score - top) * factor)
            weights.append((weight.astype(jnp.bfloat16), 1.0 / jnp.sum(weight, -1, keepdims=True)))
    results = []
    edge_lane = iota((1, LANES), 1)
    for index, (queries, keys, values, bias) in enumerate(tiles):
        count = queries.shape[0]
        pairs = []
        for pair, (span, low, mid, high) in enumerate(spans):
            weight, inverse = weights[index * len(spans) + pair]
            mixed = jnp.dot(weight, values[:, span], preferred_element_type=jnp.float32) * inverse
            pairs.append(jnp.where(lane < mid, mixed[:count], mixed[count:]))
        blocks = [pairs[0][:, :LANES]]
        for pair in range(1, len(spans)):
            cut = spans[pair][1]
            blocks.append(jnp.where(edge_lane < cut, pairs[pair - 1][:, LANES:], pairs[pair][:, :LANES]))
        blocks.append(pairs[-1][:, LANES:])
        results.append(jnp.concatenate(blocks, axis=1))
    return results


def keep_row(count, keep):
    picker = jnp.where(iota((count, LANES), 1) == 0, 1.0, 0.0).astype(jnp.bfloat16)
    return lax.dot_general(
        picker, keep, (((1,), (1,)), ((), ())), preferred_element_type=jnp.float32
    )


def make_bias(q_row, q_col, k_row, k_col, keep):
    row_gap, col_gap = k_row - q_row, k_col - q_col
    near = (jnp.abs(row_gap) <= RADIUS) & (jnp.abs(col_gap) <= RADIUS)
    itself = (row_gap == 0) & (col_gap == 0)
    return jnp.where(near & ((keep > 0.5) | itself), 0.0, NEG_FILL)


def strip_bias(rows, keep, strips=1):
    columns, key_columns = strips * STRIP, (strips + 1) * STRIP
    count, keys = rows * columns, (rows + 2 * RADIUS) * key_columns
    q, k = iota((count, keys), 0), iota((count, keys), 1)
    return make_bias(
        q // columns + RADIUS, q % columns + EDGE, k // key_columns, k % key_columns, keep_row(count, keep)
    )


def finish(heads, resid, w_out, modulation):
    stream = resid + jnp.dot(heads, w_out, preferred_element_type=jnp.float32)
    average = jnp.mean(stream, -1, keepdims=True)
    centered = stream - average
    variance = jnp.mean(centered * centered, -1, keepdims=True)
    scaled = centered * lax.rsqrt(variance + EPSILON)
    return (scaled * (1.0 + modulation[1:2]) + modulation[0:1]).astype(jnp.bfloat16)


def wide(ref, plane, rows, strip, strips=1):
    found = ref[plane, rows, pl.ds(STRIP * strip, (strips + 1) * STRIP), :].astype(jnp.float32)
    return found.reshape(found.shape[0] * found.shape[1], found.shape[2])


def window(ref, plane, rows, strip):
    return wide(ref, plane, rows, strip).astype(jnp.bfloat16)


def middle(ref, plane, rows, strip, strips=1):
    found = ref[plane, rows, pl.ds(STRIP * strip, (strips + 1) * STRIP), :].astype(jnp.float32)
    found = found[:, EDGE : EDGE + strips * STRIP]
    return found.reshape(found.shape[0] * found.shape[1], found.shape[2])


INNER_ROWS = 6
INNER_BATCH = 4
RIM_BATCH = 4
RIM_STRIPS = 2
EDGE_BATCH = 3


def batched(tiles, size):
    found = []
    for start in range(0, len(tiles), size):
        found += attend(tiles[start : start + size])
    return found


def inner_kernel(qkv, keep, resid_hbm, w_hbm, modulation, out, resid, w_out, heads, arrived):
    copies = [
        pltpu.make_async_copy(resid_hbm, resid, arrived.at[0]),
        pltpu.make_async_copy(w_hbm, w_out, arrived.at[1]),
    ]
    for copy in copies:
        copy.start()
    tile_rows, tile_cols, width = resid.shape[1:]
    rows = tile_rows - 2 * RADIUS
    strips = tile_cols // STRIP - 1
    every = pl.ds(0, tile_rows)
    mine = pl.ds(RADIUS, rows)
    step = INNER_ROWS
    tiles = []
    for strip in range(strips):
        queries = middle(qkv, 0, mine, strip)
        keys, values, flags = (window(ref, plane, every, strip) for ref, plane in ((qkv, 1), (qkv, 2), (keep, 0)))
        for start in range(0, rows, step):
            span = slice(start * 2 * STRIP, (start + step + 2 * RADIUS) * 2 * STRIP)
            tiles.append(
                (
                    queries[start * STRIP : (start + step) * STRIP],
                    keys[span],
                    values[span],
                    strip_bias(step, flags[span]),
                )
            )
    mixed = batched(tiles, INNER_BATCH * rows // step)
    heads[...] = jnp.concatenate(mixed, axis=0).astype(jnp.bfloat16)
    for copy in copies:
        copy.wait()
    source = jnp.concatenate([middle(resid, 0, mine, strip) for strip in range(strips)], axis=0)
    out[...] = finish(heads[...], source, w_out[...], modulation[...]).reshape(out.shape)


def rim_kernel(qkv, keep, halo, resid, w_out, modulation, out, heads):
    tile_rows, tile_cols, width = resid.shape[1:]
    strips = tile_cols // STRIP - 1
    near = 2 * RADIUS
    tiles = []
    sources = []
    for strip in range(0, strips, RIM_STRIPS):
        for side in range(2):
            inner = pl.ds(0 if side == 0 else tile_rows - near, near)
            mine = pl.ds(0 if side == 0 else tile_rows - RADIUS, RADIUS)
            far = wide(halo, side, pl.ds(0, RADIUS), strip, RIM_STRIPS)
            joined = []
            for at, (ref, plane) in zip((0, width, 2 * width), ((qkv, 1), (qkv, 2), (keep, 0))):
                local = wide(ref, plane, inner, strip, RIM_STRIPS)
                piece = far[:, at : at + local.shape[1]]
                both = jnp.concatenate([piece, local] if side == 0 else [local, piece], axis=0)
                joined.append(both.astype(jnp.bfloat16))
            bias = strip_bias(RADIUS, joined[2], RIM_STRIPS)
            tiles.append((middle(qkv, 0, mine, strip, RIM_STRIPS), joined[0], joined[1], bias))
            sources.append(middle(resid, 0, mine, strip, RIM_STRIPS))
    heads[...] = jnp.concatenate(batched(tiles, RIM_BATCH), axis=0).astype(jnp.bfloat16)
    out[...] = finish(heads[...], jnp.concatenate(sources, axis=0), w_out[...], modulation[...]).reshape(out.shape)


def load_kernel(odd, qkv_hbm, keep_hbm, one, two, qkv, keep, flags, packed, arrived):
    tile_rows, tile_cols, width = qkv.shape[1:]
    last = tile_rows - RADIUS
    starts = (jnp.where(odd[0] == 1, 0, last), jnp.where(odd[0] == 1, last, 0))
    copies = [pltpu.make_async_copy(keep_hbm, flags, arrived.at[0])]
    for out, start in zip((two, one), starts[::-1]):
        for plane in (1, 2):
            copies.append(
                pltpu.make_async_copy(
                    qkv_hbm.at[plane, pl.ds(start, RADIUS)],
                    out.at[0, :, :, pl.ds((plane - 1) * width, width)],
                    arrived.at[len(copies)],
                )
            )
    copies.append(pltpu.make_async_copy(qkv_hbm, qkv, arrived.at[len(copies)]))
    for copy in copies:
        copy.start()
    copies[0].wait()
    packed[...] = jnp.zeros_like(packed)
    for row in range(tile_rows):
        packed[row : row + 1, :tile_cols] = flags[row].astype(jnp.float32)
    turned = packed[...].T
    for row in range(tile_rows):
        column = jnp.broadcast_to(turned[:tile_cols, row : row + 1], (tile_cols, LANES))
        keep[0, row] = column.astype(jnp.bfloat16)
    for out, start in zip((one, two), starts):
        out[0, :, :, 2 * width :] = keep[0, pl.ds(start, RADIUS)]
    for copy in copies[1:]:
        copy.wait()


def columns_kernel(odd, qkv, keep, first, second, after, one, two, halo, arrived):
    above = jnp.where(odd[0] == 1, 0, 1)
    copies = [
        pltpu.make_async_copy(first, halo.at[pl.ds(above, 1)], arrived.at[0]),
        pltpu.make_async_copy(second, halo.at[pl.ds(1 - above, 1)], arrived.at[1]),
    ]
    for copy in copies:
        copy.start()
    tile_rows, tile_cols, width = qkv.shape[1:]
    even = odd[1] == 0
    body = slice(RADIUS, RADIUS + tile_rows)
    for ref, plane, rows, lane, lanes in (
        (qkv, 1, body, 0, width),
        (qkv, 2, body, width, width),
        (keep, 0, body, 2 * width, LANES),
        (halo, 0, slice(0, RADIUS), 0, 2 * width + LANES),
        (halo, 1, slice(RADIUS + tile_rows, 2 * RADIUS + tile_rows), 0, 2 * width + LANES),
    ):
        if ref is halo and plane == 0:
            for copy in copies:
                copy.wait()
        head = ref[plane, :, 0:STRIP, :].astype(jnp.float32)[:, :RADIUS]
        tail = ref[plane, :, tile_cols - STRIP : tile_cols, :].astype(jnp.float32)[:, STRIP - RADIUS :]
        one[0, rows, :, lane : lane + lanes] = jnp.where(even, tail, head).astype(jnp.bfloat16)
        two[0, rows, :, lane : lane + lanes] = jnp.where(even, head, tail).astype(jnp.bfloat16)


def edge_columns(ref, plane, row):
    found = ref[plane, row].astype(jnp.float32)
    return found[:STRIP], found[found.shape[0] - STRIP :]


def edge_kernel(odd, qkv, keep, halo, side_one, side_two, resid, w_out, modulation, after, out, heads, far, ends, mine):
    tile_rows, tile_cols, width = resid.shape[1:]
    pad_rows = tile_rows + 2 * RADIUS
    far[:, 2 * STRIP :, :] = jnp.zeros((pad_rows, STRIP, far.shape[2]), jnp.float32)
    for row in range(pad_rows):
        local = row - RADIUS
        if 0 <= local < tile_rows:
            sources = ((qkv, 1, local, 0, width), (qkv, 2, local, width, width), (keep, 0, local, 2 * width, LANES))
        elif local < 0:
            sources = ((halo, 0, row, 0, 2 * width + LANES),)
        else:
            sources = ((halo, 1, local - tile_rows, 0, 2 * width + LANES),)
        for ref, plane, at, lane, lanes in sources:
            head, tail = edge_columns(ref, plane, at)
            far[row, 0:STRIP, lane : lane + lanes] = head
            far[row, STRIP : 2 * STRIP, lane : lane + lanes] = tail
        far[row, 2 * STRIP : 2 * STRIP + RADIUS, :] = side_one[0, row].astype(jnp.float32)
        far[row, 2 * STRIP + RADIUS : 2 * STRIP + 2 * RADIUS, :] = side_two[0, row].astype(jnp.float32)
    one_left = odd[1] == 1
    one_col = jnp.where(one_left, -RADIUS, tile_cols)
    two_col = jnp.where(one_left, tile_cols, -RADIUS)
    for row in range(tile_rows):
        for ref, plane, target in ((qkv, 0, ends), (resid, 0, mine)):
            head, tail = edge_columns(ref, plane, row)
            target[row, 0:EDGE] = head[:EDGE]
            target[row, EDGE:STRIP] = tail[EDGE:]
    rows = 4
    span = 3 * STRIP
    tiles = []
    for start in range(0, tile_rows, rows):
        count, keys = rows * STRIP, (rows + 2 * RADIUS) * span
        found = far[start : start + rows + 2 * RADIUS].reshape(keys, 2 * width + LANES).astype(jnp.bfloat16)
        q, k = iota((count, keys), 0), iota((count, keys), 1)
        q_col = q % STRIP
        q_col = jnp.where(q_col < EDGE, q_col, q_col + tile_cols - STRIP)
        k_col = k % span
        k_col = jnp.where(
            k_col < STRIP,
            k_col,
            jnp.where(
                k_col < 2 * STRIP,
                k_col + tile_cols - 2 * STRIP,
                jnp.where(
                    k_col < 2 * STRIP + RADIUS,
                    k_col - 2 * STRIP + one_col,
                    jnp.where(
                        k_col < 2 * STRIP + 2 * RADIUS,
                        k_col - 2 * STRIP - RADIUS + two_col,
                        -100 * tile_cols,
                    ),
                ),
            ),
        )
        bias = make_bias(
            q // STRIP + RADIUS, q_col, k // span, k_col, keep_row(count, found[:, 2 * width :])
        )
        tiles.append(
            (ends[start : start + rows].reshape(count, width), found[:, :width], found[:, width : 2 * width], bias)
        )
    mixed = batched(tiles, EDGE_BATCH)
    source = mine[...].reshape(tile_rows * STRIP, width)
    heads[...] = jnp.concatenate(mixed, axis=0).astype(jnp.bfloat16)
    out[...] = finish(heads[...], source, w_out[...], modulation[...])


def project(normed, w_qkv, plane):
    width = normed.shape[1]
    return jnp.dot(normed, w_qkv[:, plane * width : (plane + 1) * width], preferred_element_type=jnp.float32)


def own_kernel(normed, w_qkv, out):
    out[...] = jnp.dot(normed[...], w_qkv[...], preferred_element_type=jnp.float32).astype(jnp.bfloat16)


def head_marks(width):
    feature, lane = np.arange(width)[:, None], np.arange(LANES)[None, :]
    return jnp.asarray(feature // (width // HEADS) == lane % HEADS, jnp.bfloat16)


def mark_heads(width):
    row, feature = np.arange(LANES)[:, None], np.arange(width)[None, :]
    return jnp.asarray((feature // (width // HEADS) == row % HEADS) & (row < 2 * HEADS), jnp.bfloat16)


def halves_of(values):
    high = values.astype(jnp.bfloat16)
    low = (values - high.astype(jnp.float32)).astype(jnp.bfloat16)
    return high, low


def temporal(own, other_key, other_value, marks, spread):
    width = other_key.shape[1]
    scale = (width // HEADS) ** (-0.5)
    lane = iota((1, LANES), 1)
    key_gap = other_key.astype(jnp.float32) - own[:, width : 2 * width].astype(jnp.float32)
    high, low = halves_of(own[:, :width].astype(jnp.float32) * key_gap)
    gap = (
        jnp.dot(high, marks, preferred_element_type=jnp.float32)
        + jnp.dot(low, marks, preferred_element_type=jnp.float32)
    ) * scale
    own_weight = jnp.exp(jnp.minimum(-gap, 0.0))
    other_weight = jnp.exp(jnp.minimum(gap, 0.0))
    inverse = 1.0 / (own_weight + other_weight)

    def share(weight):
        part = weight.astype(jnp.bfloat16).astype(jnp.float32) * inverse
        high, low = halves_of(part)
        packed = jnp.where(lane < HEADS, high.astype(jnp.float32), low.astype(jnp.float32)).astype(jnp.bfloat16)
        return jnp.dot(packed, spread, preferred_element_type=jnp.float32)

    return share(own_weight) * own[:, 2 * width :].astype(jnp.float32) + share(other_weight) * other_value.astype(
        jnp.float32
    )


def middle_kernel(own, other, fresh, w_qkv, marks, spread, out, fresh_own):
    count, width = other.shape
    stacked = jnp.concatenate([other[...], fresh[...]], axis=0)
    fresh_own[:, :width] = project(fresh[...], w_qkv, 0).astype(jnp.bfloat16)
    keys = project(stacked, w_qkv, 1).astype(jnp.bfloat16)
    values = project(stacked, w_qkv, 2).astype(jnp.bfloat16)
    fresh_own[:, width : 2 * width] = keys[count:]
    fresh_own[:, 2 * width :] = values[count:]
    out[...] = temporal(own[...], keys[:count], values[:count], marks[...], spread[...]).astype(jnp.bfloat16)


def joining_kernel(own, other, fresh, inner, w_qkv, marks, spread, out, ends, fresh_own, rim, mixed):
    tile_rows, tile_cols, width = out.shape[1:]
    strips = tile_cols // STRIP - 1
    middle_kernel(own, other, fresh, w_qkv, marks, spread, rim, fresh_own)
    for row in range(tile_rows):
        if RADIUS <= row < tile_rows - RADIUS:
            for strip in range(strips):
                start = (strip * (tile_rows - 2 * RADIUS) + row - RADIUS) * STRIP
                piece = inner[start : start + STRIP, :].astype(jnp.float32)
                mixed[row, EDGE + STRIP * strip : EDGE + STRIP * strip + STRIP] = piece
            continue
        at = row if row < RADIUS else row - tile_rows + 2 * RADIUS
        columns = RIM_STRIPS * STRIP
        for part in range(0, strips, RIM_STRIPS):
            start = part // RIM_STRIPS * 2 * RADIUS * columns + at * columns
            piece = rim[start : start + columns, :].astype(jnp.float32)
            mixed[row, EDGE + STRIP * part : EDGE + STRIP * part + columns] = piece
    mixed[:, 0:EDGE] = jnp.zeros((tile_rows, EDGE, width), jnp.float32)
    mixed[:, tile_cols - EDGE :] = jnp.zeros((tile_rows, EDGE, width), jnp.float32)
    out[0] = mixed[...].astype(jnp.bfloat16)
    ends[:, 0:STRIP] = mixed[:, 0:STRIP]
    ends[:, STRIP:] = mixed[:, tile_cols - STRIP :]


def last_kernel(own, other, w_qkv, marks, spread, ready, ends, out, mixed, left, right, arrived):
    tile_rows, tile_cols, width = ready.shape[1:]
    whole = pltpu.make_async_copy(ready, out, arrived.at[0])
    whole.start()
    keys = project(other[...], w_qkv, 1).astype(jnp.bfloat16)
    values = project(other[...], w_qkv, 2).astype(jnp.bfloat16)
    edge = temporal(own[...], keys, values, marks[...], spread[...])
    edge = edge.reshape(tile_rows, STRIP, width)
    mixed[:, 0:STRIP] = ends[:, 0:STRIP]
    mixed[:, STRIP:] = ends[:, STRIP:]
    mixed[:, 0:EDGE] = edge[:, :EDGE]
    mixed[:, STRIP + EDGE :] = edge[:, EDGE:]
    left[...] = mixed[:, :STRIP].astype(jnp.bfloat16)
    right[...] = mixed[:, STRIP:].astype(jnp.bfloat16)
    whole.wait()
    copies = [
        pltpu.make_async_copy(left, out.at[0, :, pl.ds(0, STRIP)], arrived.at[1]),
        pltpu.make_async_copy(right, out.at[0, :, pl.ds(tile_cols - STRIP, STRIP)], arrived.at[2]),
    ]
    for copy in copies:
        copy.start()
    for copy in copies:
        copy.wait()


def call(body, out_shape, operands, scratch=(), flops=0, limit=24, specs=(), out_spec=VMEM):
    in_specs = [VMEM] * len(operands)
    for index, spec in specs:
        in_specs[index] = spec
    return pl.pallas_call(
        body,
        out_shape=out_shape,
        in_specs=in_specs,
        out_specs=[VMEM] * len(out_shape) if isinstance(out_shape, list) else out_spec,
        scratch_shapes=list(scratch),
        cost_estimate=pl.CostEstimate(flops=flops, bytes_accessed=0, transcendentals=0),
        compiler_params=pltpu.CompilerParams(vmem_limit_bytes=limit * MIB),
        name=body.__name__,
    )(*operands)


def exchanges(count):
    found = []
    for start in (0, 1):
        pairs = [(i, i + 1) for i in range(start, count - 1, 2)]
        found.append(pairs + [(j, i) for i, j in pairs])
    return found


def fast_device(resid, spatial_qkv, key_keep, w_spatial_out, modulation, w_temporal_qkv):
    frame_count, tile_rows, tile_cols, width = resid.shape
    strips = tile_cols // STRIP - 1
    odd = jnp.stack([lax.axis_index("row") % 2, lax.axis_index("col") % 2]).astype(jnp.int32)
    swap = [(0, 1), (1, 0)]
    bf16 = jnp.bfloat16
    struct = lambda *shape: jax.ShapeDtypeStruct(shape, bf16)
    held = lambda *shape: pltpu.VMEM(shape, bf16)
    stay = lambda x: pltpu.with_memory_space_constraint(x, pltpu.HBM)
    smem = pl.BlockSpec(memory_space=pltpu.SMEM)
    hbm = pl.BlockSpec(memory_space=pltpu.HBM)
    anywhere = pl.BlockSpec(memory_space=pl.ANY)
    marks, spread = head_marks(width), mark_heads(width)
    lanes = 2 * width + LANES
    pad_rows = tile_rows + 2 * RADIUS
    edge_count = tile_rows * STRIP

    one, two, qkv, keep = call(
        load_kernel,
        [struct(1, RADIUS, tile_cols, lanes)] * 2
        + [held(3, tile_rows, tile_cols, width), held(1, tile_rows, tile_cols, LANES)],
        (odd, stay(spatial_qkv[:, 0]), stay(key_keep.reshape(tile_rows, 1, tile_cols))),
        [
            pltpu.VMEM((tile_rows, 1, tile_cols), jnp.int32),
            pltpu.VMEM((LANES, LANES), jnp.float32),
            pltpu.SemaphoreType.DMA((6,)),
        ],
        specs=[(0, smem), (1, hbm), (2, hbm)],
    )
    pairs_one, pairs_two = exchanges(lax.axis_size("row"))
    first = lax.ppermute(one, "row", pairs_one)
    second = lax.ppermute(two, "row", pairs_two)

    inner_count = strips * (tile_rows - 2 * RADIUS) * STRIP
    inner, resid, w_spatial_out = call(
        inner_kernel,
        [struct(inner_count, width), held(*resid.shape), held(width, width)],
        (qkv, keep, stay(resid), stay(w_spatial_out), modulation),
        [held(inner_count, width), pltpu.SemaphoreType.DMA((2,))],
        specs=[(2, hbm), (3, hbm)],
    )
    inner_other = lax.ppermute(inner, "tm", swap)
    inner_own = call(own_kernel, struct(inner_count, 3 * width), (inner, w_temporal_qkv))

    one, two, halo = call(
        columns_kernel,
        [struct(1, pad_rows, RADIUS, lanes)] * 2 + [held(2, RADIUS, tile_cols, lanes)],
        (odd, qkv, keep, first, second, inner_own),
        [pltpu.SemaphoreType.DMA((2,))],
        specs=[(0, smem), (5, anywhere)],
    )
    pairs_one, pairs_two = exchanges(lax.axis_size("col"))
    side_one = lax.ppermute(one, "col", pairs_one)
    side_two = lax.ppermute(two, "col", pairs_two)

    rim_count = strips * 2 * RADIUS * STRIP
    rim = call(
        rim_kernel,
        struct(rim_count, width),
        (qkv, keep, halo, resid, w_spatial_out, modulation),
        [held(rim_count, width)],
    )
    rim_other = lax.ppermute(rim, "tm", swap)

    inner_done, rim_own = call(
        middle_kernel,
        [struct(inner_count, width), struct(rim_count, 3 * width)],
        (inner_own, inner_other, rim, w_temporal_qkv, marks, spread),
    )

    edge = call(
        edge_kernel,
        struct(edge_count, width),
        (odd, qkv, keep, halo, side_one, side_two, resid, w_spatial_out, modulation, inner_done),
        [
            held(edge_count, width),
            pltpu.VMEM((pad_rows, 3 * STRIP, lanes), jnp.float32),
            pltpu.VMEM((tile_rows, STRIP, width), jnp.float32),
            pltpu.VMEM((tile_rows, STRIP, width), jnp.float32),
        ],
        specs=[(0, smem), (9, anywhere)],
    )
    edge_other = lax.ppermute(edge, "tm", swap)

    out = (frame_count, tile_rows, tile_cols, width)
    ready, ends, edge_own = call(
        joining_kernel,
        [struct(*out), pltpu.VMEM((tile_rows, 2 * STRIP, width), jnp.float32), struct(edge_count, 3 * width)],
        (rim_own, rim_other, edge, inner_done, w_temporal_qkv, marks, spread),
        [held(rim_count, width), pltpu.VMEM((tile_rows, tile_cols, width), jnp.float32)],
    )
    return call(
        last_kernel,
        struct(*out),
        (edge_own, edge_other, w_temporal_qkv, marks, spread, ready, ends),
        [
            pltpu.VMEM((tile_rows, 2 * STRIP, width), jnp.float32),
            held(tile_rows, STRIP, width),
            held(tile_rows, STRIP, width),
            pltpu.SemaphoreType.DMA((3,)),
        ],
        out_spec=hbm,
    )


def per_device(resid, *rest):
    frame_count, tile_rows, tile_cols, width = resid.shape
    fits = (
        frame_count == 1
        and lax.axis_size("tm") == 2
        and width == 9 * LANES
        and (tile_cols // STRIP - 1) % RIM_STRIPS == 0
        and tile_cols % STRIP == 0
        and tile_cols >= 2 * STRIP
        and tile_rows % 4 == 0
        and tile_rows > 2 * RADIUS
    )
    return (fast_device if fits else general_device)(resid, *rest)


def solution(mesh):
    return jax.shard_map(
        per_device,
        mesh=mesh,
        in_specs=(
            P("tm", "row", "col", None),
            P(None, "tm", "row", "col", None),
            P("tm", "row", "col"),
            P(),
            P(),
            P(),
        ),
        out_specs=P("tm", "row", "col", None),
        check_vma=False,
    )
```

```python
import functools
import math

import jax
import jax.numpy as jnp
import numpy as np
from jax import lax
from jax.experimental import pallas as pl
from jax.experimental.pallas import tpu as pltpu
from jax.sharding import PartitionSpec as P

HEADS = 16
RADIUS = 3


NEG_FILL = -1e30
EPSILON = 1e-06

LANES = 128
STRIP = 8
EDGE = STRIP // 2
MIB = 1024 * 1024
VMEM = pl.BlockSpec(memory_space=pltpu.VMEM)


def extended(array, sides, width):
    for axis, dim in sides:
        count, length = (lax.axis_size(axis), array.shape[dim])
        up = [(i, (i + 1) % count) for i in range(count - 1)]
        down = [(j, i) for i, j in up]
        last = lax.slice_in_dim(array, length - width, length, axis=dim)
        leading = lax.slice_in_dim(array, 0, width, axis=dim)
        before = lax.ppermute(last, axis, up)
        after = lax.ppermute(leading, axis, down)
        array = jnp.concatenate([before, array, after], axis=dim)
    return array


def softmax_parts(scores, allowed):
    masked = jnp.where(allowed, scores, NEG_FILL)
    top_score = jnp.max(masked, -1, keepdims=True)
    weights_f = jnp.where(allowed, jnp.exp(masked - top_score), 0.0)
    return (weights_f.astype(jnp.bfloat16), jnp.sum(weights_f, -1))


def frame_attend(gathered, head_count):
    frames_all, single, items, width_three = gathered.shape
    width = width_three // 3
    head_size = width // head_count
    split_qkv = gathered.reshape(frames_all, items, 3, head_count, head_size)
    scores = jnp.einsum(
        "fphd,gphd->phfg",
        split_qkv[:, :, 0],
        split_qkv[:, :, 1],
        preferred_element_type=jnp.float32,
    ) * head_size ** (-0.5)
    weights_b, totals = softmax_parts(scores, True)
    weighted = jnp.einsum(
        "phfg,gphd->fphd", weights_b, split_qkv[:, :, 2], preferred_element_type=jnp.float32
    )
    result = weighted / jnp.transpose(totals, (2, 0, 1))[..., None]
    return result.astype(jnp.bfloat16).reshape(frames_all, single, items, width)


def general_device(resid, spatial_qkv, key_keep, w_spatial_out, modulation, w_temporal_qkv):
    frame_count, tile_rows, tile_cols, width = resid.shape
    head_size = width // HEADS
    score_scale = head_size ** (-0.5)
    tile_tokens = tile_rows * tile_cols
    pair = spatial_qkv[1:3]
    keep_flags = key_keep.astype(jnp.bfloat16)[None, :, :, :, None]
    padded_pair, padded_keep = (
        extended(pair, (("row", 2), ("col", 3)), RADIUS),
        extended(keep_flags, (("row", 2), ("col", 3)), RADIUS),
    )
    pad_rows = tile_rows + 2 * RADIUS
    pad_cols = tile_cols + 2 * RADIUS
    key_count = pad_rows * pad_cols
    queries = spatial_qkv[0].reshape(frame_count, tile_tokens, HEADS, head_size)
    keys_pad = padded_pair[0].reshape(frame_count, key_count, HEADS, head_size)
    values_pad = padded_pair[1].reshape(frame_count, key_count, HEADS, head_size)
    query_index = jnp.arange(tile_tokens)
    query_row = query_index // tile_cols
    query_col = query_index % tile_cols
    key_index = jnp.arange(key_count)
    key_row = key_index // pad_cols
    key_col = key_index % pad_cols
    row_gap = key_row[None, :] - query_row[:, None] - RADIUS
    col_gap = key_col[None, :] - query_col[:, None] - RADIUS
    in_window = (jnp.abs(row_gap) <= RADIUS) & (jnp.abs(col_gap) <= RADIUS)
    itself = (row_gap == 0) & (col_gap == 0)
    key_live = padded_keep.reshape(frame_count, key_count) > 0.5
    allowed = (in_window[None] & (key_live[:, None, :] | itself[None]))[:, None]
    scores = (
        jnp.einsum("fqhd,fkhd->fhqk", queries, keys_pad, preferred_element_type=jnp.float32)
        * score_scale
    )
    weights_b, totals = softmax_parts(scores, allowed)
    weighted = jnp.einsum(
        "fhqk,fkhd->fqhd", weights_b, values_pad, preferred_element_type=jnp.float32
    )
    spatial_heads = (weighted / jnp.transpose(totals, (0, 2, 1))[..., None]).astype(jnp.bfloat16)
    spatial_heads = spatial_heads.reshape(frame_count * tile_tokens, width)
    stream = resid.reshape(frame_count * tile_tokens, width).astype(jnp.float32) + jnp.dot(
        spatial_heads, w_spatial_out, preferred_element_type=jnp.float32
    )
    average = jnp.mean(stream, -1, keepdims=True)
    centered = stream - average
    variance = jnp.mean(centered * centered, -1, keepdims=True)
    normed = (
        centered * lax.rsqrt(variance + EPSILON) * (1.0 + modulation[1]) + modulation[0]
    ).astype(jnp.bfloat16)
    tm_count = lax.axis_size("tm")
    part_tokens = tile_tokens // tm_count
    normed_parts = normed.reshape(frame_count, tm_count, part_tokens, width)
    gathered = lax.all_to_all(normed_parts, "tm", split_axis=1, concat_axis=0, tiled=True)
    frames_all, single, items, unused = gathered.shape
    projected = jnp.dot(
        gathered.reshape(frames_all * single * items, width),
        w_temporal_qkv,
        preferred_element_type=jnp.float32,
    ).astype(jnp.bfloat16)
    projected = projected.reshape(frames_all, single, items, 3 * width)
    result = lax.all_to_all(
        frame_attend(projected, HEADS), "tm", split_axis=0, concat_axis=1, tiled=True
    )
    return result.reshape(frame_count, tile_rows, tile_cols, width)


def iota(shape, dim):
    return lax.broadcasted_iota(jnp.int32, shape, dim)


def attend(tiles):
    width = tiles[0][0].shape[1]
    head = width // HEADS
    factor = head ** (-0.5) * math.log2(math.e)
    lane = iota((1, 2 * LANES), 1)
    spans = []
    for pair in range(HEADS // 2):
        start = LANES * pair
        low = 2 * head * pair - start
        spans.append((slice(start, start + 2 * LANES), low, low + head, low + 2 * head))
    scores = []
    for queries, keys, values, bias in tiles:
        for span, low, mid, high in spans:
            first = jnp.where((lane >= low) & (lane < mid), queries[:, span], 0.0)
            second = jnp.where((lane >= mid) & (lane < high), queries[:, span], 0.0)
            both = jnp.concatenate([first, second], axis=0).astype(jnp.bfloat16)
            scores.append(
                lax.dot_general(
                    both, keys[:, span], (((1,), (1,)), ((), ())), preferred_element_type=jnp.float32
                )
            )
    weights = []
    for index, (queries, keys, values, bias) in enumerate(tiles):
        bias_two = jnp.concatenate([bias, bias], axis=0)
        for pair in range(len(spans)):
            score = scores[index * len(spans) + pair] + bias_two
            top = jnp.max(score, -1, keepdims=True)
            weight = jnp.exp2((score - top) * factor)
            weights.append((weight.astype(jnp.bfloat16), 1.0 / jnp.sum(weight, -1, keepdims=True)))
    results = []
    edge_lane = iota((1, LANES), 1)
    for index, (queries, keys, values, bias) in enumerate(tiles):
        count = queries.shape[0]
        pairs = []
        for pair, (span, low, mid, high) in enumerate(spans):
            weight, inverse = weights[index * len(spans) + pair]
            mixed = jnp.dot(weight, values[:, span], preferred_element_type=jnp.float32) * inverse
            pairs.append(jnp.where(lane < mid, mixed[:count], mixed[count:]))
        blocks = [pairs[0][:, :LANES]]
        for pair in range(1, len(spans)):
            cut = spans[pair][1]
            blocks.append(jnp.where(edge_lane < cut, pairs[pair - 1][:, LANES:], pairs[pair][:, :LANES]))
        blocks.append(pairs[-1][:, LANES:])
        results.append(jnp.concatenate(blocks, axis=1))
    return results


def keep_row(count, keep):
    picker = jnp.where(iota((count, LANES), 1) == 0, 1.0, 0.0).astype(jnp.bfloat16)
    return lax.dot_general(
        picker, keep, (((1,), (1,)), ((), ())), preferred_element_type=jnp.float32
    )


def make_bias(q_row, q_col, k_row, k_col, keep):
    row_gap, col_gap = k_row - q_row, k_col - q_col
    near = (jnp.abs(row_gap) <= RADIUS) & (jnp.abs(col_gap) <= RADIUS)
    itself = (row_gap == 0) & (col_gap == 0)
    return jnp.where(near & ((keep > 0.5) | itself), 0.0, NEG_FILL)


def strip_bias(rows, keep, strips=1):
    columns, key_columns = strips * STRIP, (strips + 1) * STRIP
    count, keys = rows * columns, (rows + 2 * RADIUS) * key_columns
    q, k = iota((count, keys), 0), iota((count, keys), 1)
    return make_bias(
        q // columns + RADIUS, q % columns + EDGE, k // key_columns, k % key_columns, keep_row(count, keep)
    )


def finish(heads, resid, w_out, modulation):
    stream = resid + jnp.dot(heads, w_out, preferred_element_type=jnp.float32)
    average = jnp.mean(stream, -1, keepdims=True)
    centered = stream - average
    variance = jnp.mean(centered * centered, -1, keepdims=True)
    scaled = centered * lax.rsqrt(variance + EPSILON)
    return (scaled * (1.0 + modulation[1:2]) + modulation[0:1]).astype(jnp.bfloat16)


def wide(ref, plane, rows, strip, strips=1):
    found = ref[plane, rows, pl.ds(STRIP * strip, (strips + 1) * STRIP), :].astype(jnp.float32)
    return found.reshape(found.shape[0] * found.shape[1], found.shape[2])


def window(ref, plane, rows, strip):
    return wide(ref, plane, rows, strip).astype(jnp.bfloat16)


def middle(ref, plane, rows, strip, strips=1):
    found = ref[plane, rows, pl.ds(STRIP * strip, (strips + 1) * STRIP), :].astype(jnp.float32)
    found = found[:, EDGE : EDGE + strips * STRIP]
    return found.reshape(found.shape[0] * found.shape[1], found.shape[2])


INNER_ROWS = 6
INNER_BATCH = 4
RIM_BATCH = 4
RIM_STRIPS = 2
EDGE_BATCH = 3


def batched(tiles, size):
    found = []
    for start in range(0, len(tiles), size):
        found += attend(tiles[start : start + size])
    return found


def inner_kernel(qkv, keep, resid_hbm, w_hbm, modulation, out, resid, w_out, heads, arrived):
    copies = [
        pltpu.make_async_copy(resid_hbm, resid, arrived.at[0]),
        pltpu.make_async_copy(w_hbm, w_out, arrived.at[1]),
    ]
    for copy in copies:
        copy.start()
    tile_rows, tile_cols, width = resid.shape[1:]
    rows = tile_rows - 2 * RADIUS
    strips = tile_cols // STRIP - 1
    every = pl.ds(0, tile_rows)
    mine = pl.ds(RADIUS, rows)
    step = INNER_ROWS
    tiles = []
    for strip in range(strips):
        queries = middle(qkv, 0, mine, strip)
        keys, values, flags = (window(ref, plane, every, strip) for ref, plane in ((qkv, 1), (qkv, 2), (keep, 0)))
        for start in range(0, rows, step):
            span = slice(start * 2 * STRIP, (start + step + 2 * RADIUS) * 2 * STRIP)
            tiles.append(
                (
                    queries[start * STRIP : (start + step) * STRIP],
                    keys[span],
                    values[span],
                    strip_bias(step, flags[span]),
                )
            )
    mixed = batched(tiles, INNER_BATCH * rows // step)
    heads[...] = jnp.concatenate(mixed, axis=0).astype(jnp.bfloat16)
    for copy in copies:
        copy.wait()
    source = jnp.concatenate([middle(resid, 0, mine, strip) for strip in range(strips)], axis=0)
    out[...] = finish(heads[...], source, w_out[...], modulation[...]).reshape(out.shape)


def rim_kernel(qkv, keep, halo, resid, w_out, modulation, out, heads):
    tile_rows, tile_cols, width = resid.shape[1:]
    strips = tile_cols // STRIP - 1
    near = 2 * RADIUS
    tiles = []
    sources = []
    for strip in range(0, strips, RIM_STRIPS):
        for side in range(2):
            inner = pl.ds(0 if side == 0 else tile_rows - near, near)
            mine = pl.ds(0 if side == 0 else tile_rows - RADIUS, RADIUS)
            far = wide(halo, side, pl.ds(0, RADIUS), strip, RIM_STRIPS)
            joined = []
            for at, (ref, plane) in zip((0, width, 2 * width), ((qkv, 1), (qkv, 2), (keep, 0))):
                local = wide(ref, plane, inner, strip, RIM_STRIPS)
                piece = far[:, at : at + local.shape[1]]
                both = jnp.concatenate([piece, local] if side == 0 else [local, piece], axis=0)
                joined.append(both.astype(jnp.bfloat16))
            bias = strip_bias(RADIUS, joined[2], RIM_STRIPS)
            tiles.append((middle(qkv, 0, mine, strip, RIM_STRIPS), joined[0], joined[1], bias))
            sources.append(middle(resid, 0, mine, strip, RIM_STRIPS))
    heads[...] = jnp.concatenate(batched(tiles, RIM_BATCH), axis=0).astype(jnp.bfloat16)
    out[...] = finish(heads[...], jnp.concatenate(sources, axis=0), w_out[...], modulation[...]).reshape(out.shape)


def load_kernel(odd, qkv_hbm, keep_hbm, one, two, qkv, keep, flags, packed, arrived):
    tile_rows, tile_cols, width = qkv.shape[1:]
    last = tile_rows - RADIUS
    starts = (jnp.where(odd[0] == 1, 0, last), jnp.where(odd[0] == 1, last, 0))
    copies = [pltpu.make_async_copy(keep_hbm, flags, arrived.at[0])]
    for out, start in zip((two, one), starts[::-1]):
        for plane in (1, 2):
            copies.append(
                pltpu.make_async_copy(
                    qkv_hbm.at[plane, pl.ds(start, RADIUS)],
                    out.at[0, :, :, pl.ds((plane - 1) * width, width)],
                    arrived.at[len(copies)],
                )
            )
    copies.append(pltpu.make_async_copy(qkv_hbm, qkv, arrived.at[len(copies)]))
    for copy in copies:
        copy.start()
    copies[0].wait()
    packed[...] = jnp.zeros_like(packed)
    for row in range(tile_rows):
        packed[row : row + 1, :tile_cols] = flags[row].astype(jnp.float32)
    turned = packed[...].T
    for row in range(tile_rows):
        column = jnp.broadcast_to(turned[:tile_cols, row : row + 1], (tile_cols, LANES))
        keep[0, row] = column.astype(jnp.bfloat16)
    for out, start in zip((one, two), starts):
        out[0, :, :, 2 * width :] = keep[0, pl.ds(start, RADIUS)]
    for copy in copies[1:]:
        copy.wait()


def pack_columns(odd, sources, one, two):
    even = odd[1] == 0
    for ref, plane, rows, lane in sources:
        tile_cols, lanes = ref.shape[-2:]
        head = ref[plane, :, 0:STRIP, :].astype(jnp.float32)[:, :RADIUS]
        tail = ref[plane, :, tile_cols - STRIP : tile_cols, :].astype(jnp.float32)[:, STRIP - RADIUS :]
        one[rows, :, lane : lane + lanes] = jnp.where(even, tail, head).astype(jnp.bfloat16)
        two[rows, :, lane : lane + lanes] = jnp.where(even, head, tail).astype(jnp.bfloat16)


def own_kernel(odd, normed, w_qkv, qkv, keep, out, one, two):
    tile_rows, tile_cols, width = qkv.shape[1:]
    rows = slice(0, tile_rows)
    pack_columns(odd, ((qkv, 1, rows, 0), (qkv, 2, rows, width), (keep, 0, rows, 2 * width)), one, two)
    out[...] = jnp.dot(normed[...], w_qkv[...], preferred_element_type=jnp.float32).astype(jnp.bfloat16)


def columns_kernel(odd, first, second, one_body, two_body, one, two, halo):
    tile_rows = one_body.shape[0]
    for above in (0, 1):

        @pl.when(odd[0] == 1 - above)
        def _():
            halo[above : above + 1] = first[...]
            halo[1 - above : 2 - above] = second[...]

    body = slice(RADIUS, RADIUS + tile_rows)
    one[0, body] = one_body[...]
    two[0, body] = two_body[...]
    top, bottom = slice(0, RADIUS), slice(RADIUS + tile_rows, 2 * RADIUS + tile_rows)
    pack_columns(odd, ((halo, 0, top, 0), (halo, 1, bottom, 0)), one.at[0], two.at[0])


def edge_columns(ref, plane, row):
    found = ref[plane, row].astype(jnp.float32)
    return found[:STRIP], found[found.shape[0] - STRIP :]


def edge_kernel(odd, qkv, keep, halo, side_one, side_two, resid, w_out, modulation, after, out, heads, far, ends, mine):
    tile_rows, tile_cols, width = resid.shape[1:]
    pad_rows = tile_rows + 2 * RADIUS
    far[:, 2 * STRIP :, :] = jnp.zeros((pad_rows, STRIP, far.shape[2]), jnp.float32)
    for row in range(pad_rows):
        local = row - RADIUS
        if 0 <= local < tile_rows:
            sources = ((qkv, 1, local, 0, width), (qkv, 2, local, width, width), (keep, 0, local, 2 * width, LANES))
        elif local < 0:
            sources = ((halo, 0, row, 0, 2 * width + LANES),)
        else:
            sources = ((halo, 1, local - tile_rows, 0, 2 * width + LANES),)
        for ref, plane, at, lane, lanes in sources:
            head, tail = edge_columns(ref, plane, at)
            far[row, 0:STRIP, lane : lane + lanes] = head
            far[row, STRIP : 2 * STRIP, lane : lane + lanes] = tail
        far[row, 2 * STRIP : 2 * STRIP + RADIUS, :] = side_one[0, row].astype(jnp.float32)
        far[row, 2 * STRIP + RADIUS : 2 * STRIP + 2 * RADIUS, :] = side_two[0, row].astype(jnp.float32)
    one_left = odd[1] == 1
    one_col = jnp.where(one_left, -RADIUS, tile_cols)
    two_col = jnp.where(one_left, tile_cols, -RADIUS)
    for row in range(tile_rows):
        for ref, plane, target in ((qkv, 0, ends), (resid, 0, mine)):
            head, tail = edge_columns(ref, plane, row)
            target[row, 0:EDGE] = head[:EDGE]
            target[row, EDGE:STRIP] = tail[EDGE:]
    rows = 4
    span = 3 * STRIP
    tiles = []
    for start in range(0, tile_rows, rows):
        count, keys = rows * STRIP, (rows + 2 * RADIUS) * span
        found = far[start : start + rows + 2 * RADIUS].reshape(keys, 2 * width + LANES).astype(jnp.bfloat16)
        q, k = iota((count, keys), 0), iota((count, keys), 1)
        q_col = q % STRIP
        q_col = jnp.where(q_col < EDGE, q_col, q_col + tile_cols - STRIP)
        k_col = k % span
        k_col = jnp.where(
            k_col < STRIP,
            k_col,
            jnp.where(
                k_col < 2 * STRIP,
                k_col + tile_cols - 2 * STRIP,
                jnp.where(
                    k_col < 2 * STRIP + RADIUS,
                    k_col - 2 * STRIP + one_col,
                    jnp.where(
                        k_col < 2 * STRIP + 2 * RADIUS,
                        k_col - 2 * STRIP - RADIUS + two_col,
                        -100 * tile_cols,
                    ),
                ),
            ),
        )
        bias = make_bias(
            q // STRIP + RADIUS, q_col, k // span, k_col, keep_row(count, found[:, 2 * width :])
        )
        tiles.append(
            (ends[start : start + rows].reshape(count, width), found[:, :width], found[:, width : 2 * width], bias)
        )
    mixed = batched(tiles, EDGE_BATCH)
    source = mine[...].reshape(tile_rows * STRIP, width)
    heads[...] = jnp.concatenate(mixed, axis=0).astype(jnp.bfloat16)
    out[...] = finish(heads[...], source, w_out[...], modulation[...])


def head_marks(width):
    feature, lane = np.arange(width)[:, None], np.arange(LANES)[None, :]
    return jnp.asarray(feature // (width // HEADS) == lane % HEADS, jnp.bfloat16)


def mark_heads(width):
    row, feature = np.arange(LANES)[:, None], np.arange(width)[None, :]
    return jnp.asarray((feature // (width // HEADS) == row % HEADS) & (row < 2 * HEADS), jnp.bfloat16)


def halves_of(values):
    high = values.astype(jnp.bfloat16)
    low = (values - high.astype(jnp.float32)).astype(jnp.bfloat16)
    return high, low


def temporal(own, other_key, other_value, marks, spread):
    width = other_key.shape[1]
    scale = (width // HEADS) ** (-0.5)
    lane = iota((1, LANES), 1)
    key_gap = other_key.astype(jnp.float32) - own[:, width : 2 * width].astype(jnp.float32)
    high, low = halves_of(own[:, :width].astype(jnp.float32) * key_gap)
    gap = (
        jnp.dot(high, marks, preferred_element_type=jnp.float32)
        + jnp.dot(low, marks, preferred_element_type=jnp.float32)
    ) * scale
    own_weight = jnp.exp(jnp.minimum(-gap, 0.0))
    other_weight = jnp.exp(jnp.minimum(gap, 0.0))
    inverse = 1.0 / (own_weight + other_weight)

    def share(weight):
        part = weight.astype(jnp.bfloat16).astype(jnp.float32) * inverse
        high, low = halves_of(part)
        packed = jnp.where(lane < HEADS, high.astype(jnp.float32), low.astype(jnp.float32)).astype(jnp.bfloat16)
        return jnp.dot(packed, spread, preferred_element_type=jnp.float32)

    return share(own_weight) * own[:, 2 * width :].astype(jnp.float32) + share(other_weight) * other_value.astype(
        jnp.float32
    )


def middle_kernel(own, other, fresh, w_qkv, marks, spread, out, fresh_own):
    count, width = other.shape
    stacked = jnp.concatenate([other[...], fresh[...]], axis=0)
    query = jnp.dot(fresh[...], w_qkv[:, :width], preferred_element_type=jnp.float32)
    fresh_own[:, :width] = query.astype(jnp.bfloat16)
    pairs = jnp.dot(stacked, w_qkv[:, width:], preferred_element_type=jnp.float32).astype(jnp.bfloat16)
    fresh_own[:, width:] = pairs[count:]
    mixed = temporal(own[...], pairs[:count, :width], pairs[:count, width:], marks[...], spread[...])
    out[...] = mixed.astype(jnp.bfloat16)


def place(pieces, ready, ends, mixed):
    rows, tile_cols, width = mixed.shape
    for row, column, source, start, count in pieces:
        mixed[row, column : column + count] = source[start : start + count, :].astype(jnp.float32)
    mixed[:, 0:EDGE] = jnp.zeros((rows, EDGE, width), jnp.float32)
    mixed[:, tile_cols - EDGE :] = jnp.zeros((rows, EDGE, width), jnp.float32)
    ready[...] = mixed[...].astype(jnp.bfloat16)
    ends[:, 0:STRIP] = mixed[:, 0:STRIP]
    ends[:, STRIP:] = mixed[:, tile_cols - STRIP :]


def edge_own_kernel(edge, inner, w_qkv, out, ready, ends, mixed):
    rows, tile_cols, width = mixed.shape
    pieces = []
    for row in range(rows):
        for strip in range(tile_cols // STRIP - 1):
            pieces.append((row, EDGE + STRIP * strip, inner, (strip * rows + row) * STRIP, STRIP))
    place(pieces, ready, ends, mixed)
    out[...] = jnp.dot(edge[...], w_qkv[...], preferred_element_type=jnp.float32).astype(jnp.bfloat16)


def rim_done_kernel(own, other, w_qkv, marks, spread, ready, ends, rim, mixed):
    rows, tile_cols, width = mixed.shape
    pairs = jnp.dot(other[...], w_qkv[:, width:], preferred_element_type=jnp.float32).astype(jnp.bfloat16)
    rim[...] = temporal(own[...], pairs[:, :width], pairs[:, width:], marks[...], spread[...])
    columns = RIM_STRIPS * STRIP
    pieces = []
    for row in range(rows):
        for part in range((tile_cols // STRIP - 1) // RIM_STRIPS):
            pieces.append((row, EDGE + columns * part, rim, (part * rows + row) * columns, columns))
    place(pieces, ready, ends, mixed)


def last_kernel(own, other, w_qkv, marks, spread, inner, inner_ends, rim, rim_ends, out, mixed, left, right, arrived):
    tile_rows, tile_cols, width = out.shape[1:]
    low, high = RADIUS, tile_rows - RADIUS
    parts = (
        (slice(0, low), rim, rim_ends, slice(0, RADIUS)),
        (slice(low, high), inner, inner_ends, slice(0, high - low)),
        (slice(high, tile_rows), rim, rim_ends, slice(RADIUS, 2 * RADIUS)),
    )
    whole = []
    for target, ready, ends, rows in parts:
        size = rows.stop - rows.start
        copy = pltpu.make_async_copy(
            ready.at[pl.ds(rows.start, size), pl.ds(STRIP, tile_cols - 2 * STRIP)],
            out.at[0, pl.ds(target.start, size), pl.ds(STRIP, tile_cols - 2 * STRIP)],
            arrived.at[len(whole)],
        )
        copy.start()
        whole.append(copy)
    pairs = jnp.dot(other[...], w_qkv[:, width:], preferred_element_type=jnp.float32).astype(jnp.bfloat16)
    edge = temporal(own[...], pairs[:, :width], pairs[:, width:], marks[...], spread[...])
    edge = edge.reshape(tile_rows, STRIP, width)
    for target, ready, ends, rows in parts:
        mixed[target] = ends[rows]
    mixed[:, 0:EDGE] = edge[:, :EDGE]
    mixed[:, STRIP + EDGE :] = edge[:, EDGE:]
    left[...] = mixed[:, :STRIP].astype(jnp.bfloat16)
    right[...] = mixed[:, STRIP:].astype(jnp.bfloat16)
    copies = [
        pltpu.make_async_copy(left, out.at[0, :, pl.ds(0, STRIP)], arrived.at[3]),
        pltpu.make_async_copy(right, out.at[0, :, pl.ds(tile_cols - STRIP, STRIP)], arrived.at[4]),
    ]
    for copy in copies:
        copy.start()
    for copy in whole + copies:
        copy.wait()


def call(body, out_shape, operands, scratch=(), flops=0, limit=24, specs=(), out_spec=VMEM):
    in_specs = [VMEM] * len(operands)
    for index, spec in specs:
        in_specs[index] = spec
    return pl.pallas_call(
        body,
        out_shape=out_shape,
        in_specs=in_specs,
        out_specs=[VMEM] * len(out_shape) if isinstance(out_shape, list) else out_spec,
        scratch_shapes=list(scratch),
        cost_estimate=pl.CostEstimate(flops=flops, bytes_accessed=0, transcendentals=0),
        compiler_params=pltpu.CompilerParams(vmem_limit_bytes=limit * MIB),
        name=body.__name__,
    )(*operands)


def exchanges(count):
    found = []
    for start in (0, 1):
        pairs = [(i, i + 1) for i in range(start, count - 1, 2)]
        found.append(pairs + [(j, i) for i, j in pairs])
    return found


def fast_device(resid, spatial_qkv, key_keep, w_spatial_out, modulation, w_temporal_qkv):
    frame_count, tile_rows, tile_cols, width = resid.shape
    strips = tile_cols // STRIP - 1
    odd = jnp.stack([lax.axis_index("row") % 2, lax.axis_index("col") % 2]).astype(jnp.int32)
    swap = [(0, 1), (1, 0)]
    bf16 = jnp.bfloat16
    struct = lambda *shape: jax.ShapeDtypeStruct(shape, bf16)
    held = lambda *shape: pltpu.VMEM(shape, bf16)
    stay = lambda x: pltpu.with_memory_space_constraint(x, pltpu.HBM)
    smem = pl.BlockSpec(memory_space=pltpu.SMEM)
    hbm = pl.BlockSpec(memory_space=pltpu.HBM)
    anywhere = pl.BlockSpec(memory_space=pl.ANY)
    marks, spread = head_marks(width), mark_heads(width)
    lanes = 2 * width + LANES
    pad_rows = tile_rows + 2 * RADIUS
    edge_count = tile_rows * STRIP

    one, two, qkv, keep = call(
        load_kernel,
        [struct(1, RADIUS, tile_cols, lanes)] * 2
        + [held(3, tile_rows, tile_cols, width), held(1, tile_rows, tile_cols, LANES)],
        (odd, stay(spatial_qkv[:, 0]), stay(key_keep.reshape(tile_rows, 1, tile_cols))),
        [
            pltpu.VMEM((tile_rows, 1, tile_cols), jnp.int32),
            pltpu.VMEM((LANES, LANES), jnp.float32),
            pltpu.SemaphoreType.DMA((6,)),
        ],
        specs=[(0, smem), (1, hbm), (2, hbm)],
    )
    pairs_one, pairs_two = exchanges(lax.axis_size("row"))
    first = lax.ppermute(one, "row", pairs_one)
    second = lax.ppermute(two, "row", pairs_two)

    inner_count = strips * (tile_rows - 2 * RADIUS) * STRIP
    inner, resid, w_spatial_out = call(
        inner_kernel,
        [struct(inner_count, width), held(*resid.shape), held(width, width)],
        (qkv, keep, stay(resid), stay(w_spatial_out), modulation),
        [held(inner_count, width), pltpu.SemaphoreType.DMA((2,))],
        specs=[(2, hbm), (3, hbm)],
    )
    inner_other = lax.ppermute(inner, "tm", swap)
    inner_own, one_body, two_body = call(
        own_kernel,
        [struct(inner_count, 3 * width)] + [held(tile_rows, RADIUS, lanes)] * 2,
        (odd, inner, w_temporal_qkv, qkv, keep),
        specs=[(0, smem)],
    )

    one, two, halo = call(
        columns_kernel,
        [struct(1, pad_rows, RADIUS, lanes)] * 2 + [held(2, RADIUS, tile_cols, lanes)],
        (odd, first, second, one_body, two_body),
        specs=[(0, smem)],
    )
    pairs_one, pairs_two = exchanges(lax.axis_size("col"))
    side_one = lax.ppermute(one, "col", pairs_one)
    side_two = lax.ppermute(two, "col", pairs_two)

    rim_count = strips * 2 * RADIUS * STRIP
    rim = call(
        rim_kernel,
        struct(rim_count, width),
        (qkv, keep, halo, resid, w_spatial_out, modulation),
        [held(rim_count, width)],
    )
    rim_other = lax.ppermute(rim, "tm", swap)

    inner_done, rim_own = call(
        middle_kernel,
        [struct(inner_count, width), struct(rim_count, 3 * width)],
        (inner_own, inner_other, rim, w_temporal_qkv, marks, spread),
    )

    edge = call(
        edge_kernel,
        struct(edge_count, width),
        (odd, qkv, keep, halo, side_one, side_two, resid, w_spatial_out, modulation, inner_done),
        [
            held(edge_count, width),
            pltpu.VMEM((pad_rows, 3 * STRIP, lanes), jnp.float32),
            pltpu.VMEM((tile_rows, STRIP, width), jnp.float32),
            pltpu.VMEM((tile_rows, STRIP, width), jnp.float32),
        ],
        specs=[(0, smem), (9, anywhere)],
    )
    edge_other = lax.ppermute(edge, "tm", swap)

    def rows_of(count):
        whole, ends = (count, tile_cols, width), (count, 2 * STRIP, width)
        return [held(*whole), pltpu.VMEM(ends, jnp.float32)], pltpu.VMEM(whole, jnp.float32)

    shapes, scratch = rows_of(tile_rows - 2 * RADIUS)
    edge_own, inner_ready, inner_ends = call(
        edge_own_kernel,
        [struct(edge_count, 3 * width)] + shapes,
        (edge, inner_done, w_temporal_qkv),
        [scratch],
    )
    shapes, scratch = rows_of(2 * RADIUS)
    rim_ready, rim_ends = call(
        rim_done_kernel,
        shapes,
        (rim_own, rim_other, w_temporal_qkv, marks, spread),
        [pltpu.VMEM((rim_count, width), jnp.float32), scratch],
    )
    return call(
        last_kernel,
        struct(frame_count, tile_rows, tile_cols, width),
        (edge_own, edge_other, w_temporal_qkv, marks, spread, inner_ready, inner_ends, rim_ready, rim_ends),
        [
            pltpu.VMEM((tile_rows, 2 * STRIP, width), jnp.float32),
            held(tile_rows, STRIP, width),
            held(tile_rows, STRIP, width),
            pltpu.SemaphoreType.DMA((5,)),
        ],
        out_spec=hbm,
    )


def per_device(resid, *rest):
    frame_count, tile_rows, tile_cols, width = resid.shape
    fits = (
        frame_count == 1
        and lax.axis_size("tm") == 2
        and width == 9 * LANES
        and (tile_cols // STRIP - 1) % RIM_STRIPS == 0
        and tile_cols % STRIP == 0
        and tile_cols >= 2 * STRIP
        and tile_rows % 4 == 0
        and tile_rows > 2 * RADIUS
    )
    return (fast_device if fits else general_device)(resid, *rest)


def solution(mesh):
    return jax.shard_map(
        per_device,
        mesh=mesh,
        in_specs=(
            P("tm", "row", "col", None),
            P(None, "tm", "row", "col", None),
            P("tm", "row", "col"),
            P(),
            P(),
            P(),
        ),
        out_specs=P("tm", "row", "col", None),
        check_vma=False,
    )
```

```python
import functools
import math

import jax
import jax.numpy as jnp
import numpy as np
from jax import lax
from jax.experimental import pallas as pl
from jax.experimental.pallas import tpu as pltpu
from jax.sharding import PartitionSpec as P

HEADS = 16
RADIUS = 3


NEG_FILL = -1e30
EPSILON = 1e-06

LANES = 128
STRIP = 8
EDGE = STRIP // 2
MIB = 1024 * 1024
VMEM = pl.BlockSpec(memory_space=pltpu.VMEM)


def extended(array, sides, width):
    for axis, dim in sides:
        count, length = (lax.axis_size(axis), array.shape[dim])
        up = [(i, (i + 1) % count) for i in range(count - 1)]
        down = [(j, i) for i, j in up]
        last = lax.slice_in_dim(array, length - width, length, axis=dim)
        leading = lax.slice_in_dim(array, 0, width, axis=dim)
        before = lax.ppermute(last, axis, up)
        after = lax.ppermute(leading, axis, down)
        array = jnp.concatenate([before, array, after], axis=dim)
    return array


def softmax_parts(scores, allowed):
    masked = jnp.where(allowed, scores, NEG_FILL)
    top_score = jnp.max(masked, -1, keepdims=True)
    weights_f = jnp.where(allowed, jnp.exp(masked - top_score), 0.0)
    return (weights_f.astype(jnp.bfloat16), jnp.sum(weights_f, -1))


def frame_attend(gathered, head_count):
    frames_all, single, items, width_three = gathered.shape
    width = width_three // 3
    head_size = width // head_count
    split_qkv = gathered.reshape(frames_all, items, 3, head_count, head_size)
    scores = jnp.einsum(
        "fphd,gphd->phfg",
        split_qkv[:, :, 0],
        split_qkv[:, :, 1],
        preferred_element_type=jnp.float32,
    ) * head_size ** (-0.5)
    weights_b, totals = softmax_parts(scores, True)
    weighted = jnp.einsum(
        "phfg,gphd->fphd", weights_b, split_qkv[:, :, 2], preferred_element_type=jnp.float32
    )
    result = weighted / jnp.transpose(totals, (2, 0, 1))[..., None]
    return result.astype(jnp.bfloat16).reshape(frames_all, single, items, width)


def general_device(resid, spatial_qkv, key_keep, w_spatial_out, modulation, w_temporal_qkv):
    frame_count, tile_rows, tile_cols, width = resid.shape
    head_size = width // HEADS
    score_scale = head_size ** (-0.5)
    tile_tokens = tile_rows * tile_cols
    pair = spatial_qkv[1:3]
    keep_flags = key_keep.astype(jnp.bfloat16)[None, :, :, :, None]
    padded_pair, padded_keep = (
        extended(pair, (("row", 2), ("col", 3)), RADIUS),
        extended(keep_flags, (("row", 2), ("col", 3)), RADIUS),
    )
    pad_rows = tile_rows + 2 * RADIUS
    pad_cols = tile_cols + 2 * RADIUS
    key_count = pad_rows * pad_cols
    queries = spatial_qkv[0].reshape(frame_count, tile_tokens, HEADS, head_size)
    keys_pad = padded_pair[0].reshape(frame_count, key_count, HEADS, head_size)
    values_pad = padded_pair[1].reshape(frame_count, key_count, HEADS, head_size)
    query_index = jnp.arange(tile_tokens)
    query_row = query_index // tile_cols
    query_col = query_index % tile_cols
    key_index = jnp.arange(key_count)
    key_row = key_index // pad_cols
    key_col = key_index % pad_cols
    row_gap = key_row[None, :] - query_row[:, None] - RADIUS
    col_gap = key_col[None, :] - query_col[:, None] - RADIUS
    in_window = (jnp.abs(row_gap) <= RADIUS) & (jnp.abs(col_gap) <= RADIUS)
    itself = (row_gap == 0) & (col_gap == 0)
    key_live = padded_keep.reshape(frame_count, key_count) > 0.5
    allowed = (in_window[None] & (key_live[:, None, :] | itself[None]))[:, None]
    scores = (
        jnp.einsum("fqhd,fkhd->fhqk", queries, keys_pad, preferred_element_type=jnp.float32)
        * score_scale
    )
    weights_b, totals = softmax_parts(scores, allowed)
    weighted = jnp.einsum(
        "fhqk,fkhd->fqhd", weights_b, values_pad, preferred_element_type=jnp.float32
    )
    spatial_heads = (weighted / jnp.transpose(totals, (0, 2, 1))[..., None]).astype(jnp.bfloat16)
    spatial_heads = spatial_heads.reshape(frame_count * tile_tokens, width)
    stream = resid.reshape(frame_count * tile_tokens, width).astype(jnp.float32) + jnp.dot(
        spatial_heads, w_spatial_out, preferred_element_type=jnp.float32
    )
    average = jnp.mean(stream, -1, keepdims=True)
    centered = stream - average
    variance = jnp.mean(centered * centered, -1, keepdims=True)
    normed = (
        centered * lax.rsqrt(variance + EPSILON) * (1.0 + modulation[1]) + modulation[0]
    ).astype(jnp.bfloat16)
    tm_count = lax.axis_size("tm")
    part_tokens = tile_tokens // tm_count
    normed_parts = normed.reshape(frame_count, tm_count, part_tokens, width)
    gathered = lax.all_to_all(normed_parts, "tm", split_axis=1, concat_axis=0, tiled=True)
    frames_all, single, items, unused = gathered.shape
    projected = jnp.dot(
        gathered.reshape(frames_all * single * items, width),
        w_temporal_qkv,
        preferred_element_type=jnp.float32,
    ).astype(jnp.bfloat16)
    projected = projected.reshape(frames_all, single, items, 3 * width)
    result = lax.all_to_all(
        frame_attend(projected, HEADS), "tm", split_axis=0, concat_axis=1, tiled=True
    )
    return result.reshape(frame_count, tile_rows, tile_cols, width)


def iota(shape, dim):
    return lax.broadcasted_iota(jnp.int32, shape, dim)


def attend(tiles):
    width = tiles[0][0].shape[1]
    head = width // HEADS
    factor = head ** (-0.5) * math.log2(math.e)
    lane = iota((1, 2 * LANES), 1)
    spans = []
    for pair in range(HEADS // 2):
        start = LANES * pair
        low = 2 * head * pair - start
        spans.append((slice(start, start + 2 * LANES), low, low + head, low + 2 * head))
    scores = []
    for queries, keys, values, bias in tiles:
        for span, low, mid, high in spans:
            first = jnp.where((lane >= low) & (lane < mid), queries[:, span], 0.0)
            second = jnp.where((lane >= mid) & (lane < high), queries[:, span], 0.0)
            both = jnp.concatenate([first, second], axis=0).astype(jnp.bfloat16)
            scores.append(
                lax.dot_general(
                    both, keys[:, span], (((1,), (1,)), ((), ())), preferred_element_type=jnp.float32
                )
            )
    weights = []
    for index, (queries, keys, values, bias) in enumerate(tiles):
        bias_two = jnp.concatenate([bias, bias], axis=0)
        for pair in range(len(spans)):
            score = scores[index * len(spans) + pair] + bias_two
            top = jnp.max(score, -1, keepdims=True)
            weight = jnp.exp2((score - top) * factor)
            weights.append((weight.astype(jnp.bfloat16), 1.0 / jnp.sum(weight, -1, keepdims=True)))
    results = []
    edge_lane = iota((1, LANES), 1)
    for index, (queries, keys, values, bias) in enumerate(tiles):
        count = queries.shape[0]
        pairs = []
        for pair, (span, low, mid, high) in enumerate(spans):
            weight, inverse = weights[index * len(spans) + pair]
            mixed = jnp.dot(weight, values[:, span], preferred_element_type=jnp.float32) * inverse
            pairs.append(jnp.where(lane < mid, mixed[:count], mixed[count:]))
        blocks = [pairs[0][:, :LANES]]
        for pair in range(1, len(spans)):
            cut = spans[pair][1]
            blocks.append(jnp.where(edge_lane < cut, pairs[pair - 1][:, LANES:], pairs[pair][:, :LANES]))
        blocks.append(pairs[-1][:, LANES:])
        results.append(jnp.concatenate(blocks, axis=1))
    return results


def keep_row(count, keep):
    picker = jnp.where(iota((count, LANES), 1) == 0, 1.0, 0.0).astype(jnp.bfloat16)
    return lax.dot_general(
        picker, keep, (((1,), (1,)), ((), ())), preferred_element_type=jnp.float32
    )


def make_bias(q_row, q_col, k_row, k_col, keep):
    row_gap, col_gap = k_row - q_row, k_col - q_col
    near = (jnp.abs(row_gap) <= RADIUS) & (jnp.abs(col_gap) <= RADIUS)
    itself = (row_gap == 0) & (col_gap == 0)
    return jnp.where(near & ((keep > 0.5) | itself), 0.0, NEG_FILL)


def strip_bias(rows, keep, strips=1):
    columns, key_columns = strips * STRIP, (strips + 1) * STRIP
    count, keys = rows * columns, (rows + 2 * RADIUS) * key_columns
    q, k = iota((count, keys), 0), iota((count, keys), 1)
    return make_bias(
        q // columns + RADIUS, q % columns + EDGE, k // key_columns, k % key_columns, keep_row(count, keep)
    )


def finish(heads, resid, w_out, modulation):
    stream = resid + jnp.dot(heads, w_out, preferred_element_type=jnp.float32)
    average = jnp.mean(stream, -1, keepdims=True)
    centered = stream - average
    variance = jnp.mean(centered * centered, -1, keepdims=True)
    scaled = centered * lax.rsqrt(variance + EPSILON)
    return (scaled * (1.0 + modulation[1:2]) + modulation[0:1]).astype(jnp.bfloat16)


def wide(ref, plane, rows, strip, strips=1):
    found = ref[plane, rows, pl.ds(STRIP * strip, (strips + 1) * STRIP), :].astype(jnp.float32)
    return found.reshape(found.shape[0] * found.shape[1], found.shape[2])


def window(ref, plane, rows, strip):
    return wide(ref, plane, rows, strip).astype(jnp.bfloat16)


def middle(ref, plane, rows, strip, strips=1):
    found = ref[plane, rows, pl.ds(STRIP * strip, (strips + 1) * STRIP), :].astype(jnp.float32)
    found = found[:, EDGE : EDGE + strips * STRIP]
    return found.reshape(found.shape[0] * found.shape[1], found.shape[2])


INNER_ROWS = 6
INNER_BATCH = 4
RIM_BATCH = 4
RIM_STRIPS = 2
EDGE_BATCH = 3


def batched(tiles, size):
    found = []
    for start in range(0, len(tiles), size):
        found += attend(tiles[start : start + size])
    return found


def inner_kernel(qkv, keep, resid_hbm, w_hbm, modulation, out, resid, w_out, heads, arrived):
    copies = [
        pltpu.make_async_copy(resid_hbm, resid, arrived.at[0]),
        pltpu.make_async_copy(w_hbm, w_out, arrived.at[1]),
    ]
    for copy in copies:
        copy.start()
    tile_rows, tile_cols, width = resid.shape[1:]
    rows = tile_rows - 2 * RADIUS
    strips = tile_cols // STRIP - 1
    every = pl.ds(0, tile_rows)
    mine = pl.ds(RADIUS, rows)
    step = INNER_ROWS
    tiles = []
    for strip in range(strips):
        queries = middle(qkv, 0, mine, strip)
        keys, values, flags = (window(ref, plane, every, strip) for ref, plane in ((qkv, 1), (qkv, 2), (keep, 0)))
        for start in range(0, rows, step):
            span = slice(start * 2 * STRIP, (start + step + 2 * RADIUS) * 2 * STRIP)
            tiles.append(
                (
                    queries[start * STRIP : (start + step) * STRIP],
                    keys[span],
                    values[span],
                    strip_bias(step, flags[span]),
                )
            )
    mixed = batched(tiles, INNER_BATCH * rows // step)
    heads[...] = jnp.concatenate(mixed, axis=0).astype(jnp.bfloat16)
    for copy in copies:
        copy.wait()
    source = jnp.concatenate([middle(resid, 0, mine, strip) for strip in range(strips)], axis=0)
    out[...] = finish(heads[...], source, w_out[...], modulation[...]).reshape(out.shape)


def rim_kernel(qkv, keep, halo, resid, w_out, modulation, out, heads):
    tile_rows, tile_cols, width = resid.shape[1:]
    strips = tile_cols // STRIP - 1
    near = 2 * RADIUS
    tiles = []
    sources = []
    for strip in range(0, strips, RIM_STRIPS):
        for side in range(2):
            inner = pl.ds(0 if side == 0 else tile_rows - near, near)
            mine = pl.ds(0 if side == 0 else tile_rows - RADIUS, RADIUS)
            far = wide(halo, side, pl.ds(0, RADIUS), strip, RIM_STRIPS)
            joined = []
            for at, (ref, plane) in zip((0, width, 2 * width), ((qkv, 1), (qkv, 2), (keep, 0))):
                local = wide(ref, plane, inner, strip, RIM_STRIPS)
                piece = far[:, at : at + local.shape[1]]
                both = jnp.concatenate([piece, local] if side == 0 else [local, piece], axis=0)
                joined.append(both.astype(jnp.bfloat16))
            bias = strip_bias(RADIUS, joined[2], RIM_STRIPS)
            tiles.append((middle(qkv, 0, mine, strip, RIM_STRIPS), joined[0], joined[1], bias))
            sources.append(middle(resid, 0, mine, strip, RIM_STRIPS))
    heads[...] = jnp.concatenate(batched(tiles, RIM_BATCH), axis=0).astype(jnp.bfloat16)
    out[...] = finish(heads[...], jnp.concatenate(sources, axis=0), w_out[...], modulation[...]).reshape(out.shape)


def load_kernel(odd, qkv_hbm, keep_hbm, one, two, qkv, keep, flags, packed, arrived):
    tile_rows, tile_cols, width = qkv.shape[1:]
    last = tile_rows - RADIUS
    starts = (jnp.where(odd[0] == 1, 0, last), jnp.where(odd[0] == 1, last, 0))
    copies = [pltpu.make_async_copy(keep_hbm, flags, arrived.at[0])]
    for out, start in zip((two, one), starts[::-1]):
        for plane in (1, 2):
            copies.append(
                pltpu.make_async_copy(
                    qkv_hbm.at[plane, pl.ds(start, RADIUS)],
                    out.at[0, :, :, pl.ds((plane - 1) * width, width)],
                    arrived.at[len(copies)],
                )
            )
    copies.append(pltpu.make_async_copy(qkv_hbm, qkv, arrived.at[len(copies)]))
    for copy in copies:
        copy.start()
    copies[0].wait()
    packed[...] = jnp.zeros_like(packed)
    for row in range(tile_rows):
        packed[row : row + 1, :tile_cols] = flags[row].astype(jnp.float32)
    turned = packed[...].T
    for row in range(tile_rows):
        column = jnp.broadcast_to(turned[:tile_cols, row : row + 1], (tile_cols, LANES))
        keep[0, row] = column.astype(jnp.bfloat16)
    for out, start in zip((one, two), starts):
        out[0, :, :, 2 * width :] = keep[0, pl.ds(start, RADIUS)]
    for copy in copies[1:]:
        copy.wait()


def pack_columns(odd, sources, one, two):
    even = odd[1] == 0
    for ref, plane, rows, lane in sources:
        tile_cols, lanes = ref.shape[-2:]
        head = ref[plane, :, 0:STRIP, :].astype(jnp.float32)[:, :RADIUS]
        tail = ref[plane, :, tile_cols - STRIP : tile_cols, :].astype(jnp.float32)[:, STRIP - RADIUS :]
        one[rows, :, lane : lane + lanes] = jnp.where(even, tail, head).astype(jnp.bfloat16)
        two[rows, :, lane : lane + lanes] = jnp.where(even, head, tail).astype(jnp.bfloat16)


def own_kernel(odd, normed, w_qkv, qkv, keep, out, one, two):
    tile_rows, tile_cols, width = qkv.shape[1:]
    rows = slice(0, tile_rows)
    pack_columns(odd, ((qkv, 1, rows, 0), (qkv, 2, rows, width), (keep, 0, rows, 2 * width)), one, two)
    out[...] = jnp.dot(normed[...], w_qkv[...], preferred_element_type=jnp.float32).astype(jnp.bfloat16)


def columns_kernel(odd, first, second, one_body, two_body, one, two, halo):
    tile_rows = one_body.shape[0]
    for above in (0, 1):

        @pl.when(odd[0] == 1 - above)
        def _():
            halo[above : above + 1] = first[...]
            halo[1 - above : 2 - above] = second[...]

    body = slice(RADIUS, RADIUS + tile_rows)
    one[0, body] = one_body[...]
    two[0, body] = two_body[...]
    top, bottom = slice(0, RADIUS), slice(RADIUS + tile_rows, 2 * RADIUS + tile_rows)
    pack_columns(odd, ((halo, 0, top, 0), (halo, 1, bottom, 0)), one.at[0], two.at[0])


def edge_columns(ref, plane, row):
    found = ref[plane, row].astype(jnp.float32)
    return found[:STRIP], found[found.shape[0] - STRIP :]


def edge_kernel(odd, qkv, keep, halo, side_one, side_two, resid, w_out, modulation, after, out, heads, far, ends, mine):
    tile_rows, tile_cols, width = resid.shape[1:]
    pad_rows = tile_rows + 2 * RADIUS
    far[:, 2 * STRIP :, :] = jnp.zeros((pad_rows, STRIP, far.shape[2]), jnp.float32)
    for row in range(pad_rows):
        local = row - RADIUS
        if 0 <= local < tile_rows:
            sources = ((qkv, 1, local, 0, width), (qkv, 2, local, width, width), (keep, 0, local, 2 * width, LANES))
        elif local < 0:
            sources = ((halo, 0, row, 0, 2 * width + LANES),)
        else:
            sources = ((halo, 1, local - tile_rows, 0, 2 * width + LANES),)
        for ref, plane, at, lane, lanes in sources:
            head, tail = edge_columns(ref, plane, at)
            far[row, 0:STRIP, lane : lane + lanes] = head
            far[row, STRIP : 2 * STRIP, lane : lane + lanes] = tail
        far[row, 2 * STRIP : 2 * STRIP + RADIUS, :] = side_one[0, row].astype(jnp.float32)
        far[row, 2 * STRIP + RADIUS : 2 * STRIP + 2 * RADIUS, :] = side_two[0, row].astype(jnp.float32)
    one_left = odd[1] == 1
    one_col = jnp.where(one_left, -RADIUS, tile_cols)
    two_col = jnp.where(one_left, tile_cols, -RADIUS)
    for row in range(tile_rows):
        for ref, plane, target in ((qkv, 0, ends), (resid, 0, mine)):
            head, tail = edge_columns(ref, plane, row)
            target[row, 0:EDGE] = head[:EDGE]
            target[row, EDGE:STRIP] = tail[EDGE:]
    rows = 4
    span = 3 * STRIP
    tiles = []
    for start in range(0, tile_rows, rows):
        count, keys = rows * STRIP, (rows + 2 * RADIUS) * span
        found = far[start : start + rows + 2 * RADIUS].reshape(keys, 2 * width + LANES).astype(jnp.bfloat16)
        q, k = iota((count, keys), 0), iota((count, keys), 1)
        q_col = q % STRIP
        q_col = jnp.where(q_col < EDGE, q_col, q_col + tile_cols - STRIP)
        k_col = k % span
        k_col = jnp.where(
            k_col < STRIP,
            k_col,
            jnp.where(
                k_col < 2 * STRIP,
                k_col + tile_cols - 2 * STRIP,
                jnp.where(
                    k_col < 2 * STRIP + RADIUS,
                    k_col - 2 * STRIP + one_col,
                    jnp.where(
                        k_col < 2 * STRIP + 2 * RADIUS,
                        k_col - 2 * STRIP - RADIUS + two_col,
                        -100 * tile_cols,
                    ),
                ),
            ),
        )
        bias = make_bias(
            q // STRIP + RADIUS, q_col, k // span, k_col, keep_row(count, found[:, 2 * width :])
        )
        tiles.append(
            (ends[start : start + rows].reshape(count, width), found[:, :width], found[:, width : 2 * width], bias)
        )
    mixed = batched(tiles, EDGE_BATCH)
    source = mine[...].reshape(tile_rows * STRIP, width)
    heads[...] = jnp.concatenate(mixed, axis=0).astype(jnp.bfloat16)
    out[...] = finish(heads[...], source, w_out[...], modulation[...])


def head_marks(width):
    feature, lane = np.arange(width)[:, None], np.arange(LANES)[None, :]
    return jnp.asarray(feature // (width // HEADS) == lane % HEADS, jnp.bfloat16)


def mark_heads(width):
    row, feature = np.arange(LANES)[:, None], np.arange(width)[None, :]
    return jnp.asarray((feature // (width // HEADS) == row % HEADS) & (row < 2 * HEADS), jnp.bfloat16)


def halves_of(values):
    high = values.astype(jnp.bfloat16)
    low = (values - high.astype(jnp.float32)).astype(jnp.bfloat16)
    return high, low


def temporal(own, other_key, other_value, marks, spread):
    width = other_key.shape[1]
    scale = (width // HEADS) ** (-0.5)
    lane = iota((1, LANES), 1)
    key_gap = other_key.astype(jnp.float32) - own[:, width : 2 * width].astype(jnp.float32)
    high, low = halves_of(own[:, :width].astype(jnp.float32) * key_gap)
    gap = (
        jnp.dot(high, marks, preferred_element_type=jnp.float32)
        + jnp.dot(low, marks, preferred_element_type=jnp.float32)
    ) * scale
    own_weight = jnp.exp(jnp.minimum(-gap, 0.0))
    other_weight = jnp.exp(jnp.minimum(gap, 0.0))
    inverse = 1.0 / (own_weight + other_weight)

    def share(weight):
        part = weight.astype(jnp.bfloat16).astype(jnp.float32) * inverse
        high, low = halves_of(part)
        packed = jnp.where(lane < HEADS, high.astype(jnp.float32), low.astype(jnp.float32)).astype(jnp.bfloat16)
        return jnp.dot(packed, spread, preferred_element_type=jnp.float32)

    return share(own_weight) * own[:, 2 * width :].astype(jnp.float32) + share(other_weight) * other_value.astype(
        jnp.float32
    )


def place(pieces, ready, ends, mixed):
    rows, tile_cols, width = mixed.shape
    for row, column, source, start, count in pieces:
        mixed[row, column : column + count] = source[start : start + count, :].astype(jnp.float32)
    mixed[:, 0:EDGE] = jnp.zeros((rows, EDGE, width), jnp.float32)
    mixed[:, tile_cols - EDGE :] = jnp.zeros((rows, EDGE, width), jnp.float32)
    ready[...] = mixed[...].astype(jnp.bfloat16)
    ends[:, 0:STRIP] = mixed[:, 0:STRIP]
    ends[:, STRIP:] = mixed[:, tile_cols - STRIP :]


def attend_frames(own, other, w_qkv, marks, spread):
    width = other.shape[1]
    pairs = jnp.dot(other[...], w_qkv[:, width:], preferred_element_type=jnp.float32).astype(jnp.bfloat16)
    return temporal(own[...], pairs[:, :width], pairs[:, width:], marks[...], spread[...])


def late_own_kernel(rim, edge, w_qkv, rim_own, edge_own):
    both = jnp.concatenate([rim[...], edge[...]], axis=0)
    found = jnp.dot(both, w_qkv[...], preferred_element_type=jnp.float32).astype(jnp.bfloat16)
    rim_own[...] = found[: rim.shape[0]]
    edge_own[...] = found[rim.shape[0] :]


def inner_done_kernel(own, other, w_qkv, marks, spread, after, ready, ends, done, mixed):
    rows, tile_cols, width = mixed.shape
    done[...] = attend_frames(own, other, w_qkv, marks, spread)
    pieces = []
    for row in range(rows):
        for strip in range(tile_cols // STRIP - 1):
            pieces.append((row, EDGE + STRIP * strip, done, (strip * rows + row) * STRIP, STRIP))
    place(pieces, ready, ends, mixed)


def rim_done_kernel(own, other, w_qkv, marks, spread, ready, ends, done, mixed):
    rows, tile_cols, width = mixed.shape
    done[...] = attend_frames(own, other, w_qkv, marks, spread)
    columns = RIM_STRIPS * STRIP
    pieces = []
    for row in range(rows):
        for part in range((tile_cols // STRIP - 1) // RIM_STRIPS):
            pieces.append((row, EDGE + columns * part, done, (part * rows + row) * columns, columns))
    place(pieces, ready, ends, mixed)


def last_kernel(own, other, w_qkv, marks, spread, inner, inner_ends, rim, rim_ends, out, left, right, arrived):
    tile_rows, tile_cols, width = out.shape[1:]
    low, high = RADIUS, tile_rows - RADIUS
    parts = (
        (slice(0, low), rim, rim_ends, slice(0, RADIUS)),
        (slice(low, high), inner, inner_ends, slice(0, high - low)),
        (slice(high, tile_rows), rim, rim_ends, slice(RADIUS, 2 * RADIUS)),
    )
    whole = []
    for target, ready, ends, rows in parts:
        size = rows.stop - rows.start
        copy = pltpu.make_async_copy(
            ready.at[pl.ds(rows.start, size), pl.ds(STRIP, tile_cols - 2 * STRIP)],
            out.at[0, pl.ds(target.start, size), pl.ds(STRIP, tile_cols - 2 * STRIP)],
            arrived.at[len(whole)],
        )
        copy.start()
        whole.append(copy)
    edge = attend_frames(own, other, w_qkv, marks, spread)
    edge = edge.reshape(tile_rows, STRIP, width)
    early = iota((1, STRIP, 1), 1) < EDGE
    for target, ready, ends, rows in parts:
        left[target] = jnp.where(early, edge[target], ends[rows, :STRIP]).astype(jnp.bfloat16)
        right[target] = jnp.where(early, ends[rows, STRIP:], edge[target]).astype(jnp.bfloat16)
    copies = [
        pltpu.make_async_copy(left, out.at[0, :, pl.ds(0, STRIP)], arrived.at[3]),
        pltpu.make_async_copy(right, out.at[0, :, pl.ds(tile_cols - STRIP, STRIP)], arrived.at[4]),
    ]
    for copy in copies:
        copy.start()
    for copy in whole + copies:
        copy.wait()


def call(body, out_shape, operands, scratch=(), flops=0, limit=24, specs=(), out_spec=VMEM):
    in_specs = [VMEM] * len(operands)
    for index, spec in specs:
        in_specs[index] = spec
    return pl.pallas_call(
        body,
        out_shape=out_shape,
        in_specs=in_specs,
        out_specs=[VMEM] * len(out_shape) if isinstance(out_shape, list) else out_spec,
        scratch_shapes=list(scratch),
        cost_estimate=pl.CostEstimate(flops=flops, bytes_accessed=0, transcendentals=0),
        compiler_params=pltpu.CompilerParams(vmem_limit_bytes=limit * MIB),
        name=body.__name__,
    )(*operands)


def exchanges(count):
    found = []
    for start in (0, 1):
        pairs = [(i, i + 1) for i in range(start, count - 1, 2)]
        found.append(pairs + [(j, i) for i, j in pairs])
    return found


def fast_device(resid, spatial_qkv, key_keep, w_spatial_out, modulation, w_temporal_qkv):
    frame_count, tile_rows, tile_cols, width = resid.shape
    strips = tile_cols // STRIP - 1
    odd = jnp.stack([lax.axis_index("row") % 2, lax.axis_index("col") % 2]).astype(jnp.int32)
    swap = [(0, 1), (1, 0)]
    bf16 = jnp.bfloat16
    struct = lambda *shape: jax.ShapeDtypeStruct(shape, bf16)
    held = lambda *shape: pltpu.VMEM(shape, bf16)
    stay = lambda x: pltpu.with_memory_space_constraint(x, pltpu.HBM)
    smem = pl.BlockSpec(memory_space=pltpu.SMEM)
    hbm = pl.BlockSpec(memory_space=pltpu.HBM)
    anywhere = pl.BlockSpec(memory_space=pl.ANY)
    marks, spread = head_marks(width), mark_heads(width)
    lanes = 2 * width + LANES
    pad_rows = tile_rows + 2 * RADIUS
    edge_count = tile_rows * STRIP

    one, two, qkv, keep = call(
        load_kernel,
        [struct(1, RADIUS, tile_cols, lanes)] * 2
        + [held(3, tile_rows, tile_cols, width), held(1, tile_rows, tile_cols, LANES)],
        (odd, stay(spatial_qkv[:, 0]), stay(key_keep.reshape(tile_rows, 1, tile_cols))),
        [
            pltpu.VMEM((tile_rows, 1, tile_cols), jnp.int32),
            pltpu.VMEM((LANES, LANES), jnp.float32),
            pltpu.SemaphoreType.DMA((6,)),
        ],
        specs=[(0, smem), (1, hbm), (2, hbm)],
    )
    pairs_one, pairs_two = exchanges(lax.axis_size("row"))
    first = lax.ppermute(one, "row", pairs_one)
    second = lax.ppermute(two, "row", pairs_two)

    inner_count = strips * (tile_rows - 2 * RADIUS) * STRIP
    inner, resid, w_spatial_out = call(
        inner_kernel,
        [struct(inner_count, width), held(*resid.shape), held(width, width)],
        (qkv, keep, stay(resid), stay(w_spatial_out), modulation),
        [held(inner_count, width), pltpu.SemaphoreType.DMA((2,))],
        specs=[(2, hbm), (3, hbm)],
    )
    inner_other = lax.ppermute(inner, "tm", swap)
    inner_own, one_body, two_body = call(
        own_kernel,
        [struct(inner_count, 3 * width)] + [held(tile_rows, RADIUS, lanes)] * 2,
        (odd, inner, w_temporal_qkv, qkv, keep),
        specs=[(0, smem)],
    )

    one, two, halo = call(
        columns_kernel,
        [struct(1, pad_rows, RADIUS, lanes)] * 2 + [held(2, RADIUS, tile_cols, lanes)],
        (odd, first, second, one_body, two_body),
        specs=[(0, smem)],
    )
    pairs_one, pairs_two = exchanges(lax.axis_size("col"))
    side_one = lax.ppermute(one, "col", pairs_one)
    side_two = lax.ppermute(two, "col", pairs_two)

    rim_count = strips * 2 * RADIUS * STRIP
    rim = call(
        rim_kernel,
        struct(rim_count, width),
        (qkv, keep, halo, resid, w_spatial_out, modulation),
        [held(rim_count, width)],
    )
    rim_other = lax.ppermute(rim, "tm", swap)

    def rows_of(count):
        whole, ends = (count, tile_cols, width), (count, 2 * STRIP, width)
        return [held(*whole), pltpu.VMEM(ends, jnp.float32)], pltpu.VMEM(whole, jnp.float32)

    shapes, scratch = rows_of(tile_rows - 2 * RADIUS)
    inner_ready, inner_ends = call(
        inner_done_kernel,
        shapes,
        (inner_own, inner_other, w_temporal_qkv, marks, spread, rim),
        [pltpu.VMEM((inner_count, width), jnp.float32), scratch],
        specs=[(5, anywhere)],
    )

    edge = call(
        edge_kernel,
        struct(edge_count, width),
        (odd, qkv, keep, halo, side_one, side_two, resid, w_spatial_out, modulation, inner_ready),
        [
            held(edge_count, width),
            pltpu.VMEM((pad_rows, 3 * STRIP, lanes), jnp.float32),
            pltpu.VMEM((tile_rows, STRIP, width), jnp.float32),
            pltpu.VMEM((tile_rows, STRIP, width), jnp.float32),
        ],
        specs=[(0, smem), (9, anywhere)],
    )
    edge_other = lax.ppermute(edge, "tm", swap)

    rim_own, edge_own = call(
        late_own_kernel,
        [struct(rim_count, 3 * width), struct(edge_count, 3 * width)],
        (rim, edge, w_temporal_qkv),
    )
    shapes, scratch = rows_of(2 * RADIUS)
    rim_ready, rim_ends = call(
        rim_done_kernel,
        shapes,
        (rim_own, rim_other, w_temporal_qkv, marks, spread),
        [pltpu.VMEM((rim_count, width), jnp.float32), scratch],
    )
    return call(
        last_kernel,
        struct(frame_count, tile_rows, tile_cols, width),
        (edge_own, edge_other, w_temporal_qkv, marks, spread, inner_ready, inner_ends, rim_ready, rim_ends),
        [
            held(tile_rows, STRIP, width),
            held(tile_rows, STRIP, width),
            pltpu.SemaphoreType.DMA((5,)),
        ],
        out_spec=hbm,
    )


def per_device(resid, *rest):
    frame_count, tile_rows, tile_cols, width = resid.shape
    fits = (
        frame_count == 1
        and lax.axis_size("tm") == 2
        and width == 9 * LANES
        and (tile_cols // STRIP - 1) % RIM_STRIPS == 0
        and tile_cols % STRIP == 0
        and tile_cols >= 2 * STRIP
        and tile_rows % 4 == 0
        and tile_rows > 2 * RADIUS
    )
    return (fast_device if fits else general_device)(resid, *rest)


def solution(mesh):
    return jax.shard_map(
        per_device,
        mesh=mesh,
        in_specs=(
            P("tm", "row", "col", None),
            P(None, "tm", "row", "col", None),
            P("tm", "row", "col"),
            P(),
            P(),
            P(),
        ),
        out_specs=P("tm", "row", "col", None),
        check_vma=False,
    )
```

```python
import functools
import math

import jax
import jax.numpy as jnp
import numpy as np
from jax import lax
from jax.experimental import pallas as pl
from jax.experimental.pallas import tpu as pltpu
from jax.sharding import PartitionSpec as P

HEADS = 16
RADIUS = 3


NEG_FILL = -1e30
EPSILON = 1e-06

LANES = 128
STRIP = 8
EDGE = STRIP // 2
MIB = 1024 * 1024
VMEM = pl.BlockSpec(memory_space=pltpu.VMEM)


def extended(array, sides, width):
    for axis, dim in sides:
        count, length = (lax.axis_size(axis), array.shape[dim])
        up = [(i, (i + 1) % count) for i in range(count - 1)]
        down = [(j, i) for i, j in up]
        last = lax.slice_in_dim(array, length - width, length, axis=dim)
        leading = lax.slice_in_dim(array, 0, width, axis=dim)
        before = lax.ppermute(last, axis, up)
        after = lax.ppermute(leading, axis, down)
        array = jnp.concatenate([before, array, after], axis=dim)
    return array


def softmax_parts(scores, allowed):
    masked = jnp.where(allowed, scores, NEG_FILL)
    top_score = jnp.max(masked, -1, keepdims=True)
    weights_f = jnp.where(allowed, jnp.exp(masked - top_score), 0.0)
    return (weights_f.astype(jnp.bfloat16), jnp.sum(weights_f, -1))


def frame_attend(gathered, head_count):
    frames_all, single, items, width_three = gathered.shape
    width = width_three // 3
    head_size = width // head_count
    split_qkv = gathered.reshape(frames_all, items, 3, head_count, head_size)
    scores = jnp.einsum(
        "fphd,gphd->phfg",
        split_qkv[:, :, 0],
        split_qkv[:, :, 1],
        preferred_element_type=jnp.float32,
    ) * head_size ** (-0.5)
    weights_b, totals = softmax_parts(scores, True)
    weighted = jnp.einsum(
        "phfg,gphd->fphd", weights_b, split_qkv[:, :, 2], preferred_element_type=jnp.float32
    )
    result = weighted / jnp.transpose(totals, (2, 0, 1))[..., None]
    return result.astype(jnp.bfloat16).reshape(frames_all, single, items, width)


def general_device(resid, spatial_qkv, key_keep, w_spatial_out, modulation, w_temporal_qkv):
    frame_count, tile_rows, tile_cols, width = resid.shape
    head_size = width // HEADS
    score_scale = head_size ** (-0.5)
    tile_tokens = tile_rows * tile_cols
    pair = spatial_qkv[1:3]
    keep_flags = key_keep.astype(jnp.bfloat16)[None, :, :, :, None]
    padded_pair, padded_keep = (
        extended(pair, (("row", 2), ("col", 3)), RADIUS),
        extended(keep_flags, (("row", 2), ("col", 3)), RADIUS),
    )
    pad_rows = tile_rows + 2 * RADIUS
    pad_cols = tile_cols + 2 * RADIUS
    key_count = pad_rows * pad_cols
    queries = spatial_qkv[0].reshape(frame_count, tile_tokens, HEADS, head_size)
    keys_pad = padded_pair[0].reshape(frame_count, key_count, HEADS, head_size)
    values_pad = padded_pair[1].reshape(frame_count, key_count, HEADS, head_size)
    query_index = jnp.arange(tile_tokens)
    query_row = query_index // tile_cols
    query_col = query_index % tile_cols
    key_index = jnp.arange(key_count)
    key_row = key_index // pad_cols
    key_col = key_index % pad_cols
    row_gap = key_row[None, :] - query_row[:, None] - RADIUS
    col_gap = key_col[None, :] - query_col[:, None] - RADIUS
    in_window = (jnp.abs(row_gap) <= RADIUS) & (jnp.abs(col_gap) <= RADIUS)
    itself = (row_gap == 0) & (col_gap == 0)
    key_live = padded_keep.reshape(frame_count, key_count) > 0.5
    allowed = (in_window[None] & (key_live[:, None, :] | itself[None]))[:, None]
    scores = (
        jnp.einsum("fqhd,fkhd->fhqk", queries, keys_pad, preferred_element_type=jnp.float32)
        * score_scale
    )
    weights_b, totals = softmax_parts(scores, allowed)
    weighted = jnp.einsum(
        "fhqk,fkhd->fqhd", weights_b, values_pad, preferred_element_type=jnp.float32
    )
    spatial_heads = (weighted / jnp.transpose(totals, (0, 2, 1))[..., None]).astype(jnp.bfloat16)
    spatial_heads = spatial_heads.reshape(frame_count * tile_tokens, width)
    stream = resid.reshape(frame_count * tile_tokens, width).astype(jnp.float32) + jnp.dot(
        spatial_heads, w_spatial_out, preferred_element_type=jnp.float32
    )
    average = jnp.mean(stream, -1, keepdims=True)
    centered = stream - average
    variance = jnp.mean(centered * centered, -1, keepdims=True)
    normed = (
        centered * lax.rsqrt(variance + EPSILON) * (1.0 + modulation[1]) + modulation[0]
    ).astype(jnp.bfloat16)
    tm_count = lax.axis_size("tm")
    part_tokens = tile_tokens // tm_count
    normed_parts = normed.reshape(frame_count, tm_count, part_tokens, width)
    gathered = lax.all_to_all(normed_parts, "tm", split_axis=1, concat_axis=0, tiled=True)
    frames_all, single, items, unused = gathered.shape
    projected = jnp.dot(
        gathered.reshape(frames_all * single * items, width),
        w_temporal_qkv,
        preferred_element_type=jnp.float32,
    ).astype(jnp.bfloat16)
    projected = projected.reshape(frames_all, single, items, 3 * width)
    result = lax.all_to_all(
        frame_attend(projected, HEADS), "tm", split_axis=0, concat_axis=1, tiled=True
    )
    return result.reshape(frame_count, tile_rows, tile_cols, width)


def iota(shape, dim):
    return lax.broadcasted_iota(jnp.int32, shape, dim)


def attend(tiles):
    width = tiles[0][0].shape[1]
    head = width // HEADS
    factor = head ** (-0.5) * math.log2(math.e)
    lane = iota((1, 2 * LANES), 1)
    spans = []
    for pair in range(HEADS // 2):
        start = LANES * pair
        low = 2 * head * pair - start
        spans.append((slice(start, start + 2 * LANES), low, low + head, low + 2 * head))
    scores = []
    for queries, keys, values, bias in tiles:
        for span, low, mid, high in spans:
            first = jnp.where((lane >= low) & (lane < mid), queries[:, span], 0.0)
            second = jnp.where((lane >= mid) & (lane < high), queries[:, span], 0.0)
            both = jnp.concatenate([first, second], axis=0).astype(jnp.bfloat16)
            scores.append(
                lax.dot_general(
                    both, keys[:, span], (((1,), (1,)), ((), ())), preferred_element_type=jnp.float32
                )
            )
    weights = []
    for index, (queries, keys, values, bias) in enumerate(tiles):
        bias_two = jnp.concatenate([bias, bias], axis=0)
        for pair in range(len(spans)):
            score = scores[index * len(spans) + pair] + bias_two
            top = jnp.max(score, -1, keepdims=True)
            weight = jnp.exp2((score - top) * factor)
            weights.append((weight.astype(jnp.bfloat16), 1.0 / jnp.sum(weight, -1, keepdims=True)))
    results = []
    edge_lane = iota((1, LANES), 1)
    for index, (queries, keys, values, bias) in enumerate(tiles):
        count = queries.shape[0]
        pairs = []
        for pair, (span, low, mid, high) in enumerate(spans):
            weight, inverse = weights[index * len(spans) + pair]
            mixed = jnp.dot(weight, values[:, span], preferred_element_type=jnp.float32) * inverse
            pairs.append(jnp.where(lane < mid, mixed[:count], mixed[count:]))
        blocks = [pairs[0][:, :LANES]]
        for pair in range(1, len(spans)):
            cut = spans[pair][1]
            blocks.append(jnp.where(edge_lane < cut, pairs[pair - 1][:, LANES:], pairs[pair][:, :LANES]))
        blocks.append(pairs[-1][:, LANES:])
        results.append(jnp.concatenate(blocks, axis=1))
    return results


def keep_row(count, keep):
    picker = jnp.where(iota((count, LANES), 1) == 0, 1.0, 0.0).astype(jnp.bfloat16)
    return lax.dot_general(
        picker, keep, (((1,), (1,)), ((), ())), preferred_element_type=jnp.float32
    )


def make_bias(q_row, q_col, k_row, k_col, keep):
    row_gap, col_gap = k_row - q_row, k_col - q_col
    near = (jnp.abs(row_gap) <= RADIUS) & (jnp.abs(col_gap) <= RADIUS)
    itself = (row_gap == 0) & (col_gap == 0)
    return jnp.where(near & ((keep > 0.5) | itself), 0.0, NEG_FILL)


def strip_bias(rows, keep, strips=1):
    columns, key_columns = strips * STRIP, (strips + 1) * STRIP
    count, keys = rows * columns, (rows + 2 * RADIUS) * key_columns
    q, k = iota((count, keys), 0), iota((count, keys), 1)
    return make_bias(
        q // columns + RADIUS, q % columns + EDGE, k // key_columns, k % key_columns, keep_row(count, keep)
    )


def finish(heads, resid, w_out, modulation):
    return adapt(resid + jnp.dot(heads, w_out, preferred_element_type=jnp.float32), modulation)


def adapt(stream, modulation):
    average = jnp.mean(stream, -1, keepdims=True)
    centered = stream - average
    variance = jnp.mean(centered * centered, -1, keepdims=True)
    scaled = centered * lax.rsqrt(variance + EPSILON)
    return (scaled * (1.0 + modulation[1:2]) + modulation[0:1]).astype(jnp.bfloat16)


def wide(ref, plane, rows, strip, strips=1):
    found = ref[plane, rows, pl.ds(STRIP * strip, (strips + 1) * STRIP), :].astype(jnp.float32)
    return found.reshape(found.shape[0] * found.shape[1], found.shape[2])


def window(ref, plane, rows, strip):
    return wide(ref, plane, rows, strip).astype(jnp.bfloat16)


def middle(ref, plane, rows, strip, strips=1):
    found = ref[plane, rows, pl.ds(STRIP * strip, (strips + 1) * STRIP), :].astype(jnp.float32)
    found = found[:, EDGE : EDGE + strips * STRIP]
    return found.reshape(found.shape[0] * found.shape[1], found.shape[2])


INNER_ROWS = 6
INNER_BATCH = 4
RIM_BATCH = 4
RIM_STRIPS = 2
EDGE_BATCH = 3


def batched(tiles, size):
    found = []
    for start in range(0, len(tiles), size):
        found += attend(tiles[start : start + size])
    return found


def inner_kernel(qkv, keep, resid_hbm, w_hbm, modulation, out, resid, w_out, heads, arrived):
    copies = [
        pltpu.make_async_copy(w_hbm, w_out, arrived.at[0]),
        pltpu.make_async_copy(resid_hbm, resid, arrived.at[1]),
    ]
    for copy in copies:
        copy.start()
    tile_rows, tile_cols, width = resid.shape[1:]
    rows = tile_rows - 2 * RADIUS
    strips = tile_cols // STRIP - 1
    every = pl.ds(0, tile_rows)
    mine = pl.ds(RADIUS, rows)
    step = INNER_ROWS
    tiles = []
    for strip in range(strips):
        queries = middle(qkv, 0, mine, strip)
        keys, values, flags = (window(ref, plane, every, strip) for ref, plane in ((qkv, 1), (qkv, 2), (keep, 0)))
        for start in range(0, rows, step):
            span = slice(start * 2 * STRIP, (start + step + 2 * RADIUS) * 2 * STRIP)
            tiles.append(
                (
                    queries[start * STRIP : (start + step) * STRIP],
                    keys[span],
                    values[span],
                    strip_bias(step, flags[span]),
                )
            )
    mixed = batched(tiles, INNER_BATCH * rows // step)
    heads[...] = jnp.concatenate(mixed, axis=0).astype(jnp.bfloat16)
    copies[0].wait()
    product = jnp.dot(heads[...], w_out[...], preferred_element_type=jnp.float32)
    copies[1].wait()
    source = jnp.concatenate([middle(resid, 0, mine, strip) for strip in range(strips)], axis=0)
    out[...] = adapt(source + product, modulation[...]).reshape(out.shape)


def rim_kernel(qkv, keep, halo, resid, w_out, modulation, out, heads):
    tile_rows, tile_cols, width = resid.shape[1:]
    strips = tile_cols // STRIP - 1
    near = 2 * RADIUS
    tiles = []
    sources = []
    for strip in range(0, strips, RIM_STRIPS):
        for side in range(2):
            inner = pl.ds(0 if side == 0 else tile_rows - near, near)
            mine = pl.ds(0 if side == 0 else tile_rows - RADIUS, RADIUS)
            far = wide(halo, side, pl.ds(0, RADIUS), strip, RIM_STRIPS)
            joined = []
            for at, (ref, plane) in zip((0, width, 2 * width), ((qkv, 1), (qkv, 2), (keep, 0))):
                local = wide(ref, plane, inner, strip, RIM_STRIPS)
                piece = far[:, at : at + local.shape[1]]
                both = jnp.concatenate([piece, local] if side == 0 else [local, piece], axis=0)
                joined.append(both.astype(jnp.bfloat16))
            bias = strip_bias(RADIUS, joined[2], RIM_STRIPS)
            tiles.append((middle(qkv, 0, mine, strip, RIM_STRIPS), joined[0], joined[1], bias))
            sources.append(middle(resid, 0, mine, strip, RIM_STRIPS))
    heads[...] = jnp.concatenate(batched(tiles, RIM_BATCH), axis=0).astype(jnp.bfloat16)
    out[...] = finish(heads[...], jnp.concatenate(sources, axis=0), w_out[...], modulation[...]).reshape(out.shape)


def load_kernel(odd, qkv_hbm, keep_hbm, one, two, qkv, keep, flags, packed, arrived):
    tile_rows, tile_cols, width = qkv.shape[1:]
    last = tile_rows - RADIUS
    starts = (jnp.where(odd[0] == 1, 0, last), jnp.where(odd[0] == 1, last, 0))
    copies = [pltpu.make_async_copy(keep_hbm, flags, arrived.at[0])]
    for out, start in zip((two, one), starts[::-1]):
        for plane in (1, 2):
            copies.append(
                pltpu.make_async_copy(
                    qkv_hbm.at[plane, pl.ds(start, RADIUS)],
                    out.at[0, :, :, pl.ds((plane - 1) * width, width)],
                    arrived.at[len(copies)],
                )
            )
    copies.append(pltpu.make_async_copy(qkv_hbm, qkv, arrived.at[len(copies)]))
    for copy in copies:
        copy.start()
    copies[0].wait()
    packed[...] = jnp.zeros_like(packed)
    for row in range(tile_rows):
        packed[row : row + 1, :tile_cols] = flags[row].astype(jnp.float32)
    turned = packed[...].T
    for row in range(tile_rows):
        column = jnp.broadcast_to(turned[:tile_cols, row : row + 1], (tile_cols, LANES))
        keep[0, row] = column.astype(jnp.bfloat16)
    for out, start in zip((one, two), starts):
        out[0, :, :, 2 * width :] = keep[0, pl.ds(start, RADIUS)]
    for copy in copies[1:]:
        copy.wait()


def pack_columns(odd, sources, one, two):
    even = odd[1] == 0
    for ref, plane, rows, lane in sources:
        tile_cols, lanes = ref.shape[-2:]
        head = ref[plane, :, 0:STRIP, :].astype(jnp.float32)[:, :RADIUS]
        tail = ref[plane, :, tile_cols - STRIP : tile_cols, :].astype(jnp.float32)[:, STRIP - RADIUS :]
        one[rows, :, lane : lane + lanes] = jnp.where(even, tail, head).astype(jnp.bfloat16)
        two[rows, :, lane : lane + lanes] = jnp.where(even, head, tail).astype(jnp.bfloat16)


def own_kernel(odd, normed, w_qkv, qkv, keep, out, one, two):
    tile_rows, tile_cols, width = qkv.shape[1:]
    rows = slice(0, tile_rows)
    pack_columns(odd, ((qkv, 1, rows, 0), (qkv, 2, rows, width), (keep, 0, rows, 2 * width)), one, two)
    out[...] = jnp.dot(normed[...], w_qkv[...], preferred_element_type=jnp.float32).astype(jnp.bfloat16)


def columns_kernel(odd, first, second, one_body, two_body, one, two, halo):
    tile_rows = one_body.shape[0]
    for above in (0, 1):

        @pl.when(odd[0] == 1 - above)
        def _():
            halo[above : above + 1] = first[...]
            halo[1 - above : 2 - above] = second[...]

    body = slice(RADIUS, RADIUS + tile_rows)
    one[0, body] = one_body[...]
    two[0, body] = two_body[...]
    top, bottom = slice(0, RADIUS), slice(RADIUS + tile_rows, 2 * RADIUS + tile_rows)
    pack_columns(odd, ((halo, 0, top, 0), (halo, 1, bottom, 0)), one.at[0], two.at[0])


def edge_columns(ref, plane, row):
    found = ref[plane, row].astype(jnp.float32)
    return found[:STRIP], found[found.shape[0] - STRIP :]


def edge_kernel(odd, qkv, keep, halo, side_one, side_two, resid, w_out, modulation, after, out, heads, far, ends, mine):
    tile_rows, tile_cols, width = resid.shape[1:]
    pad_rows = tile_rows + 2 * RADIUS
    far[:, 2 * STRIP :, :] = jnp.zeros((pad_rows, STRIP, far.shape[2]), jnp.float32)
    for row in range(pad_rows):
        local = row - RADIUS
        if 0 <= local < tile_rows:
            sources = ((qkv, 1, local, 0, width), (qkv, 2, local, width, width), (keep, 0, local, 2 * width, LANES))
        elif local < 0:
            sources = ((halo, 0, row, 0, 2 * width + LANES),)
        else:
            sources = ((halo, 1, local - tile_rows, 0, 2 * width + LANES),)
        for ref, plane, at, lane, lanes in sources:
            head, tail = edge_columns(ref, plane, at)
            far[row, 0:STRIP, lane : lane + lanes] = head
            far[row, STRIP : 2 * STRIP, lane : lane + lanes] = tail
        far[row, 2 * STRIP : 2 * STRIP + RADIUS, :] = side_one[0, row].astype(jnp.float32)
        far[row, 2 * STRIP + RADIUS : 2 * STRIP + 2 * RADIUS, :] = side_two[0, row].astype(jnp.float32)
    one_left = odd[1] == 1
    one_col = jnp.where(one_left, -RADIUS, tile_cols)
    two_col = jnp.where(one_left, tile_cols, -RADIUS)
    for row in range(tile_rows):
        for ref, plane, target in ((qkv, 0, ends), (resid, 0, mine)):
            head, tail = edge_columns(ref, plane, row)
            target[row, 0:EDGE] = head[:EDGE]
            target[row, EDGE:STRIP] = tail[EDGE:]
    rows = 4
    span = 3 * STRIP
    tiles = []
    for start in range(0, tile_rows, rows):
        count, keys = rows * STRIP, (rows + 2 * RADIUS) * span
        found = far[start : start + rows + 2 * RADIUS].reshape(keys, 2 * width + LANES).astype(jnp.bfloat16)
        q, k = iota((count, keys), 0), iota((count, keys), 1)
        q_col = q % STRIP
        q_col = jnp.where(q_col < EDGE, q_col, q_col + tile_cols - STRIP)
        k_col = k % span
        k_col = jnp.where(
            k_col < STRIP,
            k_col,
            jnp.where(
                k_col < 2 * STRIP,
                k_col + tile_cols - 2 * STRIP,
                jnp.where(
                    k_col < 2 * STRIP + RADIUS,
                    k_col - 2 * STRIP + one_col,
                    jnp.where(
                        k_col < 2 * STRIP + 2 * RADIUS,
                        k_col - 2 * STRIP - RADIUS + two_col,
                        -100 * tile_cols,
                    ),
                ),
            ),
        )
        bias = make_bias(
            q // STRIP + RADIUS, q_col, k // span, k_col, keep_row(count, found[:, 2 * width :])
        )
        tiles.append(
            (ends[start : start + rows].reshape(count, width), found[:, :width], found[:, width : 2 * width], bias)
        )
    mixed = batched(tiles, EDGE_BATCH)
    source = mine[...].reshape(tile_rows * STRIP, width)
    heads[...] = jnp.concatenate(mixed, axis=0).astype(jnp.bfloat16)
    out[...] = finish(heads[...], source, w_out[...], modulation[...])


def head_marks(width):
    feature, lane = np.arange(width)[:, None], np.arange(LANES)[None, :]
    return jnp.asarray(feature // (width // HEADS) == lane % HEADS, jnp.bfloat16)


def mark_heads(width):
    row, feature = np.arange(LANES)[:, None], np.arange(2 * width)[None, :]
    mine = (feature % width) // (width // HEADS) == row % HEADS
    return jnp.asarray(mine & (row // (2 * HEADS) == feature // width), jnp.bfloat16)


def halves_of(values):
    high = values.astype(jnp.bfloat16)
    low = (values - high.astype(jnp.float32)).astype(jnp.bfloat16)
    return high, low


def temporal(own, other_key, other_value, marks, spread):
    width = other_key.shape[1]
    scale = (width // HEADS) ** (-0.5)
    lane = iota((1, LANES), 1)
    key_gap = other_key.astype(jnp.float32) - own[:, width : 2 * width].astype(jnp.float32)
    high, low = halves_of(own[:, :width].astype(jnp.float32) * key_gap)
    gap = (
        jnp.dot(high, marks, preferred_element_type=jnp.float32)
        + jnp.dot(low, marks, preferred_element_type=jnp.float32)
    ) * scale
    own_weight = jnp.exp(jnp.minimum(-gap, 0.0))
    other_weight = jnp.exp(jnp.minimum(gap, 0.0))
    inverse = 1.0 / (own_weight + other_weight)

    def halves(weight):
        return [x.astype(jnp.float32) for x in halves_of(weight.astype(jnp.bfloat16).astype(jnp.float32) * inverse)]

    own_high, own_low = halves(own_weight)
    other_high, other_low = halves(other_weight)
    packed = jnp.where(
        lane < 2 * HEADS,
        jnp.where(lane < HEADS, own_high, own_low),
        jnp.where(lane < 3 * HEADS, other_high, other_low),
    )
    shares = jnp.dot(packed.astype(jnp.bfloat16), spread, preferred_element_type=jnp.float32)
    own_part = shares[:, :width] * own[:, 2 * width :].astype(jnp.float32)
    return own_part + shares[:, width:] * other_value.astype(jnp.float32)


def place(pieces, ready, ends, mixed):
    rows, tile_cols, width = mixed.shape
    for row, column, source, start, count in pieces:
        mixed[row, column : column + count] = source[start : start + count, :].astype(jnp.float32)
    mixed[:, 0:EDGE] = jnp.zeros((rows, EDGE, width), jnp.float32)
    mixed[:, tile_cols - EDGE :] = jnp.zeros((rows, EDGE, width), jnp.float32)
    ready[...] = mixed[...].astype(jnp.bfloat16)
    ends[:, 0:STRIP] = mixed[:, 0:STRIP]
    ends[:, STRIP:] = mixed[:, tile_cols - STRIP :]


def attend_frames(own, other, w_qkv, marks, spread):
    width = other.shape[1]
    pairs = jnp.dot(other[...], w_qkv[:, width:], preferred_element_type=jnp.float32).astype(jnp.bfloat16)
    return temporal(own[...], pairs[:, :width], pairs[:, width:], marks[...], spread[...])


def late_own_kernel(rim, edge, w_qkv, rim_own, edge_own):
    both = jnp.concatenate([rim[...], edge[...]], axis=0)
    found = jnp.dot(both, w_qkv[...], preferred_element_type=jnp.float32).astype(jnp.bfloat16)
    rim_own[...] = found[: rim.shape[0]]
    edge_own[...] = found[rim.shape[0] :]


def inner_done_kernel(own, other, w_qkv, marks, spread, after, ready, ends, done, mixed):
    rows, tile_cols, width = mixed.shape
    done[...] = attend_frames(own, other, w_qkv, marks, spread)
    pieces = []
    for row in range(rows):
        for strip in range(tile_cols // STRIP - 1):
            pieces.append((row, EDGE + STRIP * strip, done, (strip * rows + row) * STRIP, STRIP))
    place(pieces, ready, ends, mixed)


def rim_done_kernel(own, other, w_qkv, marks, spread, ready, ends, done, mixed):
    rows, tile_cols, width = mixed.shape
    done[...] = attend_frames(own, other, w_qkv, marks, spread)
    columns = RIM_STRIPS * STRIP
    pieces = []
    for row in range(rows):
        for part in range((tile_cols // STRIP - 1) // RIM_STRIPS):
            pieces.append((row, EDGE + columns * part, done, (part * rows + row) * columns, columns))
    place(pieces, ready, ends, mixed)


def last_kernel(own, other, w_qkv, marks, spread, inner, inner_ends, rim, rim_ends, out, left, right, arrived):
    tile_rows, tile_cols, width = out.shape[1:]
    low, high = RADIUS, tile_rows - RADIUS
    parts = (
        (slice(0, low), rim, rim_ends, slice(0, RADIUS)),
        (slice(low, high), inner, inner_ends, slice(0, high - low)),
        (slice(high, tile_rows), rim, rim_ends, slice(RADIUS, 2 * RADIUS)),
    )
    whole = []
    for target, ready, ends, rows in parts:
        size = rows.stop - rows.start
        copy = pltpu.make_async_copy(
            ready.at[pl.ds(rows.start, size), pl.ds(STRIP, tile_cols - 2 * STRIP)],
            out.at[0, pl.ds(target.start, size), pl.ds(STRIP, tile_cols - 2 * STRIP)],
            arrived.at[len(whole)],
        )
        copy.start()
        whole.append(copy)
    edge = attend_frames(own, other, w_qkv, marks, spread)
    edge = edge.reshape(tile_rows, STRIP, width)
    early = iota((1, STRIP, 1), 1) < EDGE
    for target, ready, ends, rows in parts:
        left[target] = jnp.where(early, edge[target], ends[rows, :STRIP]).astype(jnp.bfloat16)
        right[target] = jnp.where(early, ends[rows, STRIP:], edge[target]).astype(jnp.bfloat16)
    copies = [
        pltpu.make_async_copy(left, out.at[0, :, pl.ds(0, STRIP)], arrived.at[3]),
        pltpu.make_async_copy(right, out.at[0, :, pl.ds(tile_cols - STRIP, STRIP)], arrived.at[4]),
    ]
    for copy in copies:
        copy.start()
    for copy in whole + copies:
        copy.wait()


def call(body, out_shape, operands, scratch=(), flops=0, limit=24, specs=(), out_spec=VMEM):
    in_specs = [VMEM] * len(operands)
    for index, spec in specs:
        in_specs[index] = spec
    return pl.pallas_call(
        body,
        out_shape=out_shape,
        in_specs=in_specs,
        out_specs=[VMEM] * len(out_shape) if isinstance(out_shape, list) else out_spec,
        scratch_shapes=list(scratch),
        cost_estimate=pl.CostEstimate(flops=flops, bytes_accessed=0, transcendentals=0),
        compiler_params=pltpu.CompilerParams(vmem_limit_bytes=limit * MIB),
        name=body.__name__,
    )(*operands)


def exchanges(count):
    found = []
    for start in (0, 1):
        pairs = [(i, i + 1) for i in range(start, count - 1, 2)]
        found.append(pairs + [(j, i) for i, j in pairs])
    return found


def fast_device(resid, spatial_qkv, key_keep, w_spatial_out, modulation, w_temporal_qkv):
    frame_count, tile_rows, tile_cols, width = resid.shape
    strips = tile_cols // STRIP - 1
    odd = jnp.stack([lax.axis_index("row") % 2, lax.axis_index("col") % 2]).astype(jnp.int32)
    swap = [(0, 1), (1, 0)]
    bf16 = jnp.bfloat16
    struct = lambda *shape: jax.ShapeDtypeStruct(shape, bf16)
    held = lambda *shape: pltpu.VMEM(shape, bf16)
    stay = lambda x: pltpu.with_memory_space_constraint(x, pltpu.HBM)
    smem = pl.BlockSpec(memory_space=pltpu.SMEM)
    hbm = pl.BlockSpec(memory_space=pltpu.HBM)
    anywhere = pl.BlockSpec(memory_space=pl.ANY)
    marks, spread = head_marks(width), mark_heads(width)
    lanes = 2 * width + LANES
    pad_rows = tile_rows + 2 * RADIUS
    edge_count = tile_rows * STRIP

    one, two, qkv, keep = call(
        load_kernel,
        [struct(1, RADIUS, tile_cols, lanes)] * 2
        + [held(3, tile_rows, tile_cols, width), held(1, tile_rows, tile_cols, LANES)],
        (odd, stay(spatial_qkv[:, 0]), stay(key_keep.reshape(tile_rows, 1, tile_cols))),
        [
            pltpu.VMEM((tile_rows, 1, tile_cols), jnp.int32),
            pltpu.VMEM((LANES, LANES), jnp.float32),
            pltpu.SemaphoreType.DMA((6,)),
        ],
        specs=[(0, smem), (1, hbm), (2, hbm)],
    )
    pairs_one, pairs_two = exchanges(lax.axis_size("row"))
    first = lax.ppermute(one, "row", pairs_one)
    second = lax.ppermute(two, "row", pairs_two)

    inner_count = strips * (tile_rows - 2 * RADIUS) * STRIP
    inner, resid, w_spatial_out = call(
        inner_kernel,
        [struct(inner_count, width), held(*resid.shape), held(width, width)],
        (qkv, keep, stay(resid), stay(w_spatial_out), modulation),
        [held(inner_count, width), pltpu.SemaphoreType.DMA((2,))],
        specs=[(2, hbm), (3, hbm)],
    )
    inner_other = lax.ppermute(inner, "tm", swap)
    inner_own, one_body, two_body = call(
        own_kernel,
        [struct(inner_count, 3 * width)] + [held(tile_rows, RADIUS, lanes)] * 2,
        (odd, inner, w_temporal_qkv, qkv, keep),
        specs=[(0, smem)],
    )

    one, two, halo = call(
        columns_kernel,
        [struct(1, pad_rows, RADIUS, lanes)] * 2 + [held(2, RADIUS, tile_cols, lanes)],
        (odd, first, second, one_body, two_body),
        specs=[(0, smem)],
    )
    pairs_one, pairs_two = exchanges(lax.axis_size("col"))
    side_one = lax.ppermute(one, "col", pairs_one)
    side_two = lax.ppermute(two, "col", pairs_two)

    rim_count = strips * 2 * RADIUS * STRIP
    rim = call(
        rim_kernel,
        struct(rim_count, width),
        (qkv, keep, halo, resid, w_spatial_out, modulation),
        [held(rim_count, width)],
    )
    rim_other = lax.ppermute(rim, "tm", swap)

    def rows_of(count):
        whole, ends = (count, tile_cols, width), (count, 2 * STRIP, width)
        return [held(*whole), pltpu.VMEM(ends, jnp.float32)], pltpu.VMEM(whole, jnp.float32)

    shapes, scratch = rows_of(tile_rows - 2 * RADIUS)
    inner_ready, inner_ends = call(
        inner_done_kernel,
        shapes,
        (inner_own, inner_other, w_temporal_qkv, marks, spread, rim),
        [pltpu.VMEM((inner_count, width), jnp.float32), scratch],
        specs=[(5, anywhere)],
    )

    edge = call(
        edge_kernel,
        struct(edge_count, width),
        (odd, qkv, keep, halo, side_one, side_two, resid, w_spatial_out, modulation, inner_ready),
        [
            held(edge_count, width),
            pltpu.VMEM((pad_rows, 3 * STRIP, lanes), jnp.float32),
            pltpu.VMEM((tile_rows, STRIP, width), jnp.float32),
            pltpu.VMEM((tile_rows, STRIP, width), jnp.float32),
        ],
        specs=[(0, smem), (9, anywhere)],
    )
    edge_other = lax.ppermute(edge, "tm", swap)

    rim_own, edge_own = call(
        late_own_kernel,
        [struct(rim_count, 3 * width), struct(edge_count, 3 * width)],
        (rim, edge, w_temporal_qkv),
    )
    shapes, scratch = rows_of(2 * RADIUS)
    rim_ready, rim_ends = call(
        rim_done_kernel,
        shapes,
        (rim_own, rim_other, w_temporal_qkv, marks, spread),
        [pltpu.VMEM((rim_count, width), jnp.float32), scratch],
    )
    return call(
        last_kernel,
        struct(frame_count, tile_rows, tile_cols, width),
        (edge_own, edge_other, w_temporal_qkv, marks, spread, inner_ready, inner_ends, rim_ready, rim_ends),
        [
            held(tile_rows, STRIP, width),
            held(tile_rows, STRIP, width),
            pltpu.SemaphoreType.DMA((5,)),
        ],
        out_spec=hbm,
    )


def per_device(resid, *rest):
    frame_count, tile_rows, tile_cols, width = resid.shape
    fits = (
        frame_count == 1
        and lax.axis_size("tm") == 2
        and width == 9 * LANES
        and (tile_cols // STRIP - 1) % RIM_STRIPS == 0
        and tile_cols % STRIP == 0
        and tile_cols >= 2 * STRIP
        and tile_rows % 4 == 0
        and tile_rows > 2 * RADIUS
    )
    return (fast_device if fits else general_device)(resid, *rest)


def solution(mesh):
    return jax.shard_map(
        per_device,
        mesh=mesh,
        in_specs=(
            P("tm", "row", "col", None),
            P(None, "tm", "row", "col", None),
            P("tm", "row", "col"),
            P(),
            P(),
            P(),
        ),
        out_specs=P("tm", "row", "col", None),
        check_vma=False,
    )
```

```python
import functools
import math

import jax
import jax.numpy as jnp
import numpy as np
from jax import lax
from jax.experimental import pallas as pl
from jax.experimental.pallas import tpu as pltpu
from jax.sharding import PartitionSpec as P

HEADS = 16
RADIUS = 3


NEG_FILL = -1e30
EPSILON = 1e-06

LANES = 128
STRIP = 8
EDGE = STRIP // 2
MIB = 1024 * 1024
VMEM = pl.BlockSpec(memory_space=pltpu.VMEM)


def extended(array, sides, width):
    for axis, dim in sides:
        count, length = (lax.axis_size(axis), array.shape[dim])
        up = [(i, (i + 1) % count) for i in range(count - 1)]
        down = [(j, i) for i, j in up]
        last = lax.slice_in_dim(array, length - width, length, axis=dim)
        leading = lax.slice_in_dim(array, 0, width, axis=dim)
        before = lax.ppermute(last, axis, up)
        after = lax.ppermute(leading, axis, down)
        array = jnp.concatenate([before, array, after], axis=dim)
    return array


def softmax_parts(scores, allowed):
    masked = jnp.where(allowed, scores, NEG_FILL)
    top_score = jnp.max(masked, -1, keepdims=True)
    weights_f = jnp.where(allowed, jnp.exp(masked - top_score), 0.0)
    return (weights_f.astype(jnp.bfloat16), jnp.sum(weights_f, -1))


def frame_attend(gathered, head_count):
    frames_all, single, items, width_three = gathered.shape
    width = width_three // 3
    head_size = width // head_count
    split_qkv = gathered.reshape(frames_all, items, 3, head_count, head_size)
    scores = jnp.einsum(
        "fphd,gphd->phfg",
        split_qkv[:, :, 0],
        split_qkv[:, :, 1],
        preferred_element_type=jnp.float32,
    ) * head_size ** (-0.5)
    weights_b, totals = softmax_parts(scores, True)
    weighted = jnp.einsum(
        "phfg,gphd->fphd", weights_b, split_qkv[:, :, 2], preferred_element_type=jnp.float32
    )
    result = weighted / jnp.transpose(totals, (2, 0, 1))[..., None]
    return result.astype(jnp.bfloat16).reshape(frames_all, single, items, width)


def general_device(resid, spatial_qkv, key_keep, w_spatial_out, modulation, w_temporal_qkv):
    frame_count, tile_rows, tile_cols, width = resid.shape
    head_size = width // HEADS
    score_scale = head_size ** (-0.5)
    tile_tokens = tile_rows * tile_cols
    pair = spatial_qkv[1:3]
    keep_flags = key_keep.astype(jnp.bfloat16)[None, :, :, :, None]
    padded_pair, padded_keep = (
        extended(pair, (("row", 2), ("col", 3)), RADIUS),
        extended(keep_flags, (("row", 2), ("col", 3)), RADIUS),
    )
    pad_rows = tile_rows + 2 * RADIUS
    pad_cols = tile_cols + 2 * RADIUS
    key_count = pad_rows * pad_cols
    queries = spatial_qkv[0].reshape(frame_count, tile_tokens, HEADS, head_size)
    keys_pad = padded_pair[0].reshape(frame_count, key_count, HEADS, head_size)
    values_pad = padded_pair[1].reshape(frame_count, key_count, HEADS, head_size)
    query_index = jnp.arange(tile_tokens)
    query_row = query_index // tile_cols
    query_col = query_index % tile_cols
    key_index = jnp.arange(key_count)
    key_row = key_index // pad_cols
    key_col = key_index % pad_cols
    row_gap = key_row[None, :] - query_row[:, None] - RADIUS
    col_gap = key_col[None, :] - query_col[:, None] - RADIUS
    in_window = (jnp.abs(row_gap) <= RADIUS) & (jnp.abs(col_gap) <= RADIUS)
    itself = (row_gap == 0) & (col_gap == 0)
    key_live = padded_keep.reshape(frame_count, key_count) > 0.5
    allowed = (in_window[None] & (key_live[:, None, :] | itself[None]))[:, None]
    scores = (
        jnp.einsum("fqhd,fkhd->fhqk", queries, keys_pad, preferred_element_type=jnp.float32)
        * score_scale
    )
    weights_b, totals = softmax_parts(scores, allowed)
    weighted = jnp.einsum(
        "fhqk,fkhd->fqhd", weights_b, values_pad, preferred_element_type=jnp.float32
    )
    spatial_heads = (weighted / jnp.transpose(totals, (0, 2, 1))[..., None]).astype(jnp.bfloat16)
    spatial_heads = spatial_heads.reshape(frame_count * tile_tokens, width)
    stream = resid.reshape(frame_count * tile_tokens, width).astype(jnp.float32) + jnp.dot(
        spatial_heads, w_spatial_out, preferred_element_type=jnp.float32
    )
    average = jnp.mean(stream, -1, keepdims=True)
    centered = stream - average
    variance = jnp.mean(centered * centered, -1, keepdims=True)
    normed = (
        centered * lax.rsqrt(variance + EPSILON) * (1.0 + modulation[1]) + modulation[0]
    ).astype(jnp.bfloat16)
    tm_count = lax.axis_size("tm")
    part_tokens = tile_tokens // tm_count
    normed_parts = normed.reshape(frame_count, tm_count, part_tokens, width)
    gathered = lax.all_to_all(normed_parts, "tm", split_axis=1, concat_axis=0, tiled=True)
    frames_all, single, items, unused = gathered.shape
    projected = jnp.dot(
        gathered.reshape(frames_all * single * items, width),
        w_temporal_qkv,
        preferred_element_type=jnp.float32,
    ).astype(jnp.bfloat16)
    projected = projected.reshape(frames_all, single, items, 3 * width)
    result = lax.all_to_all(
        frame_attend(projected, HEADS), "tm", split_axis=0, concat_axis=1, tiled=True
    )
    return result.reshape(frame_count, tile_rows, tile_cols, width)


def iota(shape, dim):
    return lax.broadcasted_iota(jnp.int32, shape, dim)


def attend(tiles):
    width = tiles[0][0].shape[1]
    head = width // HEADS
    factor = head ** (-0.5) * math.log2(math.e)
    lane = iota((1, 2 * LANES), 1)
    spans = []
    for pair in range(HEADS // 2):
        start = LANES * pair
        low = 2 * head * pair - start
        spans.append((slice(start, start + 2 * LANES), low, low + head, low + 2 * head))
    scores = []
    for queries, keys, values, bias in tiles:
        for span, low, mid, high in spans:
            first = jnp.where((lane >= low) & (lane < mid), queries[:, span], 0.0)
            second = jnp.where((lane >= mid) & (lane < high), queries[:, span], 0.0)
            both = jnp.concatenate([first, second], axis=0).astype(jnp.bfloat16)
            scores.append(
                lax.dot_general(
                    both, keys[:, span], (((1,), (1,)), ((), ())), preferred_element_type=jnp.float32
                )
            )
    weights = []
    for index, (queries, keys, values, bias) in enumerate(tiles):
        bias_two = jnp.concatenate([bias, bias], axis=0)
        for pair in range(len(spans)):
            score = scores[index * len(spans) + pair] + bias_two
            top = jnp.max(score, -1, keepdims=True)
            weight = jnp.exp2((score - top) * factor)
            weights.append((weight.astype(jnp.bfloat16), 1.0 / jnp.sum(weight, -1, keepdims=True)))
    results = []
    edge_lane = iota((1, LANES), 1)
    for index, (queries, keys, values, bias) in enumerate(tiles):
        count = queries.shape[0]
        pairs = []
        for pair, (span, low, mid, high) in enumerate(spans):
            weight, inverse = weights[index * len(spans) + pair]
            mixed = jnp.dot(weight, values[:, span], preferred_element_type=jnp.float32) * inverse
            pairs.append(jnp.where(lane < mid, mixed[:count], mixed[count:]))
        blocks = [pairs[0][:, :LANES]]
        for pair in range(1, len(spans)):
            cut = spans[pair][1]
            blocks.append(jnp.where(edge_lane < cut, pairs[pair - 1][:, LANES:], pairs[pair][:, :LANES]))
        blocks.append(pairs[-1][:, LANES:])
        results.append(jnp.concatenate(blocks, axis=1))
    return results


def keep_row(count, keep):
    picker = jnp.where(iota((count, LANES), 1) == 0, 1.0, 0.0).astype(jnp.bfloat16)
    return lax.dot_general(
        picker, keep, (((1,), (1,)), ((), ())), preferred_element_type=jnp.float32
    )


def make_bias(q_row, q_col, k_row, k_col, keep):
    row_gap, col_gap = k_row - q_row, k_col - q_col
    near = (jnp.abs(row_gap) <= RADIUS) & (jnp.abs(col_gap) <= RADIUS)
    itself = (row_gap == 0) & (col_gap == 0)
    return jnp.where(near & ((keep > 0.5) | itself), 0.0, NEG_FILL)


def strip_bias(rows, keep, strips=1):
    columns, key_columns = strips * STRIP, (strips + 1) * STRIP
    count, keys = rows * columns, (rows + 2 * RADIUS) * key_columns
    q, k = iota((count, keys), 0), iota((count, keys), 1)
    return make_bias(
        q // columns + RADIUS, q % columns + EDGE, k // key_columns, k % key_columns, keep_row(count, keep)
    )


def finish(heads, resid, w_out, modulation):
    return adapt(resid + jnp.dot(heads, w_out, preferred_element_type=jnp.float32), modulation)


def adapt(stream, modulation):
    average = jnp.mean(stream, -1, keepdims=True)
    centered = stream - average
    variance = jnp.mean(centered * centered, -1, keepdims=True)
    scaled = centered * lax.rsqrt(variance + EPSILON)
    return (scaled * (1.0 + modulation[1:2]) + modulation[0:1]).astype(jnp.bfloat16)


def wide(ref, plane, rows, strip, strips=1):
    found = ref[plane, rows, pl.ds(STRIP * strip, (strips + 1) * STRIP), :].astype(jnp.float32)
    return found.reshape(found.shape[0] * found.shape[1], found.shape[2])


def window(ref, plane, rows, strip):
    return wide(ref, plane, rows, strip).astype(jnp.bfloat16)


def middle(ref, plane, rows, strip, strips=1):
    found = ref[plane, rows, pl.ds(STRIP * strip, (strips + 1) * STRIP), :].astype(jnp.float32)
    found = found[:, EDGE : EDGE + strips * STRIP]
    return found.reshape(found.shape[0] * found.shape[1], found.shape[2])


INNER_ROWS = 6
INNER_BATCH = 4
RIM_BATCH = 4
RIM_STRIPS = 2
EDGE_BATCH = 3


def batched(tiles, size):
    found = []
    for start in range(0, len(tiles), size):
        found += attend(tiles[start : start + size])
    return found


def inner_kernel(qkv, keep, resid_hbm, w_hbm, modulation, out, resid, w_out, heads, arrived):
    copies = [
        pltpu.make_async_copy(w_hbm, w_out, arrived.at[0]),
        pltpu.make_async_copy(resid_hbm, resid, arrived.at[1]),
    ]
    for copy in copies:
        copy.start()
    tile_rows, tile_cols, width = resid.shape[1:]
    rows = tile_rows - 2 * RADIUS
    strips = tile_cols // STRIP - 1
    every = pl.ds(0, tile_rows)
    mine = pl.ds(RADIUS, rows)
    step = INNER_ROWS
    tiles = []
    for strip in range(strips):
        queries = middle(qkv, 0, mine, strip)
        keys, values, flags = (window(ref, plane, every, strip) for ref, plane in ((qkv, 1), (qkv, 2), (keep, 0)))
        for start in range(0, rows, step):
            span = slice(start * 2 * STRIP, (start + step + 2 * RADIUS) * 2 * STRIP)
            tiles.append(
                (
                    queries[start * STRIP : (start + step) * STRIP],
                    keys[span],
                    values[span],
                    strip_bias(step, flags[span]),
                )
            )
    mixed = batched(tiles, INNER_BATCH * rows // step)
    heads[...] = jnp.concatenate(mixed, axis=0).astype(jnp.bfloat16)
    copies[0].wait()
    product = jnp.dot(heads[...], w_out[...], preferred_element_type=jnp.float32)
    copies[1].wait()
    source = jnp.concatenate([middle(resid, 0, mine, strip) for strip in range(strips)], axis=0)
    out[...] = adapt(source + product, modulation[...]).reshape(out.shape)


def rim_kernel(qkv, keep, halo, resid, w_out, modulation, out, heads):
    tile_rows, tile_cols, width = resid.shape[1:]
    strips = tile_cols // STRIP - 1
    near = 2 * RADIUS
    tiles = []
    sources = []
    for strip in range(0, strips, RIM_STRIPS):
        for side in range(2):
            inner = pl.ds(0 if side == 0 else tile_rows - near, near)
            mine = pl.ds(0 if side == 0 else tile_rows - RADIUS, RADIUS)
            far = wide(halo, side, pl.ds(0, RADIUS), strip, RIM_STRIPS)
            joined = []
            for at, (ref, plane) in zip((0, width, 2 * width), ((qkv, 1), (qkv, 2), (keep, 0))):
                local = wide(ref, plane, inner, strip, RIM_STRIPS)
                piece = far[:, at : at + local.shape[1]]
                both = jnp.concatenate([piece, local] if side == 0 else [local, piece], axis=0)
                joined.append(both.astype(jnp.bfloat16))
            bias = strip_bias(RADIUS, joined[2], RIM_STRIPS)
            tiles.append((middle(qkv, 0, mine, strip, RIM_STRIPS), joined[0], joined[1], bias))
            sources.append(middle(resid, 0, mine, strip, RIM_STRIPS))
    heads[...] = jnp.concatenate(batched(tiles, RIM_BATCH), axis=0).astype(jnp.bfloat16)
    out[...] = finish(heads[...], jnp.concatenate(sources, axis=0), w_out[...], modulation[...]).reshape(out.shape)


def load_kernel(odd, qkv_hbm, keep_hbm, one, two, qkv, keep, flags, packed, arrived):
    tile_rows, tile_cols, width = qkv.shape[1:]
    last = tile_rows - RADIUS
    starts = (jnp.where(odd[0] == 1, 0, last), jnp.where(odd[0] == 1, last, 0))
    copies = [pltpu.make_async_copy(keep_hbm, flags, arrived.at[0])]
    for out, start in zip((two, one), starts[::-1]):
        for plane in (1, 2):
            copies.append(
                pltpu.make_async_copy(
                    qkv_hbm.at[plane, pl.ds(start, RADIUS)],
                    out.at[0, :, :, pl.ds((plane - 1) * width, width)],
                    arrived.at[len(copies)],
                )
            )
    copies.append(pltpu.make_async_copy(qkv_hbm, qkv, arrived.at[len(copies)]))
    for copy in copies:
        copy.start()
    copies[0].wait()
    packed[...] = jnp.zeros_like(packed)
    for row in range(tile_rows):
        packed[row : row + 1, :tile_cols] = flags[row].astype(jnp.float32)
    turned = packed[...].T
    for row in range(tile_rows):
        column = jnp.broadcast_to(turned[:tile_cols, row : row + 1], (tile_cols, LANES))
        keep[0, row] = column.astype(jnp.bfloat16)
    for out, start in zip((one, two), starts):
        out[0, :, :, 2 * width :] = keep[0, pl.ds(start, RADIUS)]
    for copy in copies[1:]:
        copy.wait()


def pack_columns(odd, sources, one, two):
    even = odd[1] == 0
    for ref, plane, rows, lane in sources:
        tile_cols, lanes = ref.shape[-2:]
        head = ref[plane, :, 0:STRIP, :].astype(jnp.float32)[:, :RADIUS]
        tail = ref[plane, :, tile_cols - STRIP : tile_cols, :].astype(jnp.float32)[:, STRIP - RADIUS :]
        one[rows, :, lane : lane + lanes] = jnp.where(even, tail, head).astype(jnp.bfloat16)
        two[rows, :, lane : lane + lanes] = jnp.where(even, head, tail).astype(jnp.bfloat16)


def own_kernel(odd, normed, w_qkv, qkv, keep, out, one, two):
    tile_rows, tile_cols, width = qkv.shape[1:]
    rows = slice(0, tile_rows)
    pack_columns(odd, ((qkv, 1, rows, 0), (qkv, 2, rows, width), (keep, 0, rows, 2 * width)), one, two)
    out[...] = jnp.dot(normed[...], w_qkv[...], preferred_element_type=jnp.float32).astype(jnp.bfloat16)


def columns_kernel(odd, first, second, one_body, two_body, one, two, halo):
    tile_rows = one_body.shape[0]
    for above in (0, 1):

        @pl.when(odd[0] == 1 - above)
        def _():
            halo[above : above + 1] = first[...]
            halo[1 - above : 2 - above] = second[...]

    body = slice(RADIUS, RADIUS + tile_rows)
    one[0, body] = one_body[...]
    two[0, body] = two_body[...]
    top, bottom = slice(0, RADIUS), slice(RADIUS + tile_rows, 2 * RADIUS + tile_rows)
    pack_columns(odd, ((halo, 0, top, 0), (halo, 1, bottom, 0)), one.at[0], two.at[0])


def edge_columns(ref, plane, row):
    found = ref[plane, row].astype(jnp.float32)
    return found[:STRIP], found[found.shape[0] - STRIP :]


def edge_kernel(odd, qkv, keep, halo, side_one, side_two, resid, w_out, modulation, after, out, heads, far, ends, mine):
    tile_rows, tile_cols, width = resid.shape[1:]
    pad_rows = tile_rows + 2 * RADIUS
    far[:, 2 * STRIP :, :] = jnp.zeros((pad_rows, STRIP, far.shape[2]), jnp.float32)
    for row in range(pad_rows):
        local = row - RADIUS
        if 0 <= local < tile_rows:
            sources = ((qkv, 1, local, 0, width), (qkv, 2, local, width, width), (keep, 0, local, 2 * width, LANES))
        elif local < 0:
            sources = ((halo, 0, row, 0, 2 * width + LANES),)
        else:
            sources = ((halo, 1, local - tile_rows, 0, 2 * width + LANES),)
        for ref, plane, at, lane, lanes in sources:
            head, tail = edge_columns(ref, plane, at)
            far[row, 0:STRIP, lane : lane + lanes] = head
            far[row, STRIP : 2 * STRIP, lane : lane + lanes] = tail
        far[row, 2 * STRIP : 2 * STRIP + RADIUS, :] = side_one[0, row].astype(jnp.float32)
        far[row, 2 * STRIP + RADIUS : 2 * STRIP + 2 * RADIUS, :] = side_two[0, row].astype(jnp.float32)
    one_left = odd[1] == 1
    one_col = jnp.where(one_left, -RADIUS, tile_cols)
    two_col = jnp.where(one_left, tile_cols, -RADIUS)
    for row in range(tile_rows):
        for ref, plane, target in ((qkv, 0, ends), (resid, 0, mine)):
            head, tail = edge_columns(ref, plane, row)
            target[row, 0:EDGE] = head[:EDGE]
            target[row, EDGE:STRIP] = tail[EDGE:]
    rows = 4
    span = 3 * STRIP
    tiles = []
    for start in range(0, tile_rows, rows):
        count, keys = rows * STRIP, (rows + 2 * RADIUS) * span
        found = far[start : start + rows + 2 * RADIUS].reshape(keys, 2 * width + LANES).astype(jnp.bfloat16)
        q, k = iota((count, keys), 0), iota((count, keys), 1)
        q_col = q % STRIP
        q_col = jnp.where(q_col < EDGE, q_col, q_col + tile_cols - STRIP)
        k_col = k % span
        k_col = jnp.where(
            k_col < STRIP,
            k_col,
            jnp.where(
                k_col < 2 * STRIP,
                k_col + tile_cols - 2 * STRIP,
                jnp.where(
                    k_col < 2 * STRIP + RADIUS,
                    k_col - 2 * STRIP + one_col,
                    jnp.where(
                        k_col < 2 * STRIP + 2 * RADIUS,
                        k_col - 2 * STRIP - RADIUS + two_col,
                        -100 * tile_cols,
                    ),
                ),
            ),
        )
        bias = make_bias(
            q // STRIP + RADIUS, q_col, k // span, k_col, keep_row(count, found[:, 2 * width :])
        )
        tiles.append(
            (ends[start : start + rows].reshape(count, width), found[:, :width], found[:, width : 2 * width], bias)
        )
    mixed = batched(tiles, EDGE_BATCH)
    source = mine[...].reshape(tile_rows * STRIP, width)
    heads[...] = jnp.concatenate(mixed, axis=0).astype(jnp.bfloat16)
    out[...] = finish(heads[...], source, w_out[...], modulation[...])


def head_marks(width):
    feature, lane = np.arange(width)[:, None], np.arange(LANES)[None, :]
    return jnp.asarray(feature // (width // HEADS) == lane % HEADS, jnp.bfloat16)


def mark_heads(width):
    row, feature = np.arange(LANES)[:, None], np.arange(width)[None, :]
    return jnp.asarray((feature // (width // HEADS) == row % HEADS) & (row < 2 * HEADS), jnp.bfloat16)


def halves_of(values):
    high = values.astype(jnp.bfloat16)
    low = (values - high.astype(jnp.float32)).astype(jnp.bfloat16)
    return high, low


def temporal(own, other_key, other_value, marks, spread):
    width = other_key.shape[1]
    scale = (width // HEADS) ** (-0.5)
    lane = iota((1, LANES), 1)
    key_gap = other_key.astype(jnp.float32) - own[:, width : 2 * width].astype(jnp.float32)
    high, low = halves_of(own[:, :width].astype(jnp.float32) * key_gap)
    gap = (
        jnp.dot(high, marks, preferred_element_type=jnp.float32)
        + jnp.dot(low, marks, preferred_element_type=jnp.float32)
    ) * scale
    own_weight = jnp.exp(jnp.minimum(-gap, 0.0))
    other_weight = jnp.exp(jnp.minimum(gap, 0.0))
    inverse = 1.0 / (own_weight + other_weight)

    def share(weight):
        part = weight.astype(jnp.bfloat16).astype(jnp.float32) * inverse
        high, low = halves_of(part)
        packed = jnp.where(lane < HEADS, high.astype(jnp.float32), low.astype(jnp.float32)).astype(jnp.bfloat16)
        return jnp.dot(packed, spread, preferred_element_type=jnp.float32)

    return share(own_weight) * own[:, 2 * width :].astype(jnp.float32) + share(other_weight) * other_value.astype(
        jnp.float32
    )


def place(pieces, ready, ends, mixed):
    rows, tile_cols, width = mixed.shape
    for row, column, source, start, count in pieces:
        mixed[row, column : column + count] = source[start : start + count, :].astype(jnp.float32)
    mixed[:, 0:EDGE] = jnp.zeros((rows, EDGE, width), jnp.float32)
    mixed[:, tile_cols - EDGE :] = jnp.zeros((rows, EDGE, width), jnp.float32)
    ready[...] = mixed[...].astype(jnp.bfloat16)
    ends[:, 0:STRIP] = mixed[:, 0:STRIP]
    ends[:, STRIP:] = mixed[:, tile_cols - STRIP :]


def attend_frames(own, other, w_qkv, marks, spread):
    width = other.shape[1]
    pairs = jnp.dot(other[...], w_qkv[:, width:], preferred_element_type=jnp.float32).astype(jnp.bfloat16)
    return temporal(own[...], pairs[:, :width], pairs[:, width:], marks[...], spread[...])


def late_own_kernel(rim, edge, w_qkv, rim_own, edge_own):
    both = jnp.concatenate([rim[...], edge[...]], axis=0)
    found = jnp.dot(both, w_qkv[...], preferred_element_type=jnp.float32).astype(jnp.bfloat16)
    rim_own[...] = found[: rim.shape[0]]
    edge_own[...] = found[rim.shape[0] :]


def inner_done_kernel(own, other, w_qkv, marks, spread, after, ready, ends, done, mixed):
    rows, tile_cols, width = mixed.shape
    done[...] = attend_frames(own, other, w_qkv, marks, spread)
    pieces = []
    for row in range(rows):
        for strip in range(tile_cols // STRIP - 1):
            pieces.append((row, EDGE + STRIP * strip, done, (strip * rows + row) * STRIP, STRIP))
    place(pieces, ready, ends, mixed)


def rim_done_kernel(own, other, w_qkv, marks, spread, ready, ends, done, mixed):
    rows, tile_cols, width = mixed.shape
    done[...] = attend_frames(own, other, w_qkv, marks, spread)
    columns = RIM_STRIPS * STRIP
    pieces = []
    for row in range(rows):
        for part in range((tile_cols // STRIP - 1) // RIM_STRIPS):
            pieces.append((row, EDGE + columns * part, done, (part * rows + row) * columns, columns))
    place(pieces, ready, ends, mixed)


def last_kernel(own, other, w_qkv, marks, spread, inner, inner_ends, rim, rim_ends, out, left, right, arrived):
    tile_rows, tile_cols, width = out.shape[1:]
    low, high = RADIUS, tile_rows - RADIUS
    parts = (
        (slice(0, low), rim, rim_ends, slice(0, RADIUS)),
        (slice(low, high), inner, inner_ends, slice(0, high - low)),
        (slice(high, tile_rows), rim, rim_ends, slice(RADIUS, 2 * RADIUS)),
    )
    whole = []
    for target, ready, ends, rows in parts:
        size = rows.stop - rows.start
        copy = pltpu.make_async_copy(
            ready.at[pl.ds(rows.start, size), pl.ds(STRIP, tile_cols - 2 * STRIP)],
            out.at[0, pl.ds(target.start, size), pl.ds(STRIP, tile_cols - 2 * STRIP)],
            arrived.at[len(whole)],
        )
        copy.start()
        whole.append(copy)
    edge = attend_frames(own, other, w_qkv, marks, spread)
    edge = edge.reshape(tile_rows, STRIP, width)
    early = iota((1, STRIP, 1), 1) < EDGE
    for target, ready, ends, rows in parts:
        left[target] = jnp.where(early, edge[target], ends[rows, :STRIP]).astype(jnp.bfloat16)
        right[target] = jnp.where(early, ends[rows, STRIP:], edge[target]).astype(jnp.bfloat16)
    copies = [
        pltpu.make_async_copy(left, out.at[0, :, pl.ds(0, STRIP)], arrived.at[3]),
        pltpu.make_async_copy(right, out.at[0, :, pl.ds(tile_cols - STRIP, STRIP)], arrived.at[4]),
    ]
    for copy in copies:
        copy.start()
    for copy in whole + copies:
        copy.wait()


def call(body, out_shape, operands, scratch=(), flops=0, limit=24, specs=(), out_spec=VMEM):
    in_specs = [VMEM] * len(operands)
    for index, spec in specs:
        in_specs[index] = spec
    return pl.pallas_call(
        body,
        out_shape=out_shape,
        in_specs=in_specs,
        out_specs=[VMEM] * len(out_shape) if isinstance(out_shape, list) else out_spec,
        scratch_shapes=list(scratch),
        cost_estimate=pl.CostEstimate(flops=flops, bytes_accessed=0, transcendentals=0),
        compiler_params=pltpu.CompilerParams(vmem_limit_bytes=limit * MIB),
        name=body.__name__,
    )(*operands)


def exchanges(count):
    found = []
    for start in (0, 1):
        pairs = [(i, i + 1) for i in range(start, count - 1, 2)]
        found.append(pairs + [(j, i) for i, j in pairs])
    return found


def fast_device(resid, spatial_qkv, key_keep, w_spatial_out, modulation, w_temporal_qkv):
    frame_count, tile_rows, tile_cols, width = resid.shape
    strips = tile_cols // STRIP - 1
    odd = jnp.stack([lax.axis_index("row") % 2, lax.axis_index("col") % 2]).astype(jnp.int32)
    swap = [(0, 1), (1, 0)]
    bf16 = jnp.bfloat16
    struct = lambda *shape: jax.ShapeDtypeStruct(shape, bf16)
    held = lambda *shape: pltpu.VMEM(shape, bf16)
    stay = lambda x: pltpu.with_memory_space_constraint(x, pltpu.HBM)
    smem = pl.BlockSpec(memory_space=pltpu.SMEM)
    hbm = pl.BlockSpec(memory_space=pltpu.HBM)
    anywhere = pl.BlockSpec(memory_space=pl.ANY)
    marks, spread = head_marks(width), mark_heads(width)
    lanes = 2 * width + LANES
    pad_rows = tile_rows + 2 * RADIUS
    edge_count = tile_rows * STRIP

    one, two, qkv, keep = call(
        load_kernel,
        [struct(1, RADIUS, tile_cols, lanes)] * 2
        + [held(3, tile_rows, tile_cols, width), held(1, tile_rows, tile_cols, LANES)],
        (odd, stay(spatial_qkv[:, 0]), stay(key_keep.reshape(tile_rows, 1, tile_cols))),
        [
            pltpu.VMEM((tile_rows, 1, tile_cols), jnp.int32),
            pltpu.VMEM((LANES, LANES), jnp.float32),
            pltpu.SemaphoreType.DMA((6,)),
        ],
        specs=[(0, smem), (1, hbm), (2, hbm)],
    )
    pairs_one, pairs_two = exchanges(lax.axis_size("row"))
    first = lax.ppermute(one, "row", pairs_one)
    second = lax.ppermute(two, "row", pairs_two)

    inner_count = strips * (tile_rows - 2 * RADIUS) * STRIP
    inner, resid, w_spatial_out = call(
        inner_kernel,
        [struct(inner_count, width), held(*resid.shape), held(width, width)],
        (qkv, keep, stay(resid), stay(w_spatial_out), modulation),
        [held(inner_count, width), pltpu.SemaphoreType.DMA((2,))],
        specs=[(2, hbm), (3, hbm)],
    )
    inner_other = lax.ppermute(inner, "tm", swap)
    inner_own, one_body, two_body = call(
        own_kernel,
        [struct(inner_count, 3 * width)] + [held(tile_rows, RADIUS, lanes)] * 2,
        (odd, inner, w_temporal_qkv, qkv, keep),
        specs=[(0, smem)],
    )

    one, two, halo = call(
        columns_kernel,
        [struct(1, pad_rows, RADIUS, lanes)] * 2 + [held(2, RADIUS, tile_cols, lanes)],
        (odd, first, second, one_body, two_body),
        specs=[(0, smem)],
    )
    pairs_one, pairs_two = exchanges(lax.axis_size("col"))
    side_one = lax.ppermute(one, "col", pairs_one)
    side_two = lax.ppermute(two, "col", pairs_two)

    rim_count = strips * 2 * RADIUS * STRIP
    rim = call(
        rim_kernel,
        struct(rim_count, width),
        (qkv, keep, halo, resid, w_spatial_out, modulation),
        [held(rim_count, width)],
    )
    rim_other = lax.ppermute(rim, "tm", swap)

    def rows_of(count):
        whole, ends = (count, tile_cols, width), (count, 2 * STRIP, width)
        return [held(*whole), pltpu.VMEM(ends, jnp.float32)], pltpu.VMEM(whole, jnp.float32)

    shapes, scratch = rows_of(tile_rows - 2 * RADIUS)
    inner_ready, inner_ends = call(
        inner_done_kernel,
        shapes,
        (inner_own, inner_other, w_temporal_qkv, marks, spread, rim),
        [pltpu.VMEM((inner_count, width), jnp.float32), scratch],
        specs=[(5, anywhere)],
    )

    edge = call(
        edge_kernel,
        struct(edge_count, width),
        (odd, qkv, keep, halo, side_one, side_two, resid, w_spatial_out, modulation, inner_ready),
        [
            held(edge_count, width),
            pltpu.VMEM((pad_rows, 3 * STRIP, lanes), jnp.float32),
            pltpu.VMEM((tile_rows, STRIP, width), jnp.float32),
            pltpu.VMEM((tile_rows, STRIP, width), jnp.float32),
        ],
        specs=[(0, smem), (9, anywhere)],
    )
    edge_other = lax.ppermute(edge, "tm", swap)

    rim_own, edge_own = call(
        late_own_kernel,
        [struct(rim_count, 3 * width), struct(edge_count, 3 * width)],
        (rim, edge, w_temporal_qkv),
    )
    shapes, scratch = rows_of(2 * RADIUS)
    rim_ready, rim_ends = call(
        rim_done_kernel,
        shapes,
        (rim_own, rim_other, w_temporal_qkv, marks, spread),
        [pltpu.VMEM((rim_count, width), jnp.float32), scratch],
    )
    return call(
        last_kernel,
        struct(frame_count, tile_rows, tile_cols, width),
        (edge_own, edge_other, w_temporal_qkv, marks, spread, inner_ready, inner_ends, rim_ready, rim_ends),
        [
            held(tile_rows, STRIP, width),
            held(tile_rows, STRIP, width),
            pltpu.SemaphoreType.DMA((5,)),
        ],
        out_spec=hbm,
    )


def per_device(resid, *rest):
    frame_count, tile_rows, tile_cols, width = resid.shape
    fits = (
        frame_count == 1
        and lax.axis_size("tm") == 2
        and width == 9 * LANES
        and (tile_cols // STRIP - 1) % RIM_STRIPS == 0
        and tile_cols % STRIP == 0
        and tile_cols >= 2 * STRIP
        and tile_rows % 4 == 0
        and tile_rows > 2 * RADIUS
    )
    return (fast_device if fits else general_device)(resid, *rest)


def solution(mesh):
    return jax.shard_map(
        per_device,
        mesh=mesh,
        in_specs=(
            P("tm", "row", "col", None),
            P(None, "tm", "row", "col", None),
            P("tm", "row", "col"),
            P(),
            P(),
            P(),
        ),
        out_specs=P("tm", "row", "col", None),
        check_vma=False,
    )
```

```python
import functools
import math

import jax
import jax.numpy as jnp
import numpy as np
from jax import lax
from jax.experimental import pallas as pl
from jax.experimental.pallas import tpu as pltpu
from jax.sharding import PartitionSpec as P

HEADS = 16
RADIUS = 3


NEG_FILL = -1e30
EPSILON = 1e-06

LANES = 128
STRIP = 8
EDGE = STRIP // 2
MIB = 1024 * 1024
VMEM = pl.BlockSpec(memory_space=pltpu.VMEM)


def extended(array, sides, width):
    for axis, dim in sides:
        count, length = (lax.axis_size(axis), array.shape[dim])
        up = [(i, (i + 1) % count) for i in range(count - 1)]
        down = [(j, i) for i, j in up]
        last = lax.slice_in_dim(array, length - width, length, axis=dim)
        leading = lax.slice_in_dim(array, 0, width, axis=dim)
        before = lax.ppermute(last, axis, up)
        after = lax.ppermute(leading, axis, down)
        array = jnp.concatenate([before, array, after], axis=dim)
    return array


def softmax_parts(scores, allowed):
    masked = jnp.where(allowed, scores, NEG_FILL)
    top_score = jnp.max(masked, -1, keepdims=True)
    weights_f = jnp.where(allowed, jnp.exp(masked - top_score), 0.0)
    return (weights_f.astype(jnp.bfloat16), jnp.sum(weights_f, -1))


def frame_attend(gathered, head_count):
    frames_all, single, items, width_three = gathered.shape
    width = width_three // 3
    head_size = width // head_count
    split_qkv = gathered.reshape(frames_all, items, 3, head_count, head_size)
    scores = jnp.einsum(
        "fphd,gphd->phfg",
        split_qkv[:, :, 0],
        split_qkv[:, :, 1],
        preferred_element_type=jnp.float32,
    ) * head_size ** (-0.5)
    weights_b, totals = softmax_parts(scores, True)
    weighted = jnp.einsum(
        "phfg,gphd->fphd", weights_b, split_qkv[:, :, 2], preferred_element_type=jnp.float32
    )
    result = weighted / jnp.transpose(totals, (2, 0, 1))[..., None]
    return result.astype(jnp.bfloat16).reshape(frames_all, single, items, width)


def general_device(resid, spatial_qkv, key_keep, w_spatial_out, modulation, w_temporal_qkv):
    frame_count, tile_rows, tile_cols, width = resid.shape
    head_size = width // HEADS
    score_scale = head_size ** (-0.5)
    tile_tokens = tile_rows * tile_cols
    pair = spatial_qkv[1:3]
    keep_flags = key_keep.astype(jnp.bfloat16)[None, :, :, :, None]
    padded_pair, padded_keep = (
        extended(pair, (("row", 2), ("col", 3)), RADIUS),
        extended(keep_flags, (("row", 2), ("col", 3)), RADIUS),
    )
    pad_rows = tile_rows + 2 * RADIUS
    pad_cols = tile_cols + 2 * RADIUS
    key_count = pad_rows * pad_cols
    queries = spatial_qkv[0].reshape(frame_count, tile_tokens, HEADS, head_size)
    keys_pad = padded_pair[0].reshape(frame_count, key_count, HEADS, head_size)
    values_pad = padded_pair[1].reshape(frame_count, key_count, HEADS, head_size)
    query_index = jnp.arange(tile_tokens)
    query_row = query_index // tile_cols
    query_col = query_index % tile_cols
    key_index = jnp.arange(key_count)
    key_row = key_index // pad_cols
    key_col = key_index % pad_cols
    row_gap = key_row[None, :] - query_row[:, None] - RADIUS
    col_gap = key_col[None, :] - query_col[:, None] - RADIUS
    in_window = (jnp.abs(row_gap) <= RADIUS) & (jnp.abs(col_gap) <= RADIUS)
    itself = (row_gap == 0) & (col_gap == 0)
    key_live = padded_keep.reshape(frame_count, key_count) > 0.5
    allowed = (in_window[None] & (key_live[:, None, :] | itself[None]))[:, None]
    scores = (
        jnp.einsum("fqhd,fkhd->fhqk", queries, keys_pad, preferred_element_type=jnp.float32)
        * score_scale
    )
    weights_b, totals = softmax_parts(scores, allowed)
    weighted = jnp.einsum(
        "fhqk,fkhd->fqhd", weights_b, values_pad, preferred_element_type=jnp.float32
    )
    spatial_heads = (weighted / jnp.transpose(totals, (0, 2, 1))[..., None]).astype(jnp.bfloat16)
    spatial_heads = spatial_heads.reshape(frame_count * tile_tokens, width)
    stream = resid.reshape(frame_count * tile_tokens, width).astype(jnp.float32) + jnp.dot(
        spatial_heads, w_spatial_out, preferred_element_type=jnp.float32
    )
    average = jnp.mean(stream, -1, keepdims=True)
    centered = stream - average
    variance = jnp.mean(centered * centered, -1, keepdims=True)
    normed = (
        centered * lax.rsqrt(variance + EPSILON) * (1.0 + modulation[1]) + modulation[0]
    ).astype(jnp.bfloat16)
    tm_count = lax.axis_size("tm")
    part_tokens = tile_tokens // tm_count
    normed_parts = normed.reshape(frame_count, tm_count, part_tokens, width)
    gathered = lax.all_to_all(normed_parts, "tm", split_axis=1, concat_axis=0, tiled=True)
    frames_all, single, items, unused = gathered.shape
    projected = jnp.dot(
        gathered.reshape(frames_all * single * items, width),
        w_temporal_qkv,
        preferred_element_type=jnp.float32,
    ).astype(jnp.bfloat16)
    projected = projected.reshape(frames_all, single, items, 3 * width)
    result = lax.all_to_all(
        frame_attend(projected, HEADS), "tm", split_axis=0, concat_axis=1, tiled=True
    )
    return result.reshape(frame_count, tile_rows, tile_cols, width)


def iota(shape, dim):
    return lax.broadcasted_iota(jnp.int32, shape, dim)


def attend(tiles):
    width = tiles[0][0].shape[1]
    head = width // HEADS
    factor = head ** (-0.5) * math.log2(math.e)
    lane = iota((1, 2 * LANES), 1)
    spans = []
    for pair in range(HEADS // 2):
        start = LANES * pair
        low = 2 * head * pair - start
        spans.append((slice(start, start + 2 * LANES), low, low + head, low + 2 * head))
    scores = []
    for queries, keys, values, bias in tiles:
        for span, low, mid, high in spans:
            first = jnp.where((lane >= low) & (lane < mid), queries[:, span], 0.0)
            second = jnp.where((lane >= mid) & (lane < high), queries[:, span], 0.0)
            both = jnp.concatenate([first, second], axis=0).astype(jnp.bfloat16)
            scores.append(
                lax.dot_general(
                    both, keys[:, span], (((1,), (1,)), ((), ())), preferred_element_type=jnp.float32
                )
            )
    weights = []
    for index, (queries, keys, values, bias) in enumerate(tiles):
        bias_two = jnp.concatenate([bias, bias], axis=0)
        for pair in range(len(spans)):
            score = scores[index * len(spans) + pair] + bias_two
            top = jnp.max(score, -1, keepdims=True)
            weight = jnp.exp2((score - top) * factor)
            weights.append((weight.astype(jnp.bfloat16), 1.0 / jnp.sum(weight, -1, keepdims=True)))
    results = []
    edge_lane = iota((1, LANES), 1)
    for index, (queries, keys, values, bias) in enumerate(tiles):
        count = queries.shape[0]
        pairs = []
        for pair, (span, low, mid, high) in enumerate(spans):
            weight, inverse = weights[index * len(spans) + pair]
            mixed = jnp.dot(weight, values[:, span], preferred_element_type=jnp.float32) * inverse
            pairs.append(jnp.where(lane < mid, mixed[:count], mixed[count:]))
        blocks = [pairs[0][:, :LANES]]
        for pair in range(1, len(spans)):
            cut = spans[pair][1]
            blocks.append(jnp.where(edge_lane < cut, pairs[pair - 1][:, LANES:], pairs[pair][:, :LANES]))
        blocks.append(pairs[-1][:, LANES:])
        results.append(jnp.concatenate(blocks, axis=1))
    return results


def keep_row(count, keep):
    picker = jnp.where(iota((count, LANES), 1) == 0, 1.0, 0.0).astype(jnp.bfloat16)
    return lax.dot_general(
        picker, keep, (((1,), (1,)), ((), ())), preferred_element_type=jnp.float32
    )


def make_bias(q_row, q_col, k_row, k_col, keep):
    row_gap, col_gap = k_row - q_row, k_col - q_col
    near = (jnp.abs(row_gap) <= RADIUS) & (jnp.abs(col_gap) <= RADIUS)
    itself = (row_gap == 0) & (col_gap == 0)
    return jnp.where(near & ((keep > 0.5) | itself), 0.0, NEG_FILL)


def strip_bias(rows, keep, strips=1):
    columns, key_columns = strips * STRIP, (strips + 1) * STRIP
    count, keys = rows * columns, (rows + 2 * RADIUS) * key_columns
    q, k = iota((count, keys), 0), iota((count, keys), 1)
    return make_bias(
        q // columns + RADIUS, q % columns + EDGE, k // key_columns, k % key_columns, keep_row(count, keep)
    )


def finish(heads, resid, w_out, modulation):
    stream = resid + jnp.dot(heads, w_out, preferred_element_type=jnp.float32)
    average = jnp.mean(stream, -1, keepdims=True)
    centered = stream - average
    variance = jnp.mean(centered * centered, -1, keepdims=True)
    scaled = centered * lax.rsqrt(variance + EPSILON)
    return (scaled * (1.0 + modulation[1:2]) + modulation[0:1]).astype(jnp.bfloat16)


def wide(ref, plane, rows, strip, strips=1):
    found = ref[plane, rows, pl.ds(STRIP * strip, (strips + 1) * STRIP), :].astype(jnp.float32)
    return found.reshape(found.shape[0] * found.shape[1], found.shape[2])


def window(ref, plane, rows, strip):
    return wide(ref, plane, rows, strip).astype(jnp.bfloat16)


def middle(ref, plane, rows, strip, strips=1):
    found = ref[plane, rows, pl.ds(STRIP * strip, (strips + 1) * STRIP), :].astype(jnp.float32)
    found = found[:, EDGE : EDGE + strips * STRIP]
    return found.reshape(found.shape[0] * found.shape[1], found.shape[2])


INNER_ROWS = 6
INNER_BATCH = 2
RIM_BATCH = 4
RIM_STRIPS = 2
EDGE_BATCH = 3


def batched(tiles, size):
    found = []
    for start in range(0, len(tiles), size):
        found += attend(tiles[start : start + size])
    return found


def inner_kernel(qkv, keep, resid_hbm, w_hbm, modulation, out, resid, w_out, heads, arrived):
    copies = [
        pltpu.make_async_copy(resid_hbm, resid, arrived.at[0]),
        pltpu.make_async_copy(w_hbm, w_out, arrived.at[1]),
    ]
    for copy in copies:
        copy.start()
    tile_rows, tile_cols, width = resid.shape[1:]
    rows = tile_rows - 2 * RADIUS
    strips = tile_cols // STRIP - 1
    every = pl.ds(0, tile_rows)
    mine = pl.ds(RADIUS, rows)
    step = INNER_ROWS
    tiles = []
    for strip in range(strips):
        queries = middle(qkv, 0, mine, strip)
        keys, values, flags = (window(ref, plane, every, strip) for ref, plane in ((qkv, 1), (qkv, 2), (keep, 0)))
        for start in range(0, rows, step):
            span = slice(start * 2 * STRIP, (start + step + 2 * RADIUS) * 2 * STRIP)
            tiles.append(
                (
                    queries[start * STRIP : (start + step) * STRIP],
                    keys[span],
                    values[span],
                    strip_bias(step, flags[span]),
                )
            )
    mixed = batched(tiles, INNER_BATCH * rows // step)
    heads[...] = jnp.concatenate(mixed, axis=0).astype(jnp.bfloat16)
    for copy in copies:
        copy.wait()
    source = jnp.concatenate([middle(resid, 0, mine, strip) for strip in range(strips)], axis=0)
    out[...] = finish(heads[...], source, w_out[...], modulation[...]).reshape(out.shape)


def rim_kernel(qkv, keep, halo, resid, w_out, modulation, out, heads):
    tile_rows, tile_cols, width = resid.shape[1:]
    strips = tile_cols // STRIP - 1
    near = 2 * RADIUS
    tiles = []
    sources = []
    for strip in range(0, strips, RIM_STRIPS):
        for side in range(2):
            inner = pl.ds(0 if side == 0 else tile_rows - near, near)
            mine = pl.ds(0 if side == 0 else tile_rows - RADIUS, RADIUS)
            far = wide(halo, side, pl.ds(0, RADIUS), strip, RIM_STRIPS)
            joined = []
            for at, (ref, plane) in zip((0, width, 2 * width), ((qkv, 1), (qkv, 2), (keep, 0))):
                local = wide(ref, plane, inner, strip, RIM_STRIPS)
                piece = far[:, at : at + local.shape[1]]
                both = jnp.concatenate([piece, local] if side == 0 else [local, piece], axis=0)
                joined.append(both.astype(jnp.bfloat16))
            bias = strip_bias(RADIUS, joined[2], RIM_STRIPS)
            tiles.append((middle(qkv, 0, mine, strip, RIM_STRIPS), joined[0], joined[1], bias))
            sources.append(middle(resid, 0, mine, strip, RIM_STRIPS))
    heads[...] = jnp.concatenate(batched(tiles, RIM_BATCH), axis=0).astype(jnp.bfloat16)
    out[...] = finish(heads[...], jnp.concatenate(sources, axis=0), w_out[...], modulation[...]).reshape(out.shape)


def load_kernel(odd, qkv_hbm, keep_hbm, one, two, qkv, keep, flags, packed, arrived):
    tile_rows, tile_cols, width = qkv.shape[1:]
    last = tile_rows - RADIUS
    starts = (jnp.where(odd[0] == 1, 0, last), jnp.where(odd[0] == 1, last, 0))
    copies = [pltpu.make_async_copy(keep_hbm, flags, arrived.at[0])]
    for out, start in zip((two, one), starts[::-1]):
        for plane in (1, 2):
            copies.append(
                pltpu.make_async_copy(
                    qkv_hbm.at[plane, pl.ds(start, RADIUS)],
                    out.at[0, :, :, pl.ds((plane - 1) * width, width)],
                    arrived.at[len(copies)],
                )
            )
    copies.append(pltpu.make_async_copy(qkv_hbm, qkv, arrived.at[len(copies)]))
    for copy in copies:
        copy.start()
    copies[0].wait()
    packed[...] = jnp.zeros_like(packed)
    for row in range(tile_rows):
        packed[row : row + 1, :tile_cols] = flags[row].astype(jnp.float32)
    turned = packed[...].T
    for row in range(tile_rows):
        column = jnp.broadcast_to(turned[:tile_cols, row : row + 1], (tile_cols, LANES))
        keep[0, row] = column.astype(jnp.bfloat16)
    for out, start in zip((one, two), starts):
        out[0, :, :, 2 * width :] = keep[0, pl.ds(start, RADIUS)]
    for copy in copies[1:]:
        copy.wait()


def pack_columns(odd, sources, one, two):
    even = odd[1] == 0
    for ref, plane, rows, lane in sources:
        tile_cols, lanes = ref.shape[-2:]
        head = ref[plane, :, 0:STRIP, :].astype(jnp.float32)[:, :RADIUS]
        tail = ref[plane, :, tile_cols - STRIP : tile_cols, :].astype(jnp.float32)[:, STRIP - RADIUS :]
        one[rows, :, lane : lane + lanes] = jnp.where(even, tail, head).astype(jnp.bfloat16)
        two[rows, :, lane : lane + lanes] = jnp.where(even, head, tail).astype(jnp.bfloat16)


def own_kernel(odd, normed, w_qkv, qkv, keep, out, one, two):
    tile_rows, tile_cols, width = qkv.shape[1:]
    rows = slice(0, tile_rows)
    pack_columns(odd, ((qkv, 1, rows, 0), (qkv, 2, rows, width), (keep, 0, rows, 2 * width)), one, two)
    out[...] = jnp.dot(normed[...], w_qkv[...], preferred_element_type=jnp.float32).astype(jnp.bfloat16)


def columns_kernel(odd, first, second, one_body, two_body, one, two, halo):
    tile_rows = one_body.shape[0]
    for above in (0, 1):

        @pl.when(odd[0] == 1 - above)
        def _():
            halo[above : above + 1] = first[...]
            halo[1 - above : 2 - above] = second[...]

    body = slice(RADIUS, RADIUS + tile_rows)
    one[0, body] = one_body[...]
    two[0, body] = two_body[...]
    top, bottom = slice(0, RADIUS), slice(RADIUS + tile_rows, 2 * RADIUS + tile_rows)
    pack_columns(odd, ((halo, 0, top, 0), (halo, 1, bottom, 0)), one.at[0], two.at[0])


def edge_columns(ref, plane, row):
    found = ref[plane, row].astype(jnp.float32)
    return found[:STRIP], found[found.shape[0] - STRIP :]


def edge_kernel(odd, qkv, keep, halo, side_one, side_two, resid, w_out, modulation, after, out, heads, far, ends, mine):
    tile_rows, tile_cols, width = resid.shape[1:]
    pad_rows = tile_rows + 2 * RADIUS
    far[:, 2 * STRIP :, :] = jnp.zeros((pad_rows, STRIP, far.shape[2]), jnp.float32)
    for row in range(pad_rows):
        local = row - RADIUS
        if 0 <= local < tile_rows:
            sources = ((qkv, 1, local, 0, width), (qkv, 2, local, width, width), (keep, 0, local, 2 * width, LANES))
        elif local < 0:
            sources = ((halo, 0, row, 0, 2 * width + LANES),)
        else:
            sources = ((halo, 1, local - tile_rows, 0, 2 * width + LANES),)
        for ref, plane, at, lane, lanes in sources:
            head, tail = edge_columns(ref, plane, at)
            far[row, 0:STRIP, lane : lane + lanes] = head
            far[row, STRIP : 2 * STRIP, lane : lane + lanes] = tail
        far[row, 2 * STRIP : 2 * STRIP + RADIUS, :] = side_one[0, row].astype(jnp.float32)
        far[row, 2 * STRIP + RADIUS : 2 * STRIP + 2 * RADIUS, :] = side_two[0, row].astype(jnp.float32)
    one_left = odd[1] == 1
    one_col = jnp.where(one_left, -RADIUS, tile_cols)
    two_col = jnp.where(one_left, tile_cols, -RADIUS)
    for row in range(tile_rows):
        for ref, plane, target in ((qkv, 0, ends), (resid, 0, mine)):
            head, tail = edge_columns(ref, plane, row)
            target[row, 0:EDGE] = head[:EDGE]
            target[row, EDGE:STRIP] = tail[EDGE:]
    rows = 4
    span = 3 * STRIP
    tiles = []
    for start in range(0, tile_rows, rows):
        count, keys = rows * STRIP, (rows + 2 * RADIUS) * span
        found = far[start : start + rows + 2 * RADIUS].reshape(keys, 2 * width + LANES).astype(jnp.bfloat16)
        q, k = iota((count, keys), 0), iota((count, keys), 1)
        q_col = q % STRIP
        q_col = jnp.where(q_col < EDGE, q_col, q_col + tile_cols - STRIP)
        k_col = k % span
        k_col = jnp.where(
            k_col < STRIP,
            k_col,
            jnp.where(
                k_col < 2 * STRIP,
                k_col + tile_cols - 2 * STRIP,
                jnp.where(
                    k_col < 2 * STRIP + RADIUS,
                    k_col - 2 * STRIP + one_col,
                    jnp.where(
                        k_col < 2 * STRIP + 2 * RADIUS,
                        k_col - 2 * STRIP - RADIUS + two_col,
                        -100 * tile_cols,
                    ),
                ),
            ),
        )
        bias = make_bias(
            q // STRIP + RADIUS, q_col, k // span, k_col, keep_row(count, found[:, 2 * width :])
        )
        tiles.append(
            (ends[start : start + rows].reshape(count, width), found[:, :width], found[:, width : 2 * width], bias)
        )
    mixed = batched(tiles, EDGE_BATCH)
    source = mine[...].reshape(tile_rows * STRIP, width)
    heads[...] = jnp.concatenate(mixed, axis=0).astype(jnp.bfloat16)
    out[...] = finish(heads[...], source, w_out[...], modulation[...])


def head_marks(width):
    feature, lane = np.arange(width)[:, None], np.arange(LANES)[None, :]
    return jnp.asarray(feature // (width // HEADS) == lane % HEADS, jnp.bfloat16)


def mark_heads(width):
    row, feature = np.arange(LANES)[:, None], np.arange(width)[None, :]
    return jnp.asarray((feature // (width // HEADS) == row % HEADS) & (row < 2 * HEADS), jnp.bfloat16)


def halves_of(values):
    high = values.astype(jnp.bfloat16)
    low = (values - high.astype(jnp.float32)).astype(jnp.bfloat16)
    return high, low


def temporal(own, other_key, other_value, marks, spread):
    width = other_key.shape[1]
    scale = (width // HEADS) ** (-0.5)
    lane = iota((1, LANES), 1)
    key_gap = other_key.astype(jnp.float32) - own[:, width : 2 * width].astype(jnp.float32)
    high, low = halves_of(own[:, :width].astype(jnp.float32) * key_gap)
    gap = (
        jnp.dot(high, marks, preferred_element_type=jnp.float32)
        + jnp.dot(low, marks, preferred_element_type=jnp.float32)
    ) * scale
    own_weight = jnp.exp(jnp.minimum(-gap, 0.0))
    other_weight = jnp.exp(jnp.minimum(gap, 0.0))
    inverse = 1.0 / (own_weight + other_weight)

    def share(weight):
        part = weight.astype(jnp.bfloat16).astype(jnp.float32) * inverse
        high, low = halves_of(part)
        packed = jnp.where(lane < HEADS, high.astype(jnp.float32), low.astype(jnp.float32)).astype(jnp.bfloat16)
        return jnp.dot(packed, spread, preferred_element_type=jnp.float32)

    return share(own_weight) * own[:, 2 * width :].astype(jnp.float32) + share(other_weight) * other_value.astype(
        jnp.float32
    )


def place(pieces, ready, ends, mixed):
    rows, tile_cols, width = mixed.shape
    for row, column, source, start, count in pieces:
        mixed[row, column : column + count] = source[start : start + count, :].astype(jnp.float32)
    mixed[:, 0:EDGE] = jnp.zeros((rows, EDGE, width), jnp.float32)
    mixed[:, tile_cols - EDGE :] = jnp.zeros((rows, EDGE, width), jnp.float32)
    ready[...] = mixed[...].astype(jnp.bfloat16)
    ends[:, 0:STRIP] = mixed[:, 0:STRIP]
    ends[:, STRIP:] = mixed[:, tile_cols - STRIP :]


def attend_frames(own, other, w_qkv, marks, spread):
    width = other.shape[1]
    pairs = jnp.dot(other[...], w_qkv[:, width:], preferred_element_type=jnp.float32).astype(jnp.bfloat16)
    return temporal(own[...], pairs[:, :width], pairs[:, width:], marks[...], spread[...])


def late_own_kernel(rim, edge, w_qkv, rim_own, edge_own):
    both = jnp.concatenate([rim[...], edge[...]], axis=0)
    found = jnp.dot(both, w_qkv[...], preferred_element_type=jnp.float32).astype(jnp.bfloat16)
    rim_own[...] = found[: rim.shape[0]]
    edge_own[...] = found[rim.shape[0] :]


def inner_done_kernel(own, other, w_qkv, marks, spread, after, ready, ends, done, mixed):
    rows, tile_cols, width = mixed.shape
    done[...] = attend_frames(own, other, w_qkv, marks, spread)
    pieces = []
    for row in range(rows):
        for strip in range(tile_cols // STRIP - 1):
            pieces.append((row, EDGE + STRIP * strip, done, (strip * rows + row) * STRIP, STRIP))
    place(pieces, ready, ends, mixed)


def rim_done_kernel(own, other, w_qkv, marks, spread, ready, ends, done, mixed):
    rows, tile_cols, width = mixed.shape
    done[...] = attend_frames(own, other, w_qkv, marks, spread)
    columns = RIM_STRIPS * STRIP
    pieces = []
    for row in range(rows):
        for part in range((tile_cols // STRIP - 1) // RIM_STRIPS):
            pieces.append((row, EDGE + columns * part, done, (part * rows + row) * columns, columns))
    place(pieces, ready, ends, mixed)


def last_kernel(own, other, w_qkv, marks, spread, inner, inner_ends, rim, rim_ends, out, left, right, arrived):
    tile_rows, tile_cols, width = out.shape[1:]
    low, high = RADIUS, tile_rows - RADIUS
    parts = (
        (slice(0, low), rim, rim_ends, slice(0, RADIUS)),
        (slice(low, high), inner, inner_ends, slice(0, high - low)),
        (slice(high, tile_rows), rim, rim_ends, slice(RADIUS, 2 * RADIUS)),
    )
    whole = []
    for target, ready, ends, rows in parts:
        size = rows.stop - rows.start
        copy = pltpu.make_async_copy(
            ready.at[pl.ds(rows.start, size), pl.ds(STRIP, tile_cols - 2 * STRIP)],
            out.at[0, pl.ds(target.start, size), pl.ds(STRIP, tile_cols - 2 * STRIP)],
            arrived.at[len(whole)],
        )
        copy.start()
        whole.append(copy)
    edge = attend_frames(own, other, w_qkv, marks, spread)
    edge = edge.reshape(tile_rows, STRIP, width)
    early = iota((1, STRIP, 1), 1) < EDGE
    for target, ready, ends, rows in parts:
        left[target] = jnp.where(early, edge[target], ends[rows, :STRIP]).astype(jnp.bfloat16)
        right[target] = jnp.where(early, ends[rows, STRIP:], edge[target]).astype(jnp.bfloat16)
    copies = [
        pltpu.make_async_copy(left, out.at[0, :, pl.ds(0, STRIP)], arrived.at[3]),
        pltpu.make_async_copy(right, out.at[0, :, pl.ds(tile_cols - STRIP, STRIP)], arrived.at[4]),
    ]
    for copy in copies:
        copy.start()
    for copy in whole + copies:
        copy.wait()


def call(body, out_shape, operands, scratch=(), flops=0, limit=24, specs=(), out_spec=VMEM):
    in_specs = [VMEM] * len(operands)
    for index, spec in specs:
        in_specs[index] = spec
    return pl.pallas_call(
        body,
        out_shape=out_shape,
        in_specs=in_specs,
        out_specs=[VMEM] * len(out_shape) if isinstance(out_shape, list) else out_spec,
        scratch_shapes=list(scratch),
        cost_estimate=pl.CostEstimate(flops=flops, bytes_accessed=0, transcendentals=0),
        compiler_params=pltpu.CompilerParams(vmem_limit_bytes=limit * MIB),
        name=body.__name__,
    )(*operands)


def exchanges(count):
    found = []
    for start in (0, 1):
        pairs = [(i, i + 1) for i in range(start, count - 1, 2)]
        found.append(pairs + [(j, i) for i, j in pairs])
    return found


def fast_device(resid, spatial_qkv, key_keep, w_spatial_out, modulation, w_temporal_qkv):
    frame_count, tile_rows, tile_cols, width = resid.shape
    strips = tile_cols // STRIP - 1
    odd = jnp.stack([lax.axis_index("row") % 2, lax.axis_index("col") % 2]).astype(jnp.int32)
    swap = [(0, 1), (1, 0)]
    bf16 = jnp.bfloat16
    struct = lambda *shape: jax.ShapeDtypeStruct(shape, bf16)
    held = lambda *shape: pltpu.VMEM(shape, bf16)
    stay = lambda x: pltpu.with_memory_space_constraint(x, pltpu.HBM)
    smem = pl.BlockSpec(memory_space=pltpu.SMEM)
    hbm = pl.BlockSpec(memory_space=pltpu.HBM)
    anywhere = pl.BlockSpec(memory_space=pl.ANY)
    marks, spread = head_marks(width), mark_heads(width)
    lanes = 2 * width + LANES
    pad_rows = tile_rows + 2 * RADIUS
    edge_count = tile_rows * STRIP

    one, two, qkv, keep = call(
        load_kernel,
        [struct(1, RADIUS, tile_cols, lanes)] * 2
        + [held(3, tile_rows, tile_cols, width), held(1, tile_rows, tile_cols, LANES)],
        (odd, stay(spatial_qkv[:, 0]), stay(key_keep.reshape(tile_rows, 1, tile_cols))),
        [
            pltpu.VMEM((tile_rows, 1, tile_cols), jnp.int32),
            pltpu.VMEM((LANES, LANES), jnp.float32),
            pltpu.SemaphoreType.DMA((6,)),
        ],
        specs=[(0, smem), (1, hbm), (2, hbm)],
    )
    pairs_one, pairs_two = exchanges(lax.axis_size("row"))
    first = lax.ppermute(one, "row", pairs_one)
    second = lax.ppermute(two, "row", pairs_two)

    inner_count = strips * (tile_rows - 2 * RADIUS) * STRIP
    inner, resid, w_spatial_out = call(
        inner_kernel,
        [struct(inner_count, width), held(*resid.shape), held(width, width)],
        (qkv, keep, stay(resid), stay(w_spatial_out), modulation),
        [held(inner_count, width), pltpu.SemaphoreType.DMA((2,))],
        specs=[(2, hbm), (3, hbm)],
    )
    inner_other = lax.ppermute(inner, "tm", swap)
    inner_own, one_body, two_body = call(
        own_kernel,
        [struct(inner_count, 3 * width)] + [held(tile_rows, RADIUS, lanes)] * 2,
        (odd, inner, w_temporal_qkv, qkv, keep),
        specs=[(0, smem)],
    )

    one, two, halo = call(
        columns_kernel,
        [struct(1, pad_rows, RADIUS, lanes)] * 2 + [held(2, RADIUS, tile_cols, lanes)],
        (odd, first, second, one_body, two_body),
        specs=[(0, smem)],
    )
    pairs_one, pairs_two = exchanges(lax.axis_size("col"))
    side_one = lax.ppermute(one, "col", pairs_one)
    side_two = lax.ppermute(two, "col", pairs_two)

    rim_count = strips * 2 * RADIUS * STRIP
    rim = call(
        rim_kernel,
        struct(rim_count, width),
        (qkv, keep, halo, resid, w_spatial_out, modulation),
        [held(rim_count, width)],
    )
    rim_other = lax.ppermute(rim, "tm", swap)

    def rows_of(count):
        whole, ends = (count, tile_cols, width), (count, 2 * STRIP, width)
        return [held(*whole), pltpu.VMEM(ends, jnp.float32)], pltpu.VMEM(whole, jnp.float32)

    shapes, scratch = rows_of(tile_rows - 2 * RADIUS)
    inner_ready, inner_ends = call(
        inner_done_kernel,
        shapes,
        (inner_own, inner_other, w_temporal_qkv, marks, spread, rim),
        [pltpu.VMEM((inner_count, width), jnp.float32), scratch],
        specs=[(5, anywhere)],
    )

    edge = call(
        edge_kernel,
        struct(edge_count, width),
        (odd, qkv, keep, halo, side_one, side_two, resid, w_spatial_out, modulation, inner_ready),
        [
            held(edge_count, width),
            pltpu.VMEM((pad_rows, 3 * STRIP, lanes), jnp.float32),
            pltpu.VMEM((tile_rows, STRIP, width), jnp.float32),
            pltpu.VMEM((tile_rows, STRIP, width), jnp.float32),
        ],
        specs=[(0, smem), (9, anywhere)],
    )
    edge_other = lax.ppermute(edge, "tm", swap)

    rim_own, edge_own = call(
        late_own_kernel,
        [struct(rim_count, 3 * width), struct(edge_count, 3 * width)],
        (rim, edge, w_temporal_qkv),
    )
    shapes, scratch = rows_of(2 * RADIUS)
    rim_ready, rim_ends = call(
        rim_done_kernel,
        shapes,
        (rim_own, rim_other, w_temporal_qkv, marks, spread),
        [pltpu.VMEM((rim_count, width), jnp.float32), scratch],
    )
    return call(
        last_kernel,
        struct(frame_count, tile_rows, tile_cols, width),
        (edge_own, edge_other, w_temporal_qkv, marks, spread, inner_ready, inner_ends, rim_ready, rim_ends),
        [
            held(tile_rows, STRIP, width),
            held(tile_rows, STRIP, width),
            pltpu.SemaphoreType.DMA((5,)),
        ],
        out_spec=hbm,
    )


def per_device(resid, *rest):
    frame_count, tile_rows, tile_cols, width = resid.shape
    fits = (
        frame_count == 1
        and lax.axis_size("tm") == 2
        and width == 9 * LANES
        and (tile_cols // STRIP - 1) % RIM_STRIPS == 0
        and tile_cols % STRIP == 0
        and tile_cols >= 2 * STRIP
        and tile_rows % 4 == 0
        and tile_rows > 2 * RADIUS
    )
    return (fast_device if fits else general_device)(resid, *rest)


def solution(mesh):
    return jax.shard_map(
        per_device,
        mesh=mesh,
        in_specs=(
            P("tm", "row", "col", None),
            P(None, "tm", "row", "col", None),
            P("tm", "row", "col"),
            P(),
            P(),
            P(),
        ),
        out_specs=P("tm", "row", "col", None),
        check_vma=False,
    )
```
